32 devices in a mesh: ty: 8 (over z, x), tx: 4 (over y, core).
Axes of the slice: x: 2, y: 2, z: 4, core: 2. Of those that a mesh axis runs over, the one named last changes fastest.
Arguments:
- stored_eastward_flow: float32 [30, 64, 512], P(None, 'ty', 'tx'), may hold values from -6 to 6
- stored_northward_flow: float32 [30, 64, 512], P(None, 'ty', 'tx'), may hold values from -6 to 6
- stored_heat_content: float32 [30, 64, 512], P(None, 'ty', 'tx'), may hold values from -6 to 6
- ocean_layer_tally: int32 [64, 512], P('ty', 'tx'), may hold values from 0 to 30, as said below
- eastward_flow_sensitivity: float32 [30, 64, 512], P(None, 'ty', 'tx'), may hold values from -6 to 6
- northward_flow_sensitivity: float32 [30, 64, 512], P(None, 'ty', 'tx'), may hold values from -6 to 6
- scalar_content_sensitivity: float32 [30, 64, 512], P(None, 'ty', 'tx'), may hold values from -6 to 6
- elevation_sensitivity: float32 [64, 512], P('ty', 'tx'), may hold values from -6 to 6
Outputs:
- u_gradient: float32 [30, 64, 512], P(None, 'ty', 'tx')
- v_gradient: float32 [30, 64, 512], P(None, 'ty', 'tx')
- t_gradient: float32 [30, 64, 512], P(None, 'ty', 'tx')
- eta_gradient: float32 [64, 512], P('ty', 'tx')
The draws below stay inside these ranges and needn't reach their ends.
Inputs may be any that keep to these rules, and one draw needn't show every extreme that they name: `ocean_layer_tally`: the number of wet levels of each column; 0 marks land.
All inputs are finite; a program needn't handle non-finite values.
Results may differ from the reference program's by a relative error of at most 0.0001.
Values sent between devices are 32-bit elements; how exact they have to be, the bound alone decides.
No kernel may reach another device: no remote copies, remote signals or barrier semaphores. Data moves between devices by JAX's collectives and lax.ppermute only.
A program may use at most 64 MiB of HBM per device.

```python
import jax
import jax.numpy as jnp
from jax import lax

DEPTH_LAYERS = 30
ITERS = 4
MESH_NORTHWARD_N = 64
MESH_EASTWARD_N = 512


def draw_ocean_layer_tally(key, part):
    key_depth, key_land = jax.random.split(key)
    row_number = jnp.arange(MESH_NORTHWARD_N)[:, None]
    depth_limit = 1 + (DEPTH_LAYERS - 1) * (row_number + 1) // MESH_NORTHWARD_N
    base_depth = jax.random.randint(key_depth, (MESH_NORTHWARD_N, MESH_EASTWARD_N), 1, DEPTH_LAYERS + 1)
    column_depth = jnp.minimum(base_depth, depth_limit)
    blocks = jax.random.randint(key_land, ((MESH_NORTHWARD_N + 15) // 16, (MESH_EASTWARD_N + 63) // 64), 0, 4)
    land_cell = jnp.repeat(jnp.repeat(blocks, 16, axis=0), 64, axis=1)[:MESH_NORTHWARD_N, :MESH_EASTWARD_N] == 0
    column_depth = jnp.where(land_cell, 0, column_depth)
    column_depth = column_depth.at[MESH_NORTHWARD_N - 1, MESH_EASTWARD_N - 1].set(DEPTH_LAYERS)
    column_depth = column_depth.at[0, 0].set(0)
    return column_depth.astype(jnp.int32)


def block_scale(stream_key, dims, cuts, least, top_value):
    factor_of, own = 1.0, jax.random.fold_in(stream_key, 6)
    for dim, blocks in cuts:
        steps = jnp.exp(jax.random.uniform(jax.random.fold_in(own, dim), (blocks,), jnp.float32, least / len(cuts), top_value / len(cuts)))
        factor_of = factor_of * jnp.repeat(steps, dims[dim] // blocks).reshape([-1 if axis == dim else 1 for axis in range(len(dims))])
    return factor_of


def centred(own_key, dims, width, limit, pieces=(), kind=jnp.bfloat16):
    values = jax.random.normal(own_key, dims, jnp.float32) * width
    if len(pieces) > 0:
        values = block_scale(own_key, dims, pieces, -0.22, 0.18) * values
    return jnp.clip(values, min=-limit, max=limit).astype(kind)


def setup_inputs(seed: int = 0) -> dict:
    splits = jax.random.split(jax.random.key(seed), 9)
    stored_eastward_flow = centred(splits[0], (DEPTH_LAYERS, MESH_NORTHWARD_N, MESH_EASTWARD_N), 1.0, 6.0, ((1, 8), (2, 4)), jnp.float32)
    stored_northward_flow = centred(splits[1], (DEPTH_LAYERS, MESH_NORTHWARD_N, MESH_EASTWARD_N), 1.0, 6.0, ((1, 8), (2, 4)), jnp.float32)
    stored_heat_content = centred(splits[2], (DEPTH_LAYERS, MESH_NORTHWARD_N, MESH_EASTWARD_N), 1.0, 6.0, ((1, 8), (2, 4)), jnp.float32)
    ocean_layer_tally = draw_ocean_layer_tally(jax.random.fold_in(splits[8], 71), 0)
    eastward_flow_sensitivity = centred(splits[4], (DEPTH_LAYERS, MESH_NORTHWARD_N, MESH_EASTWARD_N), 1.0, 6.0, ((1, 8), (2, 4)), jnp.float32)
    northward_flow_sensitivity = centred(splits[5], (DEPTH_LAYERS, MESH_NORTHWARD_N, MESH_EASTWARD_N), 1.0, 6.0, ((1, 8), (2, 4)), jnp.float32)
    scalar_content_sensitivity = centred(splits[6], (DEPTH_LAYERS, MESH_NORTHWARD_N, MESH_EASTWARD_N), 1.0, 6.0, ((1, 8), (2, 4)), jnp.float32)
    elevation_sensitivity = centred(splits[7], (MESH_NORTHWARD_N, MESH_EASTWARD_N), 1.0, 6.0, ((0, 8), (1, 4)), jnp.float32)
    return {"stored_eastward_flow": stored_eastward_flow, "stored_northward_flow": stored_northward_flow, "stored_heat_content": stored_heat_content, "ocean_layer_tally": ocean_layer_tally, "eastward_flow_sensitivity": eastward_flow_sensitivity, "northward_flow_sensitivity": northward_flow_sensitivity, "scalar_content_sensitivity": scalar_content_sensitivity, "elevation_sensitivity": elevation_sensitivity}


ADVECT = 0.1
GRAVITY_DT = 0.1
STEP_DT = 1.0

def wet_cells(count_float, levels):
    level_index = jnp.arange(levels).astype(jnp.float32)
    return (level_index[:, None, None] < count_float[None]).astype(jnp.float32)

def tendencies(u_input, v_input, t_input, wet_cell, coriolis_u, coriolis_v):
    row_count = u_input.shape[1] - 4
    col_count = u_input.shape[2] - 4

    def offset_view(source, shift_row, shift_col):
        return source[:, 2 + shift_row:2 + shift_row + row_count, 2 + shift_col:2 + shift_col + col_count]

    def mask_u(shift_row, shift_col):
        return offset_view(wet_cell, shift_row, shift_col) * offset_view(wet_cell, shift_row, shift_col - 1)

    def mask_v(shift_row, shift_col):
        return offset_view(wet_cell, shift_row, shift_col) * offset_view(wet_cell, shift_row - 1, shift_col)

    def flux_x(shift_col):
        face_value = (7.0 * (offset_view(t_input, 0, shift_col) + offset_view(t_input, 0, shift_col - 1)) - (offset_view(t_input, 0, shift_col + 1) + offset_view(t_input, 0, shift_col - 2))) / 12.0
        return mask_u(0, shift_col) * offset_view(u_input, 0, shift_col) * face_value

    def flux_y(shift_row):
        face_value = (7.0 * (offset_view(t_input, shift_row, 0) + offset_view(t_input, shift_row - 1, 0)) - (offset_view(t_input, shift_row + 1, 0) + offset_view(t_input, shift_row - 2, 0))) / 12.0
        return mask_v(shift_row, 0) * offset_view(v_input, shift_row, 0) * face_value
    t_new = offset_view(t_input, 0, 0) - ADVECT * offset_view(wet_cell, 0, 0) * (flux_x(1) - flux_x(0) + flux_y(1) - flux_y(0))
    u_here = offset_view(u_input, 0, 0)
    v_here = offset_view(v_input, 0, 0)
    v_bar = 0.25 * (v_here + offset_view(v_input, 1, 0) + offset_view(v_input, 0, -1) + offset_view(v_input, 1, -1))
    u_bar = 0.25 * (u_here + offset_view(u_input, 0, 1) + offset_view(u_input, -1, 0) + offset_view(u_input, -1, 1))
    u_star = u_here + ADVECT * mask_u(0, 0) * (coriolis_u * v_bar - u_here * 0.5 * (offset_view(u_input, 0, 1) - offset_view(u_input, 0, -1)) - v_bar * 0.5 * (offset_view(u_input, 1, 0) - offset_view(u_input, -1, 0)))
    v_star = v_here + ADVECT * mask_v(0, 0) * (-coriolis_v * u_bar - u_bar * 0.5 * (offset_view(v_input, 0, 1) - offset_view(v_input, 0, -1)) - v_here * 0.5 * (offset_view(v_input, 1, 0) - offset_view(v_input, -1, 0)))
    return (u_star, v_star, t_new)

def surface_apply(rimmed, depth_u, depth_v):
    centre = rimmed[1:-1, 1:-1]
    east = rimmed[1:-1, 2:]
    west = rimmed[1:-1, :-2]
    north = rimmed[2:, 1:-1]
    south = rimmed[:-2, 1:-1]
    return centre - GRAVITY_DT * STEP_DT * (depth_u[1:-1, 2:] * (east - centre) - depth_u[1:-1, 1:-1] * (centre - west) + depth_v[2:, 1:-1] * (north - centre) - depth_v[1:-1, 1:-1] * (centre - south))

def reference(stored_eastward_flow, stored_northward_flow, stored_heat_content, ocean_layer_tally, eastward_flow_sensitivity, northward_flow_sensitivity, scalar_content_sensitivity, elevation_sensitivity):
    levels, row_count, col_count = stored_eastward_flow.shape
    count_float = ocean_layer_tally.astype(jnp.float32)
    wet_padded = wet_cells(jnp.pad(count_float, 2), levels)
    row_index = jnp.arange(row_count).astype(jnp.float32)[:, None]
    coriolis_u = 0.5 + (row_index + 0.5) / row_count
    coriolis_v = 0.5 + row_index / row_count
    thickness = (1.0 + jnp.arange(levels).astype(jnp.float32) / levels)[:, None, None]
    inner_wet = wet_padded[:, 1:-1, 1:-1]
    u_mask = inner_wet * wet_padded[:, 1:-1, :-2]
    v_mask = inner_wet * wet_padded[:, :-2, 1:-1]
    depth_u = lax.optimization_barrier(jnp.sum(thickness * u_mask, axis=0))
    depth_v = lax.optimization_barrier(jnp.sum(thickness * v_mask, axis=0))
    pad_one = ((0, 0), (1, 1), (1, 1))
    col_u = lax.optimization_barrier(jnp.sum(u_mask * jnp.pad(eastward_flow_sensitivity, pad_one), axis=0))
    col_v = lax.optimization_barrier(jnp.sum(v_mask * jnp.pad(northward_flow_sensitivity, pad_one), axis=0))
    surface_load = elevation_sensitivity + GRAVITY_DT * (col_u[1:-1, 2:] - col_u[1:-1, 1:-1] + col_v[2:, 1:-1] - col_v[1:-1, 1:-1])

    def operate(direction):
        return surface_apply(jnp.pad(direction, 1), depth_u, depth_v)
    solution = jnp.zeros_like(surface_load)
    residual = surface_load
    direction = surface_load
    norm_now = jnp.sum(residual * residual)
    for iteration in range(ITERS):
        applied = operate(direction)
        step_length = norm_now / jnp.sum(direction * applied)
        solution = solution + step_length * direction
        residual = residual - step_length * applied
        norm_next = jnp.sum(residual * residual)
        direction = residual + norm_next / norm_now * direction
        norm_now = norm_next
    solution_pad = jnp.pad(solution, 1)
    u_cotangent = eastward_flow_sensitivity + STEP_DT * thickness * u_mask[:, 1:-1, 1:-1] * (solution - solution_pad[1:-1, :-2])[None]
    v_cotangent = northward_flow_sensitivity + STEP_DT * thickness * v_mask[:, 1:-1, 1:-1] * (solution - solution_pad[:-2, 1:-1])[None]
    pad_two = ((0, 0), (2, 2), (2, 2))

    def advance_ocean_once(u_input, v_input, t_input):
        return tendencies(jnp.pad(u_input, pad_two), jnp.pad(v_input, pad_two), jnp.pad(t_input, pad_two), wet_padded, coriolis_u, coriolis_v)
    advance_results, backward_chain_rule = jax.vjp(advance_ocean_once, stored_eastward_flow, stored_northward_flow, stored_heat_content)
    gradients = backward_chain_rule((u_cotangent, v_cotangent, scalar_content_sensitivity))
    return (gradients[0], gradients[1], gradients[2], solution)
```

```python
import functools

import jax
import jax.numpy as jnp
from jax import lax
from jax.experimental import pallas as pl
from jax.experimental.pallas import tpu as pltpu
from jax.sharding import Mesh, PartitionSpec as P

ITERS = 4
ADVECT = 0.1
GRAVITY_DT = 0.1

SUB = 8
LANES = 128
SEG = 32
FIELDS = ("u", "v", "t", "st", "su", "sv")
SLOTS = {"u": 0, "v": 2, "t": 4, "st": 6, "su": 8, "sv": 9}
N_SLOTS = 10
CHUNK_LOAD = SUB
CHUNK_EDGE = 2 * SUB
CHUNK_ROW = 3 * SUB
CORNER_LANE = 32
CORNER_STEP = 24


def lane_ids():
    return lax.broadcasted_iota(jnp.int32, (SUB, LANES), 1)


def row_ids():
    return lax.broadcasted_iota(jnp.int32, (SUB, LANES), 0)


def roll_lanes(value, amount):
    amount %= LANES
    return value if amount == 0 else pltpu.roll(value, amount, 1)


def roll_rows(value, amount):
    amount %= SUB
    return value if amount == 0 else pltpu.roll(value, amount, 0)


def at(value, shift):
    return roll_lanes(value, -shift)


def row_of(tile, row):
    return jnp.broadcast_to(tile[row : row + 1, :], (SUB, LANES))


def group_count(levels):
    return -(-levels // SUB)


def load_group(ref, row, q, levels):
    first = min(q * SUB, levels - SUB)
    value = ref[pl.ds(first * SUB + row, SUB, stride=SUB), :]
    return roll_rows(value, first - q * SUB)


def store_group(ref, row, q, levels, value):
    count = min(SUB, levels - q * SUB)
    ref[pl.ds(q * SUB * SUB + row, count, stride=SUB), :] = value[:count]


def level_numbers(groups):
    rows = row_ids()
    numbers = [(rows + q * SUB).astype(jnp.float32) for q in range(groups)]
    return numbers + [(rows + (lane_ids() // SEG) * SUB).astype(jnp.float32)]


def edge_of_groups(values):
    lanes = lane_ids()
    out = roll_lanes(values[0], 8)
    for q in range(1, len(values)):
        out = jnp.where(lanes >= SEG * q, roll_lanes(values[q], SEG * q + 8), out)
    return jnp.where(lanes % SEG >= 16, roll_lanes(out, 16), out)


def insert_sides(edge, west, east, field):
    place = lane_ids() % SEG
    edge = jnp.where((place == 6) | (place == 7), roll_lanes(west, 6 - 4 * field), edge)
    return jnp.where((place == 24) | (place == 25), roll_lanes(east, 22 - 4 * field), edge)


def edge_of_tile(west, centre, east):
    lanes = lane_ids()
    out = jnp.where(lanes < 8, roll_lanes(west, 8), roll_lanes(centre, 8))
    out = jnp.where(lanes >= 16, roll_lanes(centre, 24), out)
    out = jnp.where(lanes >= 24, roll_lanes(east, 24), out)
    out = jnp.where(lanes < SEG, out, roll_lanes(out, SEG))
    return jnp.where(lanes < 2 * SEG, out, roll_lanes(out, 2 * SEG))


def merge_edge(value, edge, q):
    lanes = lane_ids()
    value = jnp.where(lanes < 2, roll_lanes(edge, -(SEG * q + 8)), value)
    return jnp.where(lanes >= LANES - 2, roll_lanes(edge, 104 - SEG * q), value)


def pack_kernel(levels, peers, u_ref, v_ref, t_ref, su_ref, sv_ref, st_ref, count_ref, elev_ref, y1_ref, y2_ref, x_ref, chunk_ref):
    groups = group_count(levels)
    lanes, rows = lane_ids(), row_ids()
    even = lax.axis_index("ty") % 2 == 0
    refs = {"u": u_ref, "v": v_ref, "t": t_ref, "st": st_ref, "su": su_ref, "sv": sv_ref}
    count = count_ref[...].astype(jnp.float32)
    zero = jnp.zeros((SUB, LANES), jnp.float32)

    wet_u = jnp.where(lanes == 0, 0.0, jnp.minimum(count, roll_lanes(count, 1)))
    wet_v = jnp.where(rows == 0, 0.0, jnp.minimum(count, roll_rows(count, 1)))
    col_u, col_v, edge = zero, zero, zero
    for k in range(levels):
        su_level = su_ref[k * SUB : (k + 1) * SUB, :]
        col_u = col_u + jnp.where(wet_u > float(k), su_level, 0.0)
        col_v = col_v + jnp.where(wet_v > float(k), sv_ref[k * SUB : (k + 1) * SUB, :], 0.0)
        edge = jnp.where(lanes == k, roll_lanes(su_level, k), edge)
    load = elev_ref[...] + GRAVITY_DT * (at(col_u, 1) - col_u + roll_rows(col_v, -1) - col_v)

    loaded = {}
    for name in FIELDS:
        for row in range(SUB):
            for q in range(groups):
                loaded[name, row, q] = load_group(refs[name], row, q, levels)

    corners = (("u", 6, 0), ("u", 7, 0), ("u", 7, 1), ("su", 7, 0), ("v", 7, 127), ("u", 7, 127))
    corners += (("v", 0, 127), ("v", 1, 127), ("v", 0, 126), ("sv", 0, 127), ("v", 0, 0), ("u", 0, 0))
    for place, (name, row, column) in enumerate(corners):
        for q in range(groups):
            lane = CORNER_LANE + CORNER_STEP * q + place
            edge = jnp.where(lanes == lane, roll_lanes(loaded[name, row, q], lane - column), edge)

    for row in range(SUB):
        packet = zero
        for field, name in enumerate(FIELDS):
            for q in range(groups):
                lane = SEG * q + 4 * field
                packet = jnp.where((lanes >= lane) & (lanes < lane + 4), roll_lanes(loaded[name, row, q], lane + 2), packet)
        x_ref[row * SUB : (row + 1) * SUB, :] = packet
    x_ref[SUB * SUB :, :] = count

    for name in FIELDS:
        wide = name not in ("su", "sv")
        for offset in range(2 if wide else 1):
            for q in range(groups):
                upper = loaded[name, 6 + offset if wide else 7, q]
                lower = loaded[name, offset, q]
                place = pl.ds(((SLOTS[name] + offset) * groups + q) * SUB, SUB)
                y1_ref[place, :] = jnp.where(even, upper, lower)
                y2_ref[place, :] = jnp.where(even, lower, upper)
    y1_ref[N_SLOTS * groups * SUB :, :] = count
    y2_ref[N_SLOTS * groups * SUB :, :] = count

    south_row = [loaded["sv", 0, q] for q in range(groups)]

    def put(peer, carry):
        chunk_ref[peer, 0:SUB, :] = count
        chunk_ref[peer, CHUNK_LOAD : CHUNK_LOAD + SUB, :] = load
        chunk_ref[peer, CHUNK_EDGE : CHUNK_EDGE + SUB, :] = edge
        for q in range(groups):
            chunk_ref[peer, CHUNK_ROW + q * SUB : CHUNK_ROW + (q + 1) * SUB, :] = south_row[q]
        return carry

    lax.fori_loop(0, peers, put, 0)


def slot_reader(y1_ref, y2_ref, groups):
    even = lax.axis_index("ty") % 2 == 0

    def read(name, row, q):
        if name in ("su", "sv"):
            slot = SLOTS[name]
        else:
            slot = SLOTS[name] + (row + 2 if row < 0 else row - SUB)
        place = pl.ds((slot * groups + q) * SUB, SUB)
        north, south = jnp.where(even, y1_ref[place, :], y2_ref[place, :]), jnp.where(even, y2_ref[place, :], y1_ref[place, :])
        return south if row < 0 else north

    def counts():
        place = pl.ds(N_SLOTS * groups * SUB, SUB)
        one, two = y1_ref[place, :], y2_ref[place, :]
        return jnp.where(even, two, one), jnp.where(even, one, two)

    return read, counts


def side_reader(x1_ref, x2_ref):
    even = lax.axis_index("core") % 2 == 0

    def read(row):
        place = pl.ds(row * SUB, SUB)
        one, two = x1_ref[place, :], x2_ref[place, :]
        return jnp.where(even, two, one), jnp.where(even, one, two)

    return read


def face_value(t0, t_before, t_after, t_before2):
    return (7.0 * (t0 + t_before) - (t_after + t_before2)) * (1.0 / 12.0)


def tracer_kernel(levels, u_ref, v_ref, t_ref, st_ref, count_ref, y1_ref, y2_ref, x1_ref, x2_ref, dt_ref, du_ref, dv_ref):
    groups = group_count(levels)
    refs = {"u": u_ref, "v": v_ref, "t": t_ref, "st": st_ref}
    read_row, read_counts = slot_reader(y1_ref, y2_ref, groups)
    read_sides = side_reader(x1_ref, x2_ref)
    numbers = level_numbers(groups)

    count = count_ref[...].astype(jnp.float32)
    count_south, count_north = read_counts()
    count_west, count_east = read_sides(SUB)
    count_edge = edge_of_tile(count_west, count, count_east)
    wet_u_tile = (jnp.minimum(count, at(count, -1)), jnp.minimum(count_edge, at(count_edge, -1)))
    count_rows = {row: row_of(count, row) for row in range(SUB)}
    count_rows.update({row: row_of(count_south, row % SUB) for row in (-2, -1)})
    count_rows.update({row: row_of(count_north, row - SUB) for row in (8, 9)})
    wet_v_rows = {row: jnp.minimum(count_rows[row], count_rows[row - 1]) for row in range(-1, 10)}

    def along_columns(level, wet_count, wet_u_count, u, t, st):
        wet_u = wet_u_count > level
        cell = jnp.where(wet_count > level, -ADVECT * st, 0.0)
        flux = jnp.where(wet_u, at(cell, -1) - cell, 0.0)
        back = u * flux
        pair = back + at(back, 1)
        outer = at(back, -1) + at(back, 2)
        return (7.0 * pair - outer) * (1.0 / 12.0), flux * face_value(t, at(t, -1), at(t, 1), at(t, -2))

    sides = [read_sides(row) for row in range(SUB)]
    edge_t, edge_u = [], []
    for row in range(SUB):
        values = {}
        for name in ("u", "t", "st"):
            own = edge_of_groups([load_group(refs[name], row, q, levels) for q in range(groups)])
            values[name] = insert_sides(own, *sides[row], FIELDS.index(name))
        from_x, to_u = along_columns(
            numbers[groups], row_of(count_edge, row), row_of(wet_u_tile[1], row), values["u"], values["t"], values["st"]
        )
        edge_t.append(from_x)
        edge_u.append(to_u)

    for q in range(groups):
        level = numbers[q]

        def get(name, row):
            return load_group(refs[name], row, q, levels) if 0 <= row < SUB else read_row(name, row, q)

        t = {row: get("t", row) for row in range(-2, 9)}
        st = {row: get("st", row) for row in range(-2, 10)}
        v = {row: get("v", row) for row in range(-1, 10)}
        cell = {row: jnp.where(count_rows[row] > level, -ADVECT * st[row], 0.0) for row in range(-2, 10)}
        flux = {row: jnp.where(wet_v_rows[row] > level, cell[row - 1] - cell[row], 0.0) for row in range(-1, 10)}
        back = {row: v[row] * flux[row] for row in range(-1, 10)}
        for row in range(SUB):
            from_x, to_u = along_columns(
                level, count_rows[row], row_of(wet_u_tile[0], row), get("u", row), t[row], st[row]
            )
            from_x = merge_edge(from_x, edge_t[row], q)
            to_u = merge_edge(to_u, edge_u[row], q)
            from_y = (7.0 * (back[row] + back[row + 1]) - (back[row - 1] + back[row + 2])) * (1.0 / 12.0)
            to_v = flux[row] * face_value(t[row], t[row - 1], t[row + 1], t[row - 2])
            store_group(dt_ref, row, q, levels, st[row] + from_x + from_y)
            store_group(du_ref, row, q, levels, to_u)
            store_group(dv_ref, row, q, levels, to_v)


def total(value):
    return jnp.sum(value, axis=(0, 1), keepdims=True)


def surface_solve(levels, ny, nx, g_ref, count_ref, load_ref, face_ref, x_ref, r_ref, p_ref, q_ref):
    groups = group_count(levels)
    lanes, rows = lane_ids(), row_ids()
    numbers = level_numbers(groups)
    core = lax.axis_index("core")
    unroll = ny if ny <= 8 else 1

    def loop(body, init=0):
        return lax.fori_loop(0, ny, body, init, unroll=unroll)

    def block(ref, j, i):
        return ref[j, i]

    def west_of(ref, j, i):
        return roll_lanes(jnp.where(lanes == LANES - 1, ref[j, max(i - 1, 0)], ref[j, i]), 1)

    def east_of(ref, j, i):
        return roll_lanes(jnp.where(lanes == 0, ref[j, min(i + 1, nx - 1)], ref[j, i]), -1)

    def south_of(ref, j, i):
        return roll_rows(jnp.where(rows == SUB - 1, ref[jnp.maximum(j - 1, 0), i], ref[j, i]), 1)

    def north_of(ref, j, i):
        return roll_rows(jnp.where(rows == 0, ref[jnp.minimum(j + 1, ny - 1), i], ref[j, i]), -1)

    def chunk(j, i, first, size):
        half = jnp.where(core == i % 2, 0, 1)
        return g_ref[half][j * (nx // 2) + i // 2, first : first + size, :]

    def gather(j, carry):
        for i in range(nx):
            count_ref[j, i] = chunk(j, i, 0, SUB)
        return carry

    loop(gather)

    def depth(wet):
        return wet + wet * (wet - 1.0) * (0.5 / levels)

    def faces(j, carry):
        for i in range(nx):
            count = count_ref[j, i]
            wet_u = jnp.minimum(count, west_of(count_ref, j, i))
            wet_v = jnp.minimum(count, south_of(count_ref, j, i))
            if i == 0:
                wet_u = jnp.where(lanes == 0, 0.0, wet_u)
            wet_v = jnp.where((rows == 0) & (j == 0), 0.0, wet_v)
            face_ref[0, j, i] = GRAVITY_DT * depth(wet_u)
            face_ref[1, j, i] = GRAVITY_DT * depth(wet_v)
            edge = chunk(j, i, CHUNK_EDGE, SUB)
            wet_west = jnp.broadcast_to(wet_u[:, 0:1], (SUB, LANES))
            inside = (lanes < levels) & (wet_west > lanes.astype(jnp.float32))
            col_u = jnp.sum(jnp.where(inside, edge, 0.0), axis=1, keepdims=True)
            face_ref[2, j, i] = GRAVITY_DT * jnp.broadcast_to(col_u, (SUB, LANES))
            wet_south = row_of(wet_v, 0)
            col_v = jnp.zeros((SUB, LANES), jnp.float32)
            for q in range(groups):
                south = chunk(j, i, CHUNK_ROW + q * SUB, SUB)
                col_v = col_v + jnp.where(wet_south > numbers[q], south, 0.0)
            col_v = jnp.sum(col_v, axis=0, keepdims=True)
            face_ref[3, j, i] = GRAVITY_DT * jnp.broadcast_to(col_v, (SUB, LANES))
        return carry

    loop(faces)

    zero = jnp.zeros((SUB, LANES), jnp.float32)

    def start(j, norm):
        for i in range(nx):
            load = chunk(j, i, CHUNK_LOAD, SUB)
            load = load - jnp.where(lanes == 0, face_ref[2, j, i], 0.0)
            load = load - jnp.where(rows == 0, face_ref[3, j, i], 0.0)
            if i + 1 < nx:
                load = load + jnp.where(lanes == LANES - 1, face_ref[2, j, i + 1], 0.0)
            north = jnp.where(j + 1 < ny, face_ref[3, jnp.minimum(j + 1, ny - 1), i], 0.0)
            load = load + jnp.where(rows == SUB - 1, north, 0.0)
            r_ref[j, i] = load
            p_ref[j, i] = load
            x_ref[j, i] = zero
            norm = norm + load * load
        return norm

    norm = total(loop(start, zero))

    for iteration in range(ITERS):

        def apply(j, dot):
            for i in range(nx):
                p = p_ref[j, i]
                image = p + face_ref[0, j, i] * (p - west_of(p_ref, j, i))
                image = image + face_ref[1, j, i] * (p - south_of(p_ref, j, i))
                depth_east = east_of(face_ref.at[0], j, i)
                if i == nx - 1:
                    depth_east = jnp.where(lanes == LANES - 1, 0.0, depth_east)
                depth_north = north_of(face_ref.at[1], j, i)
                depth_north = jnp.where((rows == SUB - 1) & (j == ny - 1), 0.0, depth_north)
                image = image + depth_east * (p - east_of(p_ref, j, i))
                image = image + depth_north * (p - north_of(p_ref, j, i))
                q_ref[j, i] = image
                dot = dot + p * image
            return dot

        step = norm / total(loop(apply, zero))
        last = iteration + 1 == ITERS

        def advance(j, new):
            for i in range(nx):
                x_ref[j, i] = x_ref[j, i] + step * p_ref[j, i]
                if not last:
                    residual = r_ref[j, i] - step * q_ref[j, i]
                    r_ref[j, i] = residual
                    new = new + residual * residual
            return new

        new = loop(advance, zero)
        if not last:
            new = total(new)
            ratio = new / norm
            norm = new

            def turn(j, carry):
                for i in range(nx):
                    p_ref[j, i] = r_ref[j, i] + ratio * p_ref[j, i]
                return carry

            loop(turn)


def flow_kernel(
    levels, ny, nx, u_ref, v_ref, su_ref, sv_ref, ga_ref, gb_ref, y1_ref, y2_ref, x1_ref, x2_ref, dut_ref, dvt_ref,
    du_ref, dv_ref, eta_ref, count_s, face_s, x_s, r_s, p_s, q_s,
):
    groups = group_count(levels)
    lanes, rows = lane_ids(), row_ids()
    place = lanes % SEG
    core = lax.axis_index("core")
    my_j = lax.axis_index("ty")
    my_i = lax.axis_index("y") * 2 + core
    refs = {"u": u_ref, "v": v_ref, "su": su_ref, "sv": sv_ref}
    numbers = level_numbers(groups)
    thick = [1.0 + number * (1.0 / levels) for number in numbers]
    read_row, _ = slot_reader(y1_ref, y2_ref, groups)
    read_sides = side_reader(x1_ref, x2_ref)

    class Halves:
        def __getitem__(self, half):
            class Picked:
                def __getitem__(self, where):
                    return jnp.where(half == 0, ga_ref[where], gb_ref[where])

            return Picked()

    halves = Halves()
    surface_solve(levels, ny, nx, halves, count_s, None, face_s, x_s, r_s, p_s, q_s)
    eta_ref[...] = x_s[my_j, my_i]

    def around(ref):
        tiles = []
        for dj in (-1, 0, 1):
            j = jnp.clip(my_j + dj, 0, ny - 1)
            there = (my_j + dj >= 0) & (my_j + dj < ny)
            row = []
            for di in (-1, 0, 1):
                i = jnp.clip(my_i + di, 0, nx - 1)
                inside = there & (my_i + di >= 0) & (my_i + di < nx)
                row.append(jnp.where(inside, ref[j, i], 0.0))
            tiles.append((row[1], edge_of_tile(*row)))
        return tiles

    count_tiles, x_tiles = around(count_s), around(x_s)

    def rows_of(tiles, kind):
        out = {}
        for row in range(-2, 10):
            out[row] = row_of(tiles[row // SUB + 1][kind], row % SUB)
        return out

    def corner(dj, di):
        j, i = jnp.clip(my_j + dj, 0, ny - 1), jnp.clip(my_i + di, 0, nx - 1)
        inside = (my_j + dj >= 0) & (my_j + dj < ny) & (my_i + di >= 0) & (my_i + di < nx)
        half = jnp.where(core == i % 2, 0, 1)
        return jnp.where(inside, halves[half][j * (nx // 2) + i // 2, CHUNK_EDGE : CHUNK_EDGE + SUB, :], 0.0)

    corner_tiles = {"se": corner(-1, 1), "sw": corner(-1, -1), "nw": corner(1, -1), "ne": corner(1, 1)}
    corner_places = {
        ("u", -2): (("se", 0, 24),),
        ("u", -1): (("se", 1, 24), ("se", 2, 25), ("sw", 5, 7)),
        ("su", -1): (("se", 3, 24),),
        ("v", -1): (("sw", 4, 7),),
        ("v", 8): (("nw", 6, 7), ("nw", 8, 6), ("ne", 10, 24)),
        ("u", 8): (("ne", 11, 24),),
        ("v", 9): (("nw", 7, 7),),
        ("sv", 8): (("nw", 9, 7),),
    }

    def insert_corners(edge, name, row):
        for which, value, target in corner_places.get((name, row), ()):
            for q in range(groups):
                lane = SEG * q + target
                source = CORNER_LANE + CORNER_STEP * q + value
                edge = jnp.where(lanes == lane, roll_lanes(corner_tiles[which], lane - source), edge)
        return edge

    sides = [read_sides(row) for row in range(SUB)]
    wanted = {"u": range(-2, 9), "v": range(-1, 10), "su": range(-1, 9), "sv": range(-1, 9)}

    def get(name, row, q):
        return load_group(refs[name], row, q, levels) if 0 <= row < SUB else read_row(name, row, q)

    def get_edge(name, row):
        edge = edge_of_groups([get(name, row, q) for q in range(groups)])
        if 0 <= row < SUB:
            return insert_sides(edge, *sides[row], FIELDS.index(name))
        return insert_corners(edge, name, row)

    total_rows = ny * SUB
    first_row = (my_j * SUB).astype(jnp.float32)

    edge_u, edge_v = [], []
    for part in [groups] + list(range(groups)):
        is_edge = part == groups
        kind = 1 if is_edge else 0
        level = numbers[part]
        data = {
            name: {row: get_edge(name, row) if is_edge else get(name, row, part) for row in wanted[name]} for name in wanted
        }
        u, v, su, sv = data["u"], data["v"], data["su"], data["sv"]
        counts, x = rows_of(count_tiles, kind), rows_of(x_tiles, kind)
        u_cot, v_cot, a, b = {}, {}, {}, {}
        for row in range(-1, 9):
            wet_u = jnp.minimum(counts[row], at(counts[row], -1)) > level
            wet_v = jnp.minimum(counts[row], counts[row - 1]) > level
            u_cot[row] = su[row] + jnp.where(wet_u, thick[part] * (x[row] - at(x[row], -1)), 0.0)
            v_cot[row] = sv[row] + jnp.where(wet_v, thick[part] * (x[row] - x[row - 1]), 0.0)
            a[row] = jnp.where(wet_u, ADVECT * u_cot[row], 0.0)
            b[row] = jnp.where(wet_v, ADVECT * v_cot[row], 0.0)
        v_pair = {row: v[row] + v[row + 1] for row in range(-1, 9)}
        v_bar = {row: 0.25 * (v_pair[row] + at(v_pair[row], -1)) for row in range(-1, 9)}
        u_pair = {row: u[row] + u[row - 1] for row in range(SUB)}
        u_bar = {row: 0.25 * (u_pair[row] + at(u_pair[row], 1)) for row in range(SUB)}
        to_v_bar = {}
        for row in range(-1, 8):
            turn = 0.5 + (first_row + (row + 0.5)) * (1.0 / total_rows)
            to_v_bar[row] = a[row] * (turn - 0.5 * (u[row + 1] - u[row - 1]))
        to_u_bar = {}
        for row in range(0, 9):
            turn = 0.5 + (first_row + row) * (1.0 / total_rows)
            to_u_bar[row] = b[row] * (-turn - 0.5 * (at(v[row], 1) - at(v[row], -1)))
        for row in range(SUB):
            au, bu = a[row] * u[row], b[row] * u_bar[row]
            du = u_cot[row] + 0.5 * (
                at(au, 1) - at(au, -1) - a[row] * (at(u[row], 1) - at(u[row], -1))
                + a[row + 1] * v_bar[row + 1] - a[row - 1] * v_bar[row - 1]
            )
            pair = to_u_bar[row] + to_u_bar[row + 1]
            du = du + 0.25 * (pair + at(pair, -1))
            dv = v_cot[row] + 0.5 * (
                b[row + 1] * v[row + 1] - b[row - 1] * v[row - 1] - b[row] * (v[row + 1] - v[row - 1])
                + at(bu, 1) - at(bu, -1)
            )
            pair = to_v_bar[row] + to_v_bar[row - 1]
            dv = dv + 0.25 * (pair + at(pair, 1))
            if is_edge:
                edge_u.append(du)
                edge_v.append(dv)
            else:
                du = merge_edge(du, edge_u[row], part) + load_group(dut_ref, row, part, levels)
                dv = merge_edge(dv, edge_v[row], part) + load_group(dvt_ref, row, part, levels)
                store_group(du_ref, row, part, levels, du)
                store_group(dv_ref, row, part, levels, dv)


def swaps(mesh_shape, along, parity):
    ny, nx = mesh_shape
    pairs = []
    for j in range(ny):
        for i in range(nx):
            k, size = (j, ny) if along == "y" else (i, nx)
            other = k + 1 if k % 2 == parity else k - 1
            if 0 <= other < size:
                pairs.append((j * nx + i, other * nx + i if along == "y" else j * nx + other))
    return pairs


def call(kernel, outs, args, scratch=(), flops=0, size=0):
    vmem = pl.BlockSpec(memory_space=pltpu.VMEM)
    return pl.pallas_call(
        kernel,
        out_shape=[jax.ShapeDtypeStruct(shape, jnp.float32) for shape in outs],
        in_specs=[vmem] * len(args),
        out_specs=[vmem] * len(outs),
        scratch_shapes=list(scratch),
        compiler_params=pltpu.CompilerParams(vmem_limit_bytes=48 * 1024 * 1024),
        cost_estimate=pl.CostEstimate(flops=flops, bytes_accessed=size, transcendentals=0),
    )(*args)


def on_device(shape, u, v, t, count, su, sv, st, elev):
    ny, nx = shape
    levels = u.shape[0]
    groups = group_count(levels)
    flat = (levels * SUB, LANES)
    u, v, t, su, sv, st = (field.reshape(flat) for field in (u, v, t, su, sv, st))
    peers = ny * nx // 2
    row_packet = ((N_SLOTS * groups + 1) * SUB, LANES)
    column_packet = ((SUB + 1) * SUB, LANES)
    chunk = (peers, CHUNK_ROW + groups * SUB, LANES)
    y1, y2, xp, chunks = call(
        functools.partial(pack_kernel, levels, peers),
        [row_packet, row_packet, column_packet, chunk],
        (u, v, t, su, sv, st, count, elev),
        flops=1 << 20,
        size=1 << 21,
    )
    axes = ("ty", "y", "core")
    ga = lax.all_to_all(chunks, ("ty", "y"), 0, 0)
    x1 = lax.ppermute(xp, axes, swaps(shape, "x", 0))
    x2 = lax.ppermute(xp, axes, swaps(shape, "x", 1))
    y1 = lax.ppermute(y1, axes, swaps(shape, "y", 0))
    y2 = lax.ppermute(y2, axes, swaps(shape, "y", 1))
    gb = lax.ppermute(ga, axes, swaps(shape, "x", 0))
    dt, du_t, dv_t = call(
        functools.partial(tracer_kernel, levels),
        [flat] * 3,
        (u, v, t, st, count, y1, y2, x1, x2),
        flops=1 << 22,
        size=1 << 21,
    )
    grid = pltpu.VMEM((ny, nx, SUB, LANES), jnp.float32)
    faces = pltpu.VMEM((4, ny, nx, SUB, LANES), jnp.float32)
    du, dv, eta = call(
        functools.partial(flow_kernel, levels, ny, nx),
        [flat, flat, (SUB, LANES)],
        (u, v, su, sv, ga, gb, y1, y2, x1, x2, du_t, dv_t),
        scratch=(grid, faces, grid, grid, grid, grid),
        flops=1 << 23,
        size=1 << 22,
    )
    whole = (levels, SUB, LANES)
    return du.reshape(whole), dv.reshape(whole), dt.reshape(whole), eta


def solution(mesh):
    ny, nx = mesh.shape["ty"], mesh.shape["tx"]
    split = Mesh(mesh.devices.reshape(ny, nx // 2, 2), ("ty", "y", "core"))
    deep, flat = P(None, "ty", ("y", "core")), P("ty", ("y", "core"))
    return jax.shard_map(
        functools.partial(on_device, (ny, nx)),
        mesh=split,
        in_specs=(deep, deep, deep, flat, deep, deep, deep, flat),
        out_specs=(deep, deep, deep, flat),
        check_vma=False,
    )
```

```python
import functools

import jax
import jax.numpy as jnp
from jax import lax
from jax.experimental import pallas as pl
from jax.experimental.pallas import tpu as pltpu
from jax.sharding import Mesh, PartitionSpec as P

ITERS = 4
ADVECT = 0.1
GRAVITY_DT = 0.1

SUB = 8
LANES = 128
SEG = 32
FIELDS = ("u", "v", "t", "st", "su", "sv")
SOUTH_SLOTS = {("u", -2): 0, ("u", -1): 1, ("v", -1): 2, ("t", -2): 3, ("t", -1): 4, ("st", -2): 5, ("st", -1): 6}
SOUTH_SLOTS.update({("su", -1): 7, ("sv", -1): 8})
NORTH_SLOTS = {("u", 8): 0, ("v", 8): 1, ("v", 9): 2, ("t", 8): 3, ("st", 8): 5, ("st", 9): 6, ("su", 8): 7, ("sv", 8): 8}
N_SLOTS = 9
CHUNK_LOAD = SUB
CHUNK_EDGE = 2 * SUB
CHUNK_ROW = 3 * SUB
CORNER_LANE = 32
CORNER_STEP = 24
CORNERS = (("u", 6, 0), ("u", 7, 0), ("u", 7, 1), ("su", 7, 0), ("v", 7, 127), ("u", 7, 127))
CORNERS += (("v", 0, 127), ("v", 1, 127), ("v", 0, 126), ("sv", 0, 127), ("v", 0, 0), ("u", 0, 0))
CORNER_PLACES = {
    ("u", -2): (("se", 0, 24),),
    ("u", -1): (("se", 1, 24), ("se", 2, 25), ("sw", 5, 7)),
    ("su", -1): (("se", 3, 24),),
    ("v", -1): (("sw", 4, 7),),
    ("v", 8): (("nw", 6, 7), ("nw", 8, 6), ("ne", 10, 24)),
    ("u", 8): (("ne", 11, 24),),
    ("v", 9): (("nw", 7, 7),),
    ("sv", 8): (("nw", 9, 7),),
}


def lane_ids():
    return lax.broadcasted_iota(jnp.int32, (SUB, LANES), 1)


def row_ids():
    return lax.broadcasted_iota(jnp.int32, (SUB, LANES), 0)


def roll_lanes(value, amount):
    amount %= LANES
    return value if amount == 0 else pltpu.roll(value, amount, 1)


def roll_rows(value, amount):
    amount %= SUB
    return value if amount == 0 else pltpu.roll(value, amount, 0)


def at(value, shift):
    return roll_lanes(value, -shift)


def row_of(tile, row):
    return jnp.broadcast_to(tile[row : row + 1, :], (SUB, LANES))


def group_count(levels):
    return -(-levels // SUB)


def load_group(ref, row, q, levels):
    first = min(q * SUB, levels - SUB)
    value = ref[pl.ds(first * SUB + row, SUB, stride=SUB), :]
    return roll_rows(value, first - q * SUB)


def store_group(ref, row, q, levels, value):
    count = min(SUB, levels - q * SUB)
    ref[pl.ds(q * SUB * SUB + row, count, stride=SUB), :] = value[:count]


def level_numbers(groups):
    rows = row_ids()
    numbers = [(rows + q * SUB).astype(jnp.float32) for q in range(groups)]
    return numbers + [(rows + (lane_ids() >> 5) * SUB).astype(jnp.float32)]


def edge_of_tile(west, centre, east):
    lanes = lane_ids()
    out = jnp.where(lanes < 8, roll_lanes(west, 8), roll_lanes(centre, 8))
    out = jnp.where(lanes >= 16, roll_lanes(centre, 24), out)
    out = jnp.where(lanes >= 24, roll_lanes(east, 24), out)
    out = jnp.where(lanes < SEG, out, roll_lanes(out, SEG))
    return jnp.where(lanes < 2 * SEG, out, roll_lanes(out, 2 * SEG))


def pack_kernel(
    levels, peers, u_hbm, v_hbm, t_hbm, su_hbm, sv_hbm, st_hbm, count_hbm, elev_hbm,
    y1_hbm, y2_hbm, x_hbm, chunk_hbm,
    u_ref, v_ref, t_ref, su_ref, sv_ref, st_ref, count_ref, elev_ref, y1_ref, y2_ref, x_ref, chunk_ref, sems,
):
    pairs = (
        (count_hbm, count_ref), (su_hbm, su_ref), (sv_hbm, sv_ref), (elev_hbm, elev_ref),
        (u_hbm, u_ref), (v_hbm, v_ref), (t_hbm, t_ref), (st_hbm, st_ref),
    )
    copies = [pltpu.make_async_copy(source, target, sems.at[n]) for n, (source, target) in enumerate(pairs)]
    for copy in copies:
        copy.start()
    for copy in copies:
        copy.wait()
    groups = group_count(levels)
    lanes, rows = lane_ids(), row_ids()
    even = lax.axis_index("ty") % 2 == 0
    refs = {"u": u_ref, "v": v_ref, "t": t_ref, "st": st_ref, "su": su_ref, "sv": sv_ref}
    count = count_ref[...].astype(jnp.float32)
    zero = jnp.zeros((SUB, LANES), jnp.float32)

    wet_u = jnp.where(lanes == 0, 0.0, jnp.minimum(count, roll_lanes(count, 1)))
    wet_v = jnp.where(rows == 0, 0.0, jnp.minimum(count, roll_rows(count, 1)))
    col_u, col_v, edge = zero, zero, zero
    for k in range(levels):
        su_level = su_ref[k * SUB : (k + 1) * SUB, :]
        col_u = col_u + jnp.where(wet_u > float(k), su_level, 0.0)
        col_v = col_v + jnp.where(wet_v > float(k), sv_ref[k * SUB : (k + 1) * SUB, :], 0.0)
        edge = jnp.where(lanes == k, roll_lanes(su_level, k), edge)
    load = elev_ref[...] + GRAVITY_DT * (at(col_u, 1) - col_u + roll_rows(col_v, -1) - col_v)

    loaded = {}
    for name in FIELDS:
        for row in range(SUB):
            for q in range(groups):
                loaded[name, row, q] = load_group(refs[name], row, q, levels)

    for place, (name, row, column) in enumerate(CORNERS):
        for q in range(groups):
            lane = CORNER_LANE + CORNER_STEP * q + place
            edge = jnp.where(lanes == lane, roll_lanes(loaded[name, row, q], lane - column), edge)

    chunk_ref[0:SUB, :] = count
    chunk_ref[CHUNK_LOAD : CHUNK_LOAD + SUB, :] = load
    chunk_ref[CHUNK_EDGE : CHUNK_EDGE + SUB, :] = edge
    for q in range(groups):
        chunk_ref[CHUNK_ROW + q * SUB : CHUNK_ROW + (q + 1) * SUB, :] = loaded["sv", 0, q]

    def put(peer, carry):
        pltpu.make_async_copy(chunk_ref, chunk_hbm.at[peer], sems.at[len(pairs)]).start()
        return carry

    lax.fori_loop(0, peers, put, 0, unroll=peers <= 32)

    for slot in range(N_SLOTS):
        upper = [(name, row + SUB) for (name, row), place in SOUTH_SLOTS.items() if place == slot]
        lower = [(name, row - SUB) for (name, row), place in NORTH_SLOTS.items() if place == slot]
        for q in range(groups):
            to_north = loaded[(*upper[0], q)]
            to_south = loaded[(*lower[0], q)] if lower else zero
            place = pl.ds((slot * groups + q) * SUB, SUB)
            y1_ref[place, :] = jnp.where(even, to_north, to_south)
            y2_ref[place, :] = jnp.where(even, to_south, to_north)
    y1_ref[N_SLOTS * groups * SUB :, :] = count
    y2_ref[N_SLOTS * groups * SUB :, :] = count
    out = [pltpu.make_async_copy(y1_ref, y1_hbm, sems.at[0]), pltpu.make_async_copy(y2_ref, y2_hbm, sems.at[1])]
    out[0].start()
    out[1].start()

    for row in range(SUB):
        packet = zero
        for field, name in enumerate(FIELDS):
            for q in range(groups):
                lane = SEG * q + 4 * field
                packet = jnp.where((lanes >= lane) & (lanes < lane + 4), roll_lanes(loaded[name, row, q], lane + 2), packet)
        x_ref[row * SUB : (row + 1) * SUB, :] = packet
    x_ref[SUB * SUB :, :] = count
    out.append(pltpu.make_async_copy(x_ref, x_hbm, sems.at[2]))
    out[2].start()
    for copy in out:
        copy.wait()
    pltpu.make_async_copy(chunk_hbm, chunk_hbm, sems.at[len(pairs)]).wait()


class Many:
    def __init__(self, items):
        self.items = list(items)

    def __getitem__(self, where):
        return Many(self.items[where]) if isinstance(where, slice) else self.items[where]

    def __len__(self):
        return len(self.items)

    def apply(self, operation, *others):
        others = [other.items if isinstance(other, Many) else [other] * len(self) for other in others]
        assert all(len(other) == len(self) for other in others)
        return Many(operation(*parts) for parts in zip(self.items, *others))

    def __add__(self, other):
        return self.apply(lambda a, b: a + b, other)

    def __sub__(self, other):
        return self.apply(lambda a, b: a - b, other)

    def __mul__(self, other):
        return self.apply(lambda a, b: a * b, other)

    def __gt__(self, other):
        return self.apply(lambda a, b: a > b, other)

    def at(self, shift):
        return self.apply(lambda a: at(a, shift))

    def rolled(self, amount):
        return self.apply(lambda a: roll_lanes(a, amount))

    def minimum(self, other):
        return self.apply(jnp.minimum, other)

    def where(self, mask, other):
        return self.apply(lambda a, m, b: jnp.where(m, a, b), mask, other)


def edges_of_groups(parts):
    lanes = lane_ids()
    out = parts[0].rolled(8)
    for q in range(1, len(parts)):
        out = parts[q].rolled(SEG * q + 8).where(lanes >= SEG * q, out)
    return out.rolled(16).where((lanes & (SEG - 1)) >= 16, out)


def insert_sides(edge, west, east, field):
    place = lane_ids() & (SEG - 1)
    edge = west.rolled(6 - 4 * field).where((place == 6) | (place == 7), edge)
    return east.rolled(22 - 4 * field).where((place == 24) | (place == 25), edge)


def merge_edges(values, edge, q):
    lanes = lane_ids()
    values = edge.rolled(-(SEG * q + 8)).where(lanes < 2, values)
    return edge.rolled(104 - SEG * q).where(lanes >= LANES - 2, values)


def load_rows(ref, q, levels):
    return Many(load_group(ref, row, q, levels) for row in range(SUB))


def store_rows(ref, q, levels, values):
    for row in range(SUB):
        store_group(ref, row, q, levels, values[row])


def rows_of(tiles, first, last):
    return Many(row_of(tiles[row // SUB + 1], row % SUB) for row in range(first, last + 1))


def slot_reader(y1_ref, y2_ref, groups):
    even = lax.axis_index("ty") % 2 == 0

    def read(name, row, q):
        slot = (SOUTH_SLOTS if row < 0 else NORTH_SLOTS)[name, row]
        place = pl.ds((slot * groups + q) * SUB, SUB)
        one, two = y1_ref[place, :], y2_ref[place, :]
        return jnp.where(even, two, one) if row < 0 else jnp.where(even, one, two)

    def counts():
        place = pl.ds(N_SLOTS * groups * SUB, SUB)
        one, two = y1_ref[place, :], y2_ref[place, :]
        return jnp.where(even, two, one), jnp.where(even, one, two)

    return read, counts


def side_reader(x1_ref, x2_ref):
    even = lax.axis_index("core") % 2 == 0

    def read(row):
        place = pl.ds(row * SUB, SUB)
        one, two = x1_ref[place, :], x2_ref[place, :]
        return jnp.where(even, two, one), jnp.where(even, one, two)

    return read


def face_values(t0, t_before, t_after, t_before2):
    return ((t0 + t_before) * 7.0 - (t_after + t_before2)) * (1.0 / 12.0)


def tracer_kernel(levels, u_ref, v_ref, t_ref, st_ref, count_ref, y1_ref, y2_ref, x1_ref, x2_ref, dt_ref, du_ref, dv_ref):
    groups = group_count(levels)
    read_row, read_counts = slot_reader(y1_ref, y2_ref, groups)
    read_sides = side_reader(x1_ref, x2_ref)
    numbers = level_numbers(groups)
    zero = jnp.zeros((SUB, LANES), jnp.float32)

    count = count_ref[...].astype(jnp.float32)
    count_south, count_north = read_counts()
    count_west, count_east = read_sides(SUB)
    count_edge = edge_of_tile(count_west, count, count_east)
    counts = rows_of((count_south, count, count_north), -2, 9)
    counts_v = counts[1:].minimum(counts[:-1])
    own = (None, count, None)
    counts_u = rows_of((None, jnp.minimum(count, at(count, -1)), None), 0, 7)
    edge_counts = rows_of((None, count_edge, None), 0, 7)
    edge_counts_u = rows_of((None, jnp.minimum(count_edge, at(count_edge, -1)), None), 0, 7)
    del own

    def along_columns(level, wet, wet_u, u, t, st):
        cell = (st * -ADVECT).where(wet > level, zero)
        flux = (cell.at(-1) - cell).where(wet_u > level, zero)
        back = u * flux
        face = face_values(t, t.at(-1), t.at(1), t.at(-2))
        return ((back + back.at(1)) * 7.0 - (back.at(-1) + back.at(2))) * (1.0 / 12.0), flux * face

    sides = [read_sides(row) for row in range(SUB)]
    west, east = Many(side[0] for side in sides), Many(side[1] for side in sides)
    u, t, st = (
        insert_sides(
            edges_of_groups([load_rows(ref, q, levels) for q in range(groups)]), west, east, FIELDS.index(name)
        )
        for name, ref in (("u", u_ref), ("t", t_ref), ("st", st_ref))
    )
    edge_t, edge_u = along_columns(numbers[groups], edge_counts, edge_counts_u, u, t, st)

    for q in range(groups):
        level = numbers[q]

        def rows(name, ref, first, last):
            south = [read_row(name, row, q) for row in range(first, 0)]
            north = [read_row(name, row, q) for row in range(SUB, last + 1)]
            return Many(south + load_rows(ref, q, levels).items + north)

        t, st, v = rows("t", t_ref, -2, 8), rows("st", st_ref, -2, 9), rows("v", v_ref, -1, 9)
        from_x, to_u = along_columns(level, counts[2:10], counts_u, load_rows(u_ref, q, levels), t[2:10], st[2:10])
        cell = (st * -ADVECT).where(counts > level, zero)
        flux = (cell[:-1] - cell[1:]).where(counts_v > level, zero)
        back = v * flux
        from_y = ((back[1:9] + back[2:10]) * 7.0 - (back[0:8] + back[3:11])) * (1.0 / 12.0)
        to_v = flux[1:9] * face_values(t[2:10], t[1:9], t[3:11], t[0:8])
        store_rows(dt_ref, q, levels, st[2:10] + merge_edges(from_x, edge_t, q) + from_y)
        store_rows(du_ref, q, levels, merge_edges(to_u, edge_u, q))
        store_rows(dv_ref, q, levels, to_v)


def total(value):
    return jnp.sum(value, axis=(0, 1), keepdims=True)


def surface_solve(levels, ny, nx, read, count_ref, face_ref, x_ref, r_ref, p_ref):
    groups = group_count(levels)
    lanes, rows = lane_ids(), row_ids()
    numbers = level_numbers(groups)
    zero = jnp.zeros((SUB, LANES), jnp.float32)
    band = max(1, min(ny, 32 // nx))
    while ny % band:
        band -= 1
    cells = [(dj, i) for dj in range(band) for i in range(nx)]

    def loop(body, init=0):
        if band == ny:
            return body(0, init)
        return lax.fori_loop(0, ny // band, lambda step, carry: body(step * band, carry), init)

    def get(ref, j):
        return Many(ref[j + dj, i] for dj, i in cells)

    def put(ref, j, values):
        for (dj, i), value in zip(cells, values.items):
            ref[j + dj, i] = value

    def beside(values, step):
        return Many(values[dj * nx + min(max(i + step, 0), nx - 1)] for dj, i in cells)

    def below(ref, j, values):
        outside = [ref[jnp.maximum(j - 1, 0), i] for i in range(nx)] if band < ny else values.items[:nx]
        return Many(outside + values.items[:-nx])

    def above(ref, j, values):
        outside = [ref[jnp.minimum(j + band, ny - 1), i] for i in range(nx)] if band < ny else values.items[-nx:]
        return Many(values.items[nx:] + outside)

    def west_of(values):
        return beside(values, -1).where(lanes == LANES - 1, values).rolled(1)

    def east_of(values):
        return beside(values, 1).where(lanes == 0, values).rolled(-1)

    def south_of(ref, j, values):
        return below(ref, j, values).where(rows == SUB - 1, values).apply(lambda a: roll_rows(a, 1))

    def north_of(ref, j, values):
        return above(ref, j, values).where(rows == 0, values).apply(lambda a: roll_rows(a, -1))

    def depth(wet):
        return wet.apply(lambda m: GRAVITY_DT * (m + m * (m - 1.0) * (0.5 / levels)))

    def gather(j, carry):
        put(count_ref, j, Many(read(j + dj, i, 0) for dj, i in cells))
        return carry

    loop(gather)

    def faces(j, carry):
        count = get(count_ref, j)
        wet_u, wet_v = count.minimum(west_of(count)), count.minimum(south_of(count_ref, j, count))
        first_column = [(lanes == 0) if i == 0 else (lanes < 0) for dj, i in cells]
        first_row = [(rows == 0) & (j + dj == 0) for dj, i in cells]
        wet_u = Many([zero] * len(cells)).where(Many(first_column), wet_u)
        wet_v = Many([zero] * len(cells)).where(Many(first_row), wet_v)
        put(face_ref.at[0], j, depth(wet_u))
        put(face_ref.at[1], j, depth(wet_v))
        edge = Many(read(j + dj, i, CHUNK_EDGE) for dj, i in cells)
        wet_west = wet_u.apply(lambda a: jnp.broadcast_to(a[:, 0:1], (SUB, LANES)))
        reach = jnp.where(lanes < levels, lanes.astype(jnp.float32), float(levels))
        inside = edge.where(wet_west > reach, zero)
        col_u = inside.apply(lambda a: jnp.broadcast_to(jnp.sum(a, axis=1, keepdims=True), (SUB, LANES)))
        put(face_ref.at[4], j, col_u * GRAVITY_DT)
        wet_south = wet_v.apply(lambda a: row_of(a, 0))
        col_v = Many([zero] * len(cells))
        for q in range(groups):
            south = Many(read(j + dj, i, CHUNK_ROW + q * SUB) for dj, i in cells)
            col_v = col_v + south.where(wet_south > numbers[q], zero)
        col_v = col_v.apply(lambda a: jnp.broadcast_to(jnp.sum(a, axis=0, keepdims=True), (SUB, LANES)))
        put(face_ref.at[5], j, col_v * GRAVITY_DT)
        return carry

    loop(faces)

    def start(j, norm):
        load = Many(read(j + dj, i, CHUNK_LOAD) for dj, i in cells)
        col_u, col_v = get(face_ref.at[4], j), get(face_ref.at[5], j)
        depth_u, depth_v = get(face_ref.at[0], j), get(face_ref.at[1], j)
        last_column = Many((lanes == LANES - 1) if i + 1 < nx else (lanes < 0) for dj, i in cells)
        at_end = Many((lanes == LANES - 1) if i + 1 == nx else (lanes < 0) for dj, i in cells)
        last_row = Many((rows == SUB - 1) & (j + dj + 1 < ny) for dj, i in cells)
        at_top = Many((rows == SUB - 1) & (j + dj + 1 == ny) for dj, i in cells)
        none = Many([zero] * len(cells))
        load = load - col_u.where(lanes == 0, zero) - col_v.where(rows == 0, zero)
        load = load + beside(col_u, 1).where(last_column, none) + above(face_ref.at[5], j, col_v).where(last_row, none)
        put(face_ref.at[2], j, none.where(at_end, east_of(depth_u)))
        put(face_ref.at[3], j, none.where(at_top, north_of(face_ref.at[1], j, depth_v)))
        put(r_ref, j, load)
        put(p_ref, j, load)
        put(x_ref, j, none)
        return gathered(norm, load * load)

    def gathered(partial, values):
        items = list(values.items)
        while len(items) > 1:
            items = [a + b for a, b in zip(items[::2], items[1::2])] + items[len(items) // 2 * 2 :]
        return partial + items[0]

    norm = total(loop(start, zero))

    for iteration in range(ITERS):
        last = iteration + 1 == ITERS

        def image_of(j):
            p = get(p_ref, j)
            image = p + get(face_ref.at[0], j) * (p - west_of(p)) + get(face_ref.at[2], j) * (p - east_of(p))
            image = image + get(face_ref.at[1], j) * (p - south_of(p_ref, j, p))
            return p, image + get(face_ref.at[3], j) * (p - north_of(p_ref, j, p))

        def product(j, dot):
            p, image = image_of(j)
            put(face_ref.at[4], j, image)
            return gathered(dot, p * image)

        step = norm / total(loop(product, zero))

        def advance(j, new):
            put(x_ref, j, get(x_ref, j) + get(p_ref, j) * step)
            if last:
                return new
            residual = get(r_ref, j) - get(face_ref.at[4], j) * step
            put(r_ref, j, residual)
            return gathered(new, residual * residual)

        new = loop(advance, zero)
        if not last:
            new = total(new)
            ratio = new / norm
            norm = new

            def turn(j, carry):
                put(p_ref, j, get(r_ref, j) + get(p_ref, j) * ratio)
                return carry

            loop(turn)


def flow_kernel(
    levels, ny, nx, u_ref, v_ref, su_ref, sv_ref, ga_ref, gb_ref, y1_ref, y2_ref, x1_ref, x2_ref, dut_ref, dvt_ref,
    du_ref, dv_ref, eta_ref, count_s, face_s, x_s, r_s, p_s,
):
    groups = group_count(levels)
    lanes = lane_ids()
    core = lax.axis_index("core")
    my_j = lax.axis_index("ty")
    my_i = lax.axis_index("y") * 2 + core
    numbers = level_numbers(groups)
    thick = [1.0 + number * (1.0 / levels) for number in numbers]
    read_row, _ = slot_reader(y1_ref, y2_ref, groups)
    read_sides = side_reader(x1_ref, x2_ref)
    zero = jnp.zeros((SUB, LANES), jnp.float32)

    def read(j, i, first):
        where = (j * (nx // 2) + i // 2, pl.ds(first, SUB), slice(None))
        return jnp.where(core == i % 2, ga_ref[where], gb_ref[where])

    surface_solve(levels, ny, nx, read, count_s, face_s, x_s, r_s, p_s)
    eta_ref[...] = x_s[my_j, my_i]

    def near(dj, di, get):
        j, i = jnp.clip(my_j + dj, 0, ny - 1), jnp.clip(my_i + di, 0, nx - 1)
        inside = (my_j + dj >= 0) & (my_j + dj < ny) & (my_i + di >= 0) & (my_i + di < nx)
        return jnp.where(inside, get(j, i), 0.0)

    def around(ref):
        tiles = [[near(dj, di, lambda j, i: ref[j, i]) for di in (-1, 0, 1)] for dj in (-1, 0, 1)]
        return [row[1] for row in tiles], [edge_of_tile(*row) for row in tiles]

    count_tiles, x_tiles = around(count_s), around(x_s)

    corner_tiles = {
        name: near(dj, di, lambda j, i: read(j, i, CHUNK_EDGE))
        for name, dj, di in (("se", -1, 1), ("sw", -1, -1), ("nw", 1, -1), ("ne", 1, 1))
    }

    def insert_corners(edge, name, row):
        for which, value, target in CORNER_PLACES.get((name, row), ()):
            for q in range(groups):
                lane = SEG * q + target
                source = CORNER_LANE + CORNER_STEP * q + value
                edge = jnp.where(lanes == lane, roll_lanes(corner_tiles[which], lane - source), edge)
        return edge

    sides = [read_sides(row) for row in range(SUB)]
    west, east = Many(side[0] for side in sides), Many(side[1] for side in sides)

    def rows(name, ref, q, first, last):
        south = [read_row(name, row, q) for row in range(first, 0)]
        north = [read_row(name, row, q) for row in range(SUB, last + 1)]
        return Many(south + load_rows(ref, q, levels).items + north)

    def edges(name, ref, first, last):
        out = edges_of_groups([rows(name, ref, q, first, last) for q in range(groups)])
        south = [insert_corners(out[row - first], name, row) for row in range(first, 0)]
        north = [insert_corners(out[row - first], name, row) for row in range(SUB, last + 1)]
        inner = insert_sides(out[-first : SUB - first], west, east, FIELDS.index(name))
        return Many(south + inner.items + north)

    total_rows = ny * SUB
    first_row = (my_j * SUB).astype(jnp.float32)
    turn_u = Many(0.5 + (first_row + (row + 0.5)) * (1.0 / total_rows) for row in range(-1, 8))
    turn_v = Many(-0.5 - (first_row + row) * (1.0 / total_rows) for row in range(0, 9))

    def adjoint(part, u, v, su, sv):
        kind = 1 if part == groups else 0
        level = numbers[part]
        counts, x = rows_of(count_tiles[kind], -2, 8), rows_of(x_tiles[kind], -2, 8)
        wet_u = counts[1:].minimum(counts[1:].at(-1)) > level
        wet_v = counts[1:].minimum(counts[:-1]) > level
        u_cot = su + ((x[1:] - x[1:].at(-1)) * thick[part]).where(wet_u, zero)
        v_cot = sv + ((x[1:] - x[:-1]) * thick[part]).where(wet_v, zero)
        a, b = (u_cot * ADVECT).where(wet_u, zero), (v_cot * ADVECT).where(wet_v, zero)
        v_pair = v[:-1] + v[1:]
        av = a * (v_pair + v_pair.at(-1)) * 0.25
        u_pair = u[2:10] + u[1:9]
        bu = b[1:9] * (u_pair + u_pair.at(1)) * 0.25
        au, bv = a[1:9] * u[2:10], b * v[:-1]
        to_v_bar = a[:-1] * ((u[:-2] - u[2:]) * 0.5 + turn_u)
        to_u_bar = b[1:] * ((v[1:10].at(-1) - v[1:10].at(1)) * 0.5 + turn_v)
        near_u, near_v = to_u_bar[:-1] + to_u_bar[1:], to_v_bar[1:] + to_v_bar[:-1]
        twist_u = au.at(1) - au.at(-1) - a[1:9] * (u[2:10].at(1) - u[2:10].at(-1)) + av[2:] - av[:-2]
        twist_v = bu.at(1) - bu.at(-1) - b[1:9] * (v[2:10] - v[0:8]) + bv[2:] - bv[:-2]
        du = u_cot[1:9] + twist_u * 0.5 + (near_u + near_u.at(-1)) * 0.25
        dv = v_cot[1:9] + twist_v * 0.5 + (near_v + near_v.at(1)) * 0.25
        return du, dv

    fields = (("u", u_ref, -2, 8), ("v", v_ref, -1, 9), ("su", su_ref, -1, 8), ("sv", sv_ref, -1, 8))
    edge_u, edge_v = adjoint(groups, *(edges(*field) for field in fields))
    for q in range(groups):
        du, dv = adjoint(q, *(rows(name, ref, q, first, last) for name, ref, first, last in fields))
        store_rows(du_ref, q, levels, merge_edges(du, edge_u, q) + load_rows(dut_ref, q, levels))
        store_rows(dv_ref, q, levels, merge_edges(dv, edge_v, q) + load_rows(dvt_ref, q, levels))


def swaps(mesh_shape, along, parity):
    ny, nx = mesh_shape
    pairs = []
    for j in range(ny):
        for i in range(nx):
            k, size = (j, ny) if along == "y" else (i, nx)
            other = k + 1 if k % 2 == parity else k - 1
            if 0 <= other < size:
                pairs.append((j * nx + i, other * nx + i if along == "y" else j * nx + other))
    return pairs


def call(kernel, outs, args, scratch=(), flops=0, size=0, far_in=False, far_out=(), limit=48):
    near, far = pl.BlockSpec(memory_space=pltpu.VMEM), pl.BlockSpec(memory_space=pltpu.HBM)
    outs = [out if isinstance(out, jax.ShapeDtypeStruct) else jax.ShapeDtypeStruct(out, jnp.float32) for out in outs]
    return pl.pallas_call(
        kernel,
        out_shape=outs,
        in_specs=[far if far_in else near] * len(args),
        out_specs=[far if n in far_out else near for n in range(len(outs))],
        scratch_shapes=list(scratch),
        compiler_params=pltpu.CompilerParams(vmem_limit_bytes=limit * 1024 * 1024),
        cost_estimate=pl.CostEstimate(flops=flops, bytes_accessed=size, transcendentals=0),
    )(*args)


def on_device(shape, u, v, t, count, su, sv, st, elev):
    ny, nx = shape
    levels = u.shape[0]
    groups = group_count(levels)
    flat = (levels * SUB, LANES)
    u, v, t, su, sv, st = (field.reshape(flat) for field in (u, v, t, su, sv, st))
    peers = ny * nx // 2
    row_packet = ((N_SLOTS * groups + 1) * SUB, LANES)
    column_packet = ((SUB + 1) * SUB, LANES)
    chunk = (peers, CHUNK_ROW + groups * SUB, LANES)
    tile = (SUB, LANES)
    y1, y2, xp, chunks = call(
        functools.partial(pack_kernel, levels, peers),
        [row_packet, row_packet, column_packet, chunk],
        (u, v, t, su, sv, st, count, elev),
        scratch=[pltpu.VMEM(flat, jnp.float32)] * 6
        + [pltpu.VMEM(tile, count.dtype)]
        + [pltpu.VMEM(shape, jnp.float32) for shape in (tile, row_packet, row_packet, column_packet, chunk[1:])]
        + [pltpu.SemaphoreType.DMA((9,))],
        flops=1 << 20,
        size=1 << 21,
        far_in=True,
        far_out=(0, 1, 2, 3),
        limit=60,
    )
    axes = ("ty", "y", "core")
    ga = lax.all_to_all(chunks, ("ty", "y"), 0, 0)
    x1 = lax.ppermute(xp, axes, swaps(shape, "x", 0))
    x2 = lax.ppermute(xp, axes, swaps(shape, "x", 1))
    y1 = lax.ppermute(y1, axes, swaps(shape, "y", 0))
    y2 = lax.ppermute(y2, axes, swaps(shape, "y", 1))
    dt, du_t, dv_t = call(
        functools.partial(tracer_kernel, levels),
        [flat] * 3,
        (u, v, t, st, count, y1, y2, x1, x2),
        flops=1 << 22,
        size=1 << 21,
    )
    ga, du_t = lax.optimization_barrier((ga, du_t))
    gb = lax.ppermute(ga, axes, swaps(shape, "x", 0))
    grid = pltpu.VMEM((ny, nx, SUB, LANES), jnp.float32)
    faces = pltpu.VMEM((6, ny, nx, SUB, LANES), jnp.float32)
    du, dv, eta = call(
        functools.partial(flow_kernel, levels, ny, nx),
        [flat, flat, (SUB, LANES)],
        (u, v, su, sv, ga, gb, y1, y2, x1, x2, du_t, dv_t),
        scratch=(grid, faces, grid, grid, grid),
        flops=1 << 23,
        size=1 << 22,
    )
    whole = (levels, SUB, LANES)
    return du.reshape(whole), dv.reshape(whole), dt.reshape(whole), eta


def solution(mesh):
    ny, nx = mesh.shape["ty"], mesh.shape["tx"]
    split = Mesh(mesh.devices.reshape(ny, nx // 2, 2), ("ty", "y", "core"))
    deep, flat = P(None, "ty", ("y", "core")), P("ty", ("y", "core"))
    return jax.shard_map(
        functools.partial(on_device, (ny, nx)),
        mesh=split,
        in_specs=(deep, deep, deep, flat, deep, deep, deep, flat),
        out_specs=(deep, deep, deep, flat),
        check_vma=False,
    )
```

```python
import functools

import jax
import jax.numpy as jnp
from jax import lax
from jax.experimental import pallas as pl
from jax.experimental.pallas import tpu as pltpu
from jax.sharding import Mesh, PartitionSpec as P

ITERS = 4
ADVECT = 0.1
GRAVITY_DT = 0.1

SUB = 8
LANES = 128
SEG = 32
FIELDS = ("u", "v", "t", "st", "su", "sv")
FLOW_FIELDS = ("u", "v", "su", "sv")
SOUTH_SLOTS = {("u", -2): 0, ("u", -1): 1, ("v", -1): 2, ("t", -2): 3, ("t", -1): 4, ("st", -2): 5, ("st", -1): 6}
SOUTH_SLOTS.update({("su", -1): 7, ("sv", -1): 8})
NORTH_SLOTS = {("u", 8): 0, ("v", 8): 1, ("v", 9): 2, ("t", 8): 3, ("st", 8): 5, ("st", 9): 6, ("su", 8): 7, ("sv", 8): 8}
N_SLOTS = 9
CHUNK_LOAD = SUB
CHUNK_EDGE = 2 * SUB
CHUNK_ROW = 3 * SUB
CORNER_LANE = 32
CORNER_STEP = 24
CORNERS = (("u", 6, 0), ("u", 7, 0), ("u", 7, 1), ("su", 7, 0), ("v", 7, 127), ("u", 7, 127))
CORNERS += (("v", 0, 127), ("v", 1, 127), ("v", 0, 126), ("sv", 0, 127), ("v", 0, 0), ("u", 0, 0))
CORNER_PLACES = {
    ("u", -2): (("se", 0, 24),),
    ("u", -1): (("se", 1, 24), ("se", 2, 25), ("sw", 5, 7)),
    ("su", -1): (("se", 3, 24),),
    ("v", -1): (("sw", 4, 7),),
    ("v", 8): (("nw", 6, 7), ("nw", 8, 6), ("ne", 10, 24)),
    ("u", 8): (("ne", 11, 24),),
    ("v", 9): (("nw", 7, 7),),
    ("sv", 8): (("nw", 9, 7),),
}


def lane_ids():
    return lax.broadcasted_iota(jnp.int32, (SUB, LANES), 1)


def row_ids():
    return lax.broadcasted_iota(jnp.int32, (SUB, LANES), 0)


def roll_lanes(value, amount):
    amount %= LANES
    return value if amount == 0 else pltpu.roll(value, amount, 1)


def roll_rows(value, amount):
    amount %= SUB
    return value if amount == 0 else pltpu.roll(value, amount, 0)


def at(value, shift):
    return roll_lanes(value, -shift)


def row_of(tile, row):
    return jnp.broadcast_to(tile[row : row + 1, :], (SUB, LANES))


def group_count(levels):
    return -(-levels // SUB)


def load_group(ref, row, q, levels):
    first = min(q * SUB, levels - SUB)
    value = ref[pl.ds(first * SUB + row, SUB, stride=SUB), :]
    return roll_rows(value, first - q * SUB)


def store_group(ref, row, q, levels, value):
    count = min(SUB, levels - q * SUB)
    ref[pl.ds(q * SUB * SUB + row, count, stride=SUB), :] = value[:count]


def level_numbers(groups):
    rows = row_ids()
    numbers = [(rows + q * SUB).astype(jnp.float32) for q in range(groups)]
    return numbers + [(rows + (lane_ids() >> 5) * SUB).astype(jnp.float32)]


def edge_of_tile(west, centre, east):
    lanes = lane_ids()
    out = jnp.where(lanes < 8, roll_lanes(west, 8), roll_lanes(centre, 8))
    out = jnp.where(lanes >= 16, roll_lanes(centre, 24), out)
    out = jnp.where(lanes >= 24, roll_lanes(east, 24), out)
    out = jnp.where(lanes < SEG, out, roll_lanes(out, SEG))
    return jnp.where(lanes < 2 * SEG, out, roll_lanes(out, 2 * SEG))


def chunk_kernel(
    levels, peers, u_hbm, v_hbm, su_hbm, sv_hbm, count_hbm, elev_hbm, chunk_hbm,
    u_ref, v_ref, su_ref, sv_ref, count_ref, elev_ref, chunk_ref, sems,
):
    pairs = (
        (count_hbm, count_ref), (su_hbm, su_ref), (sv_hbm, sv_ref), (elev_hbm, elev_ref), (u_hbm, u_ref), (v_hbm, v_ref),
    )
    copies = [pltpu.make_async_copy(source, target, sems.at[n]) for n, (source, target) in enumerate(pairs)]
    for copy in copies:
        copy.start()
    groups = group_count(levels)
    lanes, rows = lane_ids(), row_ids()
    refs = {"u": u_ref, "v": v_ref, "su": su_ref, "sv": sv_ref}
    for copy in copies[:4]:
        copy.wait()
    count = count_ref[...].astype(jnp.float32)
    zero = jnp.zeros((SUB, LANES), jnp.float32)

    wet_u = jnp.where(lanes == 0, 0.0, jnp.minimum(count, roll_lanes(count, 1)))
    wet_v = jnp.where(rows == 0, 0.0, jnp.minimum(count, roll_rows(count, 1)))
    col_u, col_v, edge = [zero] * 4, [zero] * 4, zero
    for k in range(levels):
        su_level = su_ref[k * SUB : (k + 1) * SUB, :]
        col_u[k % 4] = col_u[k % 4] + jnp.where(wet_u > float(k), su_level, 0.0)
        col_v[k % 4] = col_v[k % 4] + jnp.where(wet_v > float(k), sv_ref[k * SUB : (k + 1) * SUB, :], 0.0)
        edge = jnp.where(lanes == k, roll_lanes(su_level, k), edge)
    col_u, col_v = ((col[0] + col[1]) + (col[2] + col[3]) for col in (col_u, col_v))
    load = elev_ref[...] + GRAVITY_DT * (at(col_u, 1) - col_u + roll_rows(col_v, -1) - col_v)

    for copy in copies[4:]:
        copy.wait()
    for place, (name, row, column) in enumerate(CORNERS):
        for q in range(groups):
            lane = CORNER_LANE + CORNER_STEP * q + place
            edge = jnp.where(lanes == lane, roll_lanes(load_group(refs[name], row, q, levels), lane - column), edge)

    chunk_ref[0:SUB, :] = count
    chunk_ref[CHUNK_LOAD : CHUNK_LOAD + SUB, :] = load
    chunk_ref[CHUNK_EDGE : CHUNK_EDGE + SUB, :] = edge
    for q in range(groups):
        chunk_ref[CHUNK_ROW + q * SUB : CHUNK_ROW + (q + 1) * SUB, :] = load_group(sv_ref, 0, q, levels)

    def put(peer, carry):
        pltpu.make_async_copy(chunk_ref, chunk_hbm.at[peer], sems.at[len(pairs)]).start()
        return carry

    lax.fori_loop(0, peers, put, 0, unroll=peers <= 32)
    pltpu.make_async_copy(chunk_hbm, chunk_hbm, sems.at[len(pairs)]).wait()


def packet_kernel(levels, u_ref, v_ref, t_ref, su_ref, sv_ref, st_ref, count_ref, y1_ref, y2_ref, x_ref):
    groups = group_count(levels)
    lanes = lane_ids()
    zero = jnp.zeros((SUB, LANES), jnp.float32)
    count = count_ref[...].astype(jnp.float32)
    even = lax.axis_index("ty") % 2 == 0
    refs = {"u": u_ref, "v": v_ref, "t": t_ref, "st": st_ref, "su": su_ref, "sv": sv_ref}
    loaded = {}
    for name in FIELDS:
        for row in range(SUB):
            for q in range(groups):
                loaded[name, row, q] = load_group(refs[name], row, q, levels)

    for slot in range(N_SLOTS):
        upper = [(name, row + SUB) for (name, row), place in SOUTH_SLOTS.items() if place == slot]
        lower = [(name, row - SUB) for (name, row), place in NORTH_SLOTS.items() if place == slot]
        for q in range(groups):
            to_north = loaded[(*upper[0], q)]
            to_south = loaded[(*lower[0], q)] if lower else zero
            place = pl.ds((slot * groups + q) * SUB, SUB)
            y1_ref[place, :] = jnp.where(even, to_north, to_south)
            y2_ref[place, :] = jnp.where(even, to_south, to_north)
    y1_ref[N_SLOTS * groups * SUB :, :] = count
    y2_ref[N_SLOTS * groups * SUB :, :] = count

    for row in range(SUB):
        packet = zero
        for field, name in enumerate(FIELDS):
            for q in range(groups):
                lane = SEG * q + 4 * field
                packet = jnp.where((lanes >= lane) & (lanes < lane + 4), roll_lanes(loaded[name, row, q], lane + 2), packet)
        x_ref[row * SUB : (row + 1) * SUB, :] = packet
    x_ref[SUB * SUB :, :] = count


class Many:
    def __init__(self, items):
        self.items = list(items)

    def __getitem__(self, where):
        return Many(self.items[where]) if isinstance(where, slice) else self.items[where]

    def __len__(self):
        return len(self.items)

    def apply(self, operation, *others):
        others = [other.items if isinstance(other, Many) else [other] * len(self) for other in others]
        assert all(len(other) == len(self) for other in others)
        return Many(operation(*parts) for parts in zip(self.items, *others))

    def __add__(self, other):
        return self.apply(lambda a, b: a + b, other)

    def __sub__(self, other):
        return self.apply(lambda a, b: a - b, other)

    def __mul__(self, other):
        return self.apply(lambda a, b: a * b, other)

    def __gt__(self, other):
        return self.apply(lambda a, b: a > b, other)

    def at(self, shift):
        return self.apply(lambda a: at(a, shift))

    def rolled(self, amount):
        return self.apply(lambda a: roll_lanes(a, amount))

    def minimum(self, other):
        return self.apply(jnp.minimum, other)

    def where(self, mask, other):
        return self.apply(lambda a, m, b: jnp.where(m, a, b), mask, other)


def edges_of_groups(parts):
    lanes = lane_ids()
    out = parts[0].rolled(8)
    for q in range(1, len(parts)):
        out = parts[q].rolled(SEG * q + 8).where(lanes >= SEG * q, out)
    return out.rolled(16).where((lanes & (SEG - 1)) >= 16, out)


def insert_sides(edge, west, east, field):
    place = lane_ids() & (SEG - 1)
    edge = west.rolled(6 - 4 * field).where((place == 6) | (place == 7), edge)
    return east.rolled(22 - 4 * field).where((place == 24) | (place == 25), edge)


def merge_edges(values, edge, q):
    lanes = lane_ids()
    values = edge.rolled(-(SEG * q + 8)).where(lanes < 2, values)
    return edge.rolled(104 - SEG * q).where(lanes >= LANES - 2, values)


def load_rows(ref, q, levels):
    return Many(load_group(ref, row, q, levels) for row in range(SUB))


def store_rows(ref, q, levels, values):
    for row in range(SUB):
        store_group(ref, row, q, levels, values[row])


def rows_of(tiles, first, last):
    return Many(row_of(tiles[row // SUB + 1], row % SUB) for row in range(first, last + 1))


def slot_reader(y1_ref, y2_ref, groups):
    even = lax.axis_index("ty") % 2 == 0

    def read(name, row, q):
        slot = (SOUTH_SLOTS if row < 0 else NORTH_SLOTS)[name, row]
        place = pl.ds((slot * groups + q) * SUB, SUB)
        one, two = y1_ref[place, :], y2_ref[place, :]
        return jnp.where(even, two, one) if row < 0 else jnp.where(even, one, two)

    def counts():
        place = pl.ds(N_SLOTS * groups * SUB, SUB)
        one, two = y1_ref[place, :], y2_ref[place, :]
        return jnp.where(even, two, one), jnp.where(even, one, two)

    return read, counts


def side_reader(x1_ref, x2_ref):
    even = lax.axis_index("core") % 2 == 0

    def read(row):
        place = pl.ds(row * SUB, SUB)
        one, two = x1_ref[place, :], x2_ref[place, :]
        return jnp.where(even, two, one), jnp.where(even, one, two)

    return read


def face_values(t0, t_before, t_after, t_before2):
    return ((t0 + t_before) * 7.0 - (t_after + t_before2)) * (1.0 / 12.0)


def edge_rows(ref, west, east, levels, groups, name):
    own = edges_of_groups([load_rows(ref, q, levels) for q in range(groups)])
    return insert_sides(own, west, east, FIELDS.index(name))


def column_kernel(
    levels, u_ref, v_ref, t_ref, st_ref, su_ref, sv_ref, count_ref, x1_ref, x2_ref, dt_ref, du_ref, edge_ref
):
    groups = group_count(levels)
    read_sides = side_reader(x1_ref, x2_ref)
    numbers = level_numbers(groups)
    zero = jnp.zeros((SUB, LANES), jnp.float32)
    count = count_ref[...].astype(jnp.float32)
    count_west, count_east = read_sides(SUB)
    count_edge = edge_of_tile(count_west, count, count_east)

    def counts(tile):
        return tuple(rows_of((None, part, None), 0, 7) for part in (tile, jnp.minimum(tile, at(tile, -1))))

    def along(level, wet, wet_u, u, t, st):
        cell = (st * -ADVECT).where(wet > level, zero)
        flux = (cell.at(-1) - cell).where(wet_u > level, zero)
        back = u * flux
        face = face_values(t, t.at(-1), t.at(1), t.at(-2))
        return ((back + back.at(1)) * 7.0 - (back.at(-1) + back.at(2))) * (1.0 / 12.0), flux * face

    sides = [read_sides(row) for row in range(SUB)]
    west, east = Many(side[0] for side in sides), Many(side[1] for side in sides)
    u, t, st = (
        edge_rows(ref, west, east, levels, groups, name) for name, ref in (("u", u_ref), ("t", t_ref), ("st", st_ref))
    )
    edge_t, edge_u = along(numbers[groups], *counts(count_edge), u, t, st)
    own = counts(count)
    for q in range(groups):
        st = load_rows(st_ref, q, levels)
        from_x, to_u = along(numbers[q], *own, load_rows(u_ref, q, levels), load_rows(t_ref, q, levels), st)
        store_rows(dt_ref, q, levels, st + merge_edges(from_x, edge_t, q))
        store_rows(du_ref, q, levels, merge_edges(to_u, edge_u, q))
    flow = (u,) + tuple(
        edge_rows(ref, west, east, levels, groups, name) for name, ref in (("v", v_ref), ("su", su_ref), ("sv", sv_ref))
    )
    for n, rows in enumerate(flow):
        for row in range(SUB):
            edge_ref[(n * SUB + row) * SUB : (n * SUB + row + 1) * SUB, :] = rows[row]


def row_kernel(levels, v_ref, t_ref, st_ref, count_ref, y1_ref, y2_ref, dtx_ref, dt_hbm, dv_ref, dt_ref, sems):
    groups = group_count(levels)
    read_row, read_counts = slot_reader(y1_ref, y2_ref, groups)
    numbers = level_numbers(groups)
    zero = jnp.zeros((SUB, LANES), jnp.float32)
    count = count_ref[...].astype(jnp.float32)
    count_south, count_north = read_counts()
    counts = rows_of((count_south, count, count_north), -2, 9)
    counts_v = counts[1:].minimum(counts[:-1])
    out = []
    for q in range(groups):
        level = numbers[q]

        def rows(name, ref, first, last):
            south = [read_row(name, row, q) for row in range(first, 0)]
            north = [read_row(name, row, q) for row in range(SUB, last + 1)]
            return Many(south + load_rows(ref, q, levels).items + north)

        t, st, v = rows("t", t_ref, -2, 8), rows("st", st_ref, -2, 9), rows("v", v_ref, -1, 9)
        cell = (st * -ADVECT).where(counts > level, zero)
        flux = (cell[:-1] - cell[1:]).where(counts_v > level, zero)
        back = v * flux
        from_y = ((back[1:9] + back[2:10]) * 7.0 - (back[0:8] + back[3:11])) * (1.0 / 12.0)
        to_v = flux[1:9] * face_values(t[2:10], t[1:9], t[3:11], t[0:8])
        store_rows(dt_ref, q, levels, load_rows(dtx_ref, q, levels) + from_y)
        store_rows(dv_ref, q, levels, to_v)
        part = pl.ds(q * SUB * SUB, min(SUB, levels - q * SUB) * SUB)
        out.append(pltpu.make_async_copy(dt_ref.at[part, :], dt_hbm.at[part, :], sems.at[q]))
        out[-1].start()
    for copy in out:
        copy.wait()


def total(value):
    return jnp.sum(value, axis=(0, 1), keepdims=True)


def surface_solve(levels, ny, nx, read, count_ref, face_ref, x_ref, r_ref, p_ref, beside_work):
    groups = group_count(levels)
    lanes, rows = lane_ids(), row_ids()
    numbers = level_numbers(groups)
    zero = jnp.zeros((SUB, LANES), jnp.float32)
    band = max(1, min(ny, 32 // nx))
    while ny % band:
        band -= 1
    cells = [(dj, i) for dj in range(band) for i in range(nx)]

    def loop(body, init=0):
        if band == ny:
            return body(0, init)
        return lax.fori_loop(0, ny // band, lambda step, carry: body(step * band, carry), init)

    def get(ref, j):
        return Many(ref[j + dj, i] for dj, i in cells)

    def put(ref, j, values):
        for (dj, i), value in zip(cells, values.items):
            ref[j + dj, i] = value

    def beside(values, step):
        return Many(values[dj * nx + min(max(i + step, 0), nx - 1)] for dj, i in cells)

    def below(ref, j, values):
        outside = [ref[jnp.maximum(j - 1, 0), i] for i in range(nx)] if band < ny else values.items[:nx]
        return Many(outside + values.items[:-nx])

    def above(ref, j, values):
        outside = [ref[jnp.minimum(j + band, ny - 1), i] for i in range(nx)] if band < ny else values.items[-nx:]
        return Many(values.items[nx:] + outside)

    def west_of(values):
        return beside(values, -1).where(lanes == LANES - 1, values).rolled(1)

    def east_of(values):
        return beside(values, 1).where(lanes == 0, values).rolled(-1)

    def south_of(ref, j, values):
        return below(ref, j, values).where(rows == SUB - 1, values).apply(lambda a: roll_rows(a, 1))

    def north_of(ref, j, values):
        return above(ref, j, values).where(rows == 0, values).apply(lambda a: roll_rows(a, -1))

    def depth(wet):
        return wet.apply(lambda m: GRAVITY_DT * (m + m * (m - 1.0) * (0.5 / levels)))

    def gather(j, carry):
        put(count_ref, j, Many(read(j + dj, i, 0) for dj, i in cells))
        return carry

    loop(gather)

    def faces(j, carry):
        count = get(count_ref, j)
        wet_u, wet_v = count.minimum(west_of(count)), count.minimum(south_of(count_ref, j, count))
        first_column = [(lanes == 0) if i == 0 else (lanes < 0) for dj, i in cells]
        first_row = [(rows == 0) & (j + dj == 0) for dj, i in cells]
        wet_u = Many([zero] * len(cells)).where(Many(first_column), wet_u)
        wet_v = Many([zero] * len(cells)).where(Many(first_row), wet_v)
        put(face_ref.at[0], j, depth(wet_u))
        put(face_ref.at[1], j, depth(wet_v))
        edge = Many(read(j + dj, i, CHUNK_EDGE) for dj, i in cells)
        wet_west = wet_u.apply(lambda a: jnp.broadcast_to(a[:, 0:1], (SUB, LANES)))
        reach = jnp.where(lanes < levels, lanes.astype(jnp.float32), float(levels))
        inside = edge.where(wet_west > reach, zero)
        col_u = inside.apply(lambda a: jnp.broadcast_to(jnp.sum(a, axis=1, keepdims=True), (SUB, LANES)))
        put(face_ref.at[4], j, col_u * GRAVITY_DT)
        wet_south = wet_v.apply(lambda a: row_of(a, 0))
        col_v = Many([zero] * len(cells))
        for q in range(groups):
            south = Many(read(j + dj, i, CHUNK_ROW + q * SUB) for dj, i in cells)
            col_v = col_v + south.where(wet_south > numbers[q], zero)
        col_v = col_v.apply(lambda a: jnp.broadcast_to(jnp.sum(a, axis=0, keepdims=True), (SUB, LANES)))
        put(face_ref.at[5], j, col_v * GRAVITY_DT)
        return carry

    loop(faces)
    next(beside_work, None)

    def start(j, carry):
        load = Many(read(j + dj, i, CHUNK_LOAD) for dj, i in cells)
        col_u, col_v = get(face_ref.at[4], j), get(face_ref.at[5], j)
        depth_u, depth_v = get(face_ref.at[0], j), get(face_ref.at[1], j)
        last_column = Many((lanes == LANES - 1) if i + 1 < nx else (lanes < 0) for dj, i in cells)
        at_end = Many((lanes == LANES - 1) if i + 1 == nx else (lanes < 0) for dj, i in cells)
        last_row = Many((rows == SUB - 1) & (j + dj + 1 < ny) for dj, i in cells)
        at_top = Many((rows == SUB - 1) & (j + dj + 1 == ny) for dj, i in cells)
        none = Many([zero] * len(cells))
        load = load - col_u.where(lanes == 0, zero) - col_v.where(rows == 0, zero)
        load = load + beside(col_u, 1).where(last_column, none) + above(face_ref.at[5], j, col_v).where(last_row, none)
        put(face_ref.at[2], j, none.where(at_end, east_of(depth_u)))
        put(face_ref.at[3], j, none.where(at_top, north_of(face_ref.at[1], j, depth_v)))
        put(r_ref, j, load)
        return carry

    def gathered(partial, values):
        items = list(values.items)
        while len(items) > 1:
            items = [a + b for a, b in zip(items[::2], items[1::2])] + items[len(items) // 2 * 2 :]
        return partial + items[0]

    loop(start)

    def products(j, carry):
        r = get(r_ref, j)
        image = r + get(face_ref.at[0], j) * (r - west_of(r)) + get(face_ref.at[2], j) * (r - east_of(r))
        image = image + get(face_ref.at[1], j) * (r - south_of(r_ref, j, r))
        image = image + get(face_ref.at[3], j) * (r - north_of(r_ref, j, r))
        put(face_ref.at[4], j, image)
        return gathered(carry[0], r * r), gathered(carry[1], r * image)

    norm, product = [total(part) for part in loop(products, (zero, zero))]
    next(beside_work, None)
    step, ratio = norm / product, None

    for iteration in range(ITERS):
        last = iteration + 1 == ITERS

        def advance(j, carry):
            r = get(r_ref, j)
            p = r if ratio is None else r + get(p_ref, j) * ratio
            put(x_ref, j, p * step if ratio is None else get(x_ref, j) + p * step)
            if not last:
                image = get(face_ref.at[4], j)
                image = image if ratio is None else image + get(face_ref.at[5], j) * ratio
                put(p_ref, j, p)
                put(face_ref.at[5], j, image)
                put(r_ref, j, r - image * step)
            return carry

        loop(advance)
        if not last:
            new, product = [total(part) for part in loop(products, (zero, zero))]
            next(beside_work, None)
            ratio = new / norm
            step = new / (product - ratio * new / step)
            norm = new


def flow_kernel(
    levels, ny, nx, u_ref, v_ref, su_ref, sv_ref, ga_ref, gb_ref, y1_ref, y2_ref, edge_ref, dut_ref, dvt_ref,
    du_hbm, dv_hbm, eta_hbm, count_s, face_s, x_s, r_s, p_s, du_ref, dv_ref, sems,
):
    groups = group_count(levels)
    lanes = lane_ids()
    core = lax.axis_index("core")
    my_j = lax.axis_index("ty")
    my_i = lax.axis_index("y") * 2 + core
    numbers = level_numbers(groups)
    thick = [1.0 + number * (1.0 / levels) for number in numbers]
    read_row, _ = slot_reader(y1_ref, y2_ref, groups)
    zero = jnp.zeros((SUB, LANES), jnp.float32)

    def read(j, i, first):
        where = (j * (nx // 2) + i // 2, pl.ds(first, SUB), slice(None))
        return jnp.where(core == i % 2, ga_ref[where], gb_ref[where])

    def near(dj, di, get):
        j, i = jnp.clip(my_j + dj, 0, ny - 1), jnp.clip(my_i + di, 0, nx - 1)
        inside = (my_j + dj >= 0) & (my_j + dj < ny) & (my_i + di >= 0) & (my_i + di < nx)
        return jnp.where(inside, get(j, i), 0.0)

    corner_tiles = {
        name: near(dj, di, lambda j, i: read(j, i, CHUNK_EDGE))
        for name, dj, di in (("se", -1, 1), ("sw", -1, -1), ("nw", 1, -1), ("ne", 1, 1))
    }

    def insert_corners(edge, name, row):
        for which, value, target in CORNER_PLACES.get((name, row), ()):
            for q in range(groups):
                lane = SEG * q + target
                source = CORNER_LANE + CORNER_STEP * q + value
                edge = jnp.where(lanes == lane, roll_lanes(corner_tiles[which], lane - source), edge)
        return edge

    def rows(name, ref, q, first, last):
        south = [read_row(name, row, q) for row in range(first, 0)]
        north = [read_row(name, row, q) for row in range(SUB, last + 1)]
        return Many(south + load_rows(ref, q, levels).items + north)

    def edges(name, first, last):
        outer = [row for row in range(first, last + 1) if not 0 <= row < SUB]
        made = edges_of_groups([Many(read_row(name, row, q) for row in outer) for q in range(groups)])
        made = [insert_corners(edge, name, row) for edge, row in zip(made.items, outer)]
        n = FLOW_FIELDS.index(name)
        own = [edge_ref[(n * SUB + row) * SUB : (n * SUB + row + 1) * SUB, :] for row in range(SUB)]
        return Many(made[:-first] + own + made[-first:])

    total_rows = ny * SUB
    first_row = (my_j * SUB).astype(jnp.float32)
    turn_u = Many(0.5 + (first_row + (row + 0.5)) * (1.0 / total_rows) for row in range(-1, 8))
    turn_v = Many(-0.5 - (first_row + row) * (1.0 / total_rows) for row in range(0, 9))

    fields = (("u", u_ref, -2, 8), ("v", v_ref, -1, 9), ("su", su_ref, -1, 8), ("sv", sv_ref, -1, 8))
    data, made = {}, {}

    def prepare(part):
        if part == groups:
            data[part] = [data[name] for name in FLOW_FIELDS]
        else:
            data[part] = [rows(name, ref, part, first, last) for name, ref, first, last in fields]
        u, v = data[part][:2]
        v_pair, u_pair = v[:-1] + v[1:], u[2:10] + u[1:9]
        made[part] = (
            (v_pair + v_pair.at(-1)) * 0.25,
            (u_pair + u_pair.at(1)) * 0.25,
            (u[:-2] - u[2:]) * 0.5 + turn_u,
            (v[1:10].at(-1) - v[1:10].at(1)) * 0.5 + turn_v,
            u[2:10].at(1) - u[2:10].at(-1),
        )

    def beside_work():
        for name, ref, first, last in fields:
            data[name] = edges(name, first, last)
            yield
        prepare(groups)
        yield

    work = beside_work()
    surface_solve(levels, ny, nx, read, count_s, face_s, x_s, r_s, p_s, work)
    for _ in work:
        pass
    out = [pltpu.make_async_copy(x_s.at[my_j, my_i], eta_hbm, sems.at[0])]
    out[0].start()

    def around(ref):
        tiles = [[near(dj, di, lambda j, i: ref[j, i]) for di in (-1, 0, 1)] for dj in (-1, 0, 1)]
        return [row[1] for row in tiles], [edge_of_tile(*row) for row in tiles]

    count_tiles, x_tiles = around(count_s), around(x_s)

    def adjoint(part):
        kind = 1 if part == groups else 0
        level = numbers[part]
        u, v, su, sv = data[part]
        v_bar, u_bar, from_v_bar, from_u_bar, u_across = made[part]
        counts, x = rows_of(count_tiles[kind], -2, 8), rows_of(x_tiles[kind], -2, 8)
        wet_u = counts[1:].minimum(counts[1:].at(-1)) > level
        wet_v = counts[1:].minimum(counts[:-1]) > level
        u_cot = su + ((x[1:] - x[1:].at(-1)) * thick[part]).where(wet_u, zero)
        v_cot = sv + ((x[1:] - x[:-1]) * thick[part]).where(wet_v, zero)
        a, b = (u_cot * ADVECT).where(wet_u, zero), (v_cot * ADVECT).where(wet_v, zero)
        av, bu = a * v_bar, b[1:9] * u_bar
        au, bv = a[1:9] * u[2:10], b * v[:-1]
        to_v_bar, to_u_bar = a[:-1] * from_v_bar, b[1:] * from_u_bar
        near_u, near_v = to_u_bar[:-1] + to_u_bar[1:], to_v_bar[1:] + to_v_bar[:-1]
        twist_u = au.at(1) - au.at(-1) - a[1:9] * u_across + av[2:] - av[:-2]
        twist_v = bu.at(1) - bu.at(-1) - b[1:9] * (v[2:10] - v[0:8]) + bv[2:] - bv[:-2]
        du = u_cot[1:9] + twist_u * 0.5 + (near_u + near_u.at(-1)) * 0.25
        dv = v_cot[1:9] + twist_v * 0.5 + (near_v + near_v.at(1)) * 0.25
        return du, dv

    edge_u, edge_v = adjoint(groups)
    for q in range(groups):
        prepare(q)
        du, dv = adjoint(q)
        store_rows(du_ref, q, levels, merge_edges(du, edge_u, q) + load_rows(dut_ref, q, levels))
        store_rows(dv_ref, q, levels, merge_edges(dv, edge_v, q) + load_rows(dvt_ref, q, levels))
        part = pl.ds(q * SUB * SUB, min(SUB, levels - q * SUB) * SUB)
        for target, source in ((du_hbm, du_ref), (dv_hbm, dv_ref)):
            out.append(pltpu.make_async_copy(source.at[part, :], target.at[part, :], sems.at[len(out)]))
            out[-1].start()
    for copy in out:
        copy.wait()


def swaps(mesh_shape, along, parity):
    ny, nx = mesh_shape
    pairs = []
    for j in range(ny):
        for i in range(nx):
            k, size = (j, ny) if along == "y" else (i, nx)
            other = k + 1 if k % 2 == parity else k - 1
            if 0 <= other < size:
                pairs.append((j * nx + i, other * nx + i if along == "y" else j * nx + other))
    return pairs


def call(kernel, outs, args, scratch=(), flops=0, size=0, far_in=False, far_out=(), limit=48):
    near, far = pl.BlockSpec(memory_space=pltpu.VMEM), pl.BlockSpec(memory_space=pltpu.HBM)
    outs = [out if isinstance(out, jax.ShapeDtypeStruct) else jax.ShapeDtypeStruct(out, jnp.float32) for out in outs]
    return pl.pallas_call(
        kernel,
        out_shape=outs,
        in_specs=[far if far_in else near] * len(args),
        out_specs=[far if n in far_out else near for n in range(len(outs))],
        scratch_shapes=list(scratch),
        compiler_params=pltpu.CompilerParams(vmem_limit_bytes=limit * 1024 * 1024),
        cost_estimate=pl.CostEstimate(flops=flops, bytes_accessed=size, transcendentals=0),
    )(*args)


def on_device(shape, u, v, t, count, su, sv, st, elev):
    ny, nx = shape
    levels = u.shape[0]
    groups = group_count(levels)
    flat = (levels * SUB, LANES)
    u, v, t, su, sv, st = (field.reshape(flat) for field in (u, v, t, su, sv, st))
    peers = ny * nx // 2
    row_packet = ((N_SLOTS * groups + 1) * SUB, LANES)
    column_packet = ((SUB + 1) * SUB, LANES)
    chunk = (peers, CHUNK_ROW + groups * SUB, LANES)
    tile = (SUB, LANES)
    (chunks,) = call(
        functools.partial(chunk_kernel, levels, peers),
        [chunk],
        (u, v, su, sv, count, elev),
        scratch=[pltpu.VMEM(flat, jnp.float32)] * 4
        + [pltpu.VMEM(tile, count.dtype), pltpu.VMEM(tile, jnp.float32), pltpu.VMEM(chunk[1:], jnp.float32)]
        + [pltpu.SemaphoreType.DMA((7,))],
        flops=1 << 20,
        size=1 << 21,
        far_in=True,
        far_out=(0,),
        limit=60,
    )
    y1, y2, xp = call(
        functools.partial(packet_kernel, levels),
        [row_packet, row_packet, column_packet],
        (u, v, t, su, sv, st, count),
        flops=1 << 20,
        size=1 << 21,
    )
    axes = ("ty", "y", "core")
    ga = lax.all_to_all(chunks, ("ty", "y"), 0, 0)
    x1 = lax.ppermute(xp, axes, swaps(shape, "x", 0))
    x2 = lax.ppermute(xp, axes, swaps(shape, "x", 1))
    y1 = lax.ppermute(y1, axes, swaps(shape, "y", 0))
    y2 = lax.ppermute(y2, axes, swaps(shape, "y", 1))
    dtx, du_t, edge = call(
        functools.partial(column_kernel, levels),
        [flat, flat, (len(FLOW_FIELDS) * SUB * SUB, LANES)],
        (u, v, t, st, su, sv, count, x1, x2),
        flops=1 << 22,
        size=1 << 21,
    )
    ga, y1, y2, dtx = lax.optimization_barrier((ga, y1, y2, dtx))
    gb = lax.ppermute(ga, axes, swaps(shape, "x", 0))
    dt, dv_t = call(
        functools.partial(row_kernel, levels),
        [flat, flat],
        (v, t, st, count, y1, y2, dtx),
        scratch=(pltpu.VMEM(flat, jnp.float32), pltpu.SemaphoreType.DMA((groups,))),
        flops=1 << 22,
        size=1 << 21,
        far_out=(0,),
    )
    grid = pltpu.VMEM((ny, nx, SUB, LANES), jnp.float32)
    faces = pltpu.VMEM((6, ny, nx, SUB, LANES), jnp.float32)
    du, dv, eta = call(
        functools.partial(flow_kernel, levels, ny, nx),
        [flat, flat, (SUB, LANES)],
        (u, v, su, sv, ga, gb, y1, y2, edge, du_t, dv_t),
        far_out=(0, 1, 2),
        scratch=(grid, faces, grid, grid, grid, pltpu.VMEM(flat, jnp.float32), pltpu.VMEM(flat, jnp.float32))
        + (pltpu.SemaphoreType.DMA((2 * groups + 1,)),),
        flops=1 << 23,
        size=1 << 22,
    )
    whole = (levels, SUB, LANES)
    return du.reshape(whole), dv.reshape(whole), dt.reshape(whole), eta


def solution(mesh):
    ny, nx = mesh.shape["ty"], mesh.shape["tx"]
    split = Mesh(mesh.devices.reshape(ny, nx // 2, 2), ("ty", "y", "core"))
    deep, flat = P(None, "ty", ("y", "core")), P("ty", ("y", "core"))
    return jax.shard_map(
        functools.partial(on_device, (ny, nx)),
        mesh=split,
        in_specs=(deep, deep, deep, flat, deep, deep, deep, flat),
        out_specs=(deep, deep, deep, flat),
        check_vma=False,
    )
```

```python
import functools

import jax
import jax.numpy as jnp
from jax import lax
from jax.experimental import pallas as pl
from jax.experimental.pallas import tpu as pltpu
from jax.sharding import Mesh, PartitionSpec as P

ITERS = 4
ADVECT = 0.1
GRAVITY_DT = 0.1

SUB = 8
LANES = 128
SEG = 32
FIELDS = ("u", "v", "t", "st", "su", "sv")
BAND_BLOCKS = 32
FLOW_FIELDS = ("u", "v", "su", "sv")
FLOW_ROWS = {"u": (-2, 8), "v": (-1, 9), "su": (-1, 8), "sv": (-1, 8)}
OUTER_ROWS = tuple((n, r) for n in FLOW_FIELDS for r in range(FLOW_ROWS[n][0], FLOW_ROWS[n][1] + 1) if not 0 <= r < 8)
MADE_SIZES = (10, 8, 9, 9, 8, 8)
MADE_ROWS = sum(MADE_SIZES)
SOUTH_SLOTS = {("u", -2): 0, ("u", -1): 1, ("v", -1): 2, ("t", -2): 3, ("t", -1): 4, ("st", -2): 5, ("st", -1): 6}
SOUTH_SLOTS.update({("su", -1): 7, ("sv", -1): 8})
NORTH_SLOTS = {("u", 8): 0, ("v", 8): 1, ("v", 9): 2, ("t", 8): 3, ("st", 8): 5, ("st", 9): 6, ("su", 8): 7, ("sv", 8): 8}
N_SLOTS = 9
CHUNK_LOAD = SUB
CHUNK_EDGE = 2 * SUB
CHUNK_ROW = 3 * SUB
EDGE_LEVELS = 20
CORNERS = (("u", 6, 0), ("u", 7, 0), ("u", 7, 1), ("su", 7, 0), ("v", 7, 127), ("u", 7, 127))
CORNERS += (("v", 0, 127), ("v", 1, 127), ("v", 0, 126), ("sv", 0, 127), ("v", 0, 0), ("u", 0, 0))
CORNER_PLACES = {
    ("u", -2): (("se", 0, 24),),
    ("u", -1): (("se", 1, 24), ("se", 2, 25), ("sw", 5, 7)),
    ("su", -1): (("se", 3, 24),),
    ("v", -1): (("sw", 4, 7),),
    ("v", 8): (("nw", 6, 7), ("nw", 8, 6), ("ne", 10, 24)),
    ("u", 8): (("ne", 11, 24),),
    ("v", 9): (("nw", 7, 7),),
    ("sv", 8): (("nw", 9, 7),),
}


def lane_ids():
    return lax.broadcasted_iota(jnp.int32, (SUB, LANES), 1)


def row_ids():
    return lax.broadcasted_iota(jnp.int32, (SUB, LANES), 0)


def roll_lanes(value, amount):
    amount %= LANES
    return value if amount == 0 else pltpu.roll(value, amount, 1)


def roll_rows(value, amount):
    amount %= SUB
    return value if amount == 0 else pltpu.roll(value, amount, 0)


def at(value, shift):
    return roll_lanes(value, -shift)


def row_of(tile, row):
    return jnp.broadcast_to(tile[row : row + 1, :], (SUB, LANES))


def group_count(levels):
    return -(-levels // SUB)


def load_group(ref, row, q, levels):
    first = min(q * SUB, levels - SUB)
    value = ref[pl.ds(first * SUB + row, SUB, stride=SUB), :]
    return roll_rows(value, first - q * SUB)


def store_group(ref, row, q, levels, value):
    count = min(SUB, levels - q * SUB)
    ref[pl.ds(q * SUB * SUB + row, count, stride=SUB), :] = value[:count]


def level_numbers(groups):
    rows = row_ids()
    numbers = [(rows + q * SUB).astype(jnp.float32) for q in range(groups)]
    return numbers + [(rows + (lane_ids() >> 5) * SUB).astype(jnp.float32)]


def edge_of_tile(west, centre, east):
    lanes = lane_ids()
    out = jnp.where(lanes < 8, roll_lanes(west, 8), roll_lanes(centre, 8))
    out = jnp.where(lanes >= 16, roll_lanes(centre, 24), out)
    out = jnp.where(lanes >= 24, roll_lanes(east, 24), out)
    out = jnp.where(lanes < SEG, out, roll_lanes(out, SEG))
    return jnp.where(lanes < 2 * SEG, out, roll_lanes(out, 2 * SEG))


def chunk_kernel(
    levels, peers, u_hbm, v_hbm, su_hbm, sv_hbm, count_hbm, elev_hbm, chunk_ref,
    u_ref, v_ref, su_ref, sv_ref, count_ref, elev_ref, sems,
):
    pairs = (
        (count_hbm, count_ref), (su_hbm, su_ref), (sv_hbm, sv_ref), (elev_hbm, elev_ref), (u_hbm, u_ref), (v_hbm, v_ref),
    )
    copies = [pltpu.make_async_copy(source, target, sems.at[n]) for n, (source, target) in enumerate(pairs)]
    for copy in copies:
        copy.start()
    groups = group_count(levels)
    lanes, rows = lane_ids(), row_ids()
    refs = {"u": u_ref, "v": v_ref, "su": su_ref, "sv": sv_ref}
    for copy in copies[:4]:
        copy.wait()
    count = count_ref[...].astype(jnp.float32)
    zero = jnp.zeros((SUB, LANES), jnp.float32)

    wet_u = jnp.where(lanes == 0, 0.0, jnp.minimum(count, roll_lanes(count, 1)))
    wet_v = jnp.where(rows == 0, 0.0, jnp.minimum(count, roll_rows(count, 1)))
    col_u, col_v, edge = [zero] * 4, [zero] * 4, zero
    for k in range(levels):
        su_level = su_ref[k * SUB : (k + 1) * SUB, :]
        col_u[k % 4] = col_u[k % 4] + jnp.where(wet_u > float(k), su_level, 0.0)
        col_v[k % 4] = col_v[k % 4] + jnp.where(wet_v > float(k), sv_ref[k * SUB : (k + 1) * SUB, :], 0.0)
        lane = SEG * (k // EDGE_LEVELS) + k % EDGE_LEVELS
        edge = jnp.where(lanes == lane, roll_lanes(su_level, lane), edge)
    col_u, col_v = ((col[0] + col[1]) + (col[2] + col[3]) for col in (col_u, col_v))
    load = elev_ref[...] + GRAVITY_DT * (at(col_u, 1) - col_u + roll_rows(col_v, -1) - col_v)

    for copy in copies[4:]:
        copy.wait()
    for place, (name, row, column) in enumerate(CORNERS):
        for q in range(groups):
            lane = SEG * q + EDGE_LEVELS + place
            edge = jnp.where(lanes == lane, roll_lanes(load_group(refs[name], row, q, levels), lane - column), edge)

    south_row = [load_group(sv_ref, 0, q, levels) for q in range(groups)]

    def put(peer, carry):
        chunk_ref[peer, 0:SUB, :] = count
        chunk_ref[peer, CHUNK_LOAD : CHUNK_LOAD + SUB, :] = load
        chunk_ref[peer, CHUNK_EDGE : CHUNK_EDGE + SUB, :] = edge
        for q in range(groups):
            chunk_ref[peer, CHUNK_ROW + q * SUB : CHUNK_ROW + (q + 1) * SUB, :] = south_row[q]
        return carry

    lax.fori_loop(0, peers, put, 0, unroll=4)


def packet_kernel(levels, u_ref, v_ref, t_ref, su_ref, sv_ref, st_ref, count_ref, y1_ref, y2_ref, x_ref):
    groups = group_count(levels)
    lanes = lane_ids()
    zero = jnp.zeros((SUB, LANES), jnp.float32)
    count = count_ref[...].astype(jnp.float32)
    even = lax.axis_index("ty") % 2 == 0
    refs = {"u": u_ref, "v": v_ref, "t": t_ref, "st": st_ref, "su": su_ref, "sv": sv_ref}
    loaded = {}
    for name in FIELDS:
        for row in range(SUB):
            for q in range(groups):
                loaded[name, row, q] = load_group(refs[name], row, q, levels)

    for slot in range(N_SLOTS):
        upper = [(name, row + SUB) for (name, row), place in SOUTH_SLOTS.items() if place == slot]
        lower = [(name, row - SUB) for (name, row), place in NORTH_SLOTS.items() if place == slot]
        for q in range(groups):
            to_north = loaded[(*upper[0], q)]
            to_south = loaded[(*lower[0], q)] if lower else zero
            place = pl.ds((slot * groups + q) * SUB, SUB)
            y1_ref[place, :] = jnp.where(even, to_north, to_south)
            y2_ref[place, :] = jnp.where(even, to_south, to_north)
    y1_ref[N_SLOTS * groups * SUB :, :] = count
    y2_ref[N_SLOTS * groups * SUB :, :] = count

    for row in range(SUB):
        packet = zero
        for field, name in enumerate(FIELDS):
            for q in range(groups):
                lane = SEG * q + 4 * field
                packet = jnp.where((lanes >= lane) & (lanes < lane + 4), roll_lanes(loaded[name, row, q], lane + 2), packet)
        x_ref[row * SUB : (row + 1) * SUB, :] = packet
    x_ref[SUB * SUB :, :] = count


class Many:
    def __init__(self, items):
        self.items = list(items)

    def __getitem__(self, where):
        return Many(self.items[where]) if isinstance(where, slice) else self.items[where]

    def __len__(self):
        return len(self.items)

    def apply(self, operation, *others):
        others = [other.items if isinstance(other, Many) else [other] * len(self) for other in others]
        assert all(len(other) == len(self) for other in others)
        return Many(operation(*parts) for parts in zip(self.items, *others))

    def __add__(self, other):
        return self.apply(lambda a, b: a + b, other)

    def __sub__(self, other):
        return self.apply(lambda a, b: a - b, other)

    def __mul__(self, other):
        return self.apply(lambda a, b: a * b, other)

    def __gt__(self, other):
        return self.apply(lambda a, b: a > b, other)

    def at(self, shift):
        return self.apply(lambda a: at(a, shift))

    def rolled(self, amount):
        return self.apply(lambda a: roll_lanes(a, amount))

    def minimum(self, other):
        return self.apply(jnp.minimum, other)

    def where(self, mask, other):
        return self.apply(lambda a, m, b: jnp.where(m, a, b), mask, other)


def edges_of_groups(parts):
    lanes = lane_ids()
    out = parts[0].rolled(8)
    for q in range(1, len(parts)):
        out = parts[q].rolled(SEG * q + 8).where(lanes >= SEG * q, out)
    return out.rolled(16).where((lanes & (SEG - 1)) >= 16, out)


def insert_sides(edge, west, east, field):
    place = lane_ids() & (SEG - 1)
    edge = west.rolled(6 - 4 * field).where((place == 6) | (place == 7), edge)
    return east.rolled(22 - 4 * field).where((place == 24) | (place == 25), edge)


def outer_columns(edge):
    return edge.rolled(-16).where((lane_ids() & (SEG - 1)) < 8, edge)


def merge_edges(values, outer, q):
    lanes = lane_ids()
    return outer.rolled(-(SEG * q + 8)).where((lanes < 2) | (lanes >= LANES - 2), values)


def load_rows(ref, q, levels):
    return Many(load_group(ref, row, q, levels) for row in range(SUB))


def store_rows(ref, q, levels, values):
    for row in range(SUB):
        store_group(ref, row, q, levels, values[row])


def rows_of(tiles, first, last):
    return Many(row_of(tiles[row // SUB + 1], row % SUB) for row in range(first, last + 1))


def slot_reader(y1_ref, y2_ref, groups):
    even = lax.axis_index("ty") % 2 == 0

    def read(name, row, q):
        slot = (SOUTH_SLOTS if row < 0 else NORTH_SLOTS)[name, row]
        place = pl.ds((slot * groups + q) * SUB, SUB)
        one, two = y1_ref[place, :], y2_ref[place, :]
        return jnp.where(even, two, one) if row < 0 else jnp.where(even, one, two)

    def counts():
        place = pl.ds(N_SLOTS * groups * SUB, SUB)
        one, two = y1_ref[place, :], y2_ref[place, :]
        return jnp.where(even, two, one), jnp.where(even, one, two)

    return read, counts


def side_reader(x1_ref, x2_ref):
    even = lax.axis_index("core") % 2 == 0

    def read(row):
        place = pl.ds(row * SUB, SUB)
        one, two = x1_ref[place, :], x2_ref[place, :]
        return jnp.where(even, two, one), jnp.where(even, one, two)

    return read


def face_values(t0, t_before, t_after, t_before2):
    return ((t0 + t_before) * 7.0 - (t_after + t_before2)) * (1.0 / 12.0)


def edge_rows(ref, west, east, levels, groups, name):
    own = edges_of_groups([load_rows(ref, q, levels) for q in range(groups)])
    return insert_sides(own, west, east, FIELDS.index(name))


def column_kernel(
    levels, u_ref, v_ref, t_ref, st_ref, su_ref, sv_ref, count_ref, x1_ref, x2_ref, dt_ref, du_ref, edge_ref
):
    groups = group_count(levels)
    read_sides = side_reader(x1_ref, x2_ref)
    numbers = level_numbers(groups)
    zero = jnp.zeros((SUB, LANES), jnp.float32)
    count = count_ref[...].astype(jnp.float32)
    count_west, count_east = read_sides(SUB)
    count_edge = edge_of_tile(count_west, count, count_east)

    def counts(tile):
        return tuple(rows_of((None, part, None), 0, 7) for part in (tile, jnp.minimum(tile, at(tile, -1))))

    def along(level, wet, wet_u, u, t, st):
        cell = (st * -ADVECT).where(wet > level, zero)
        flux = (cell.at(-1) - cell).where(wet_u > level, zero)
        back = u * flux
        face = face_values(t, t.at(-1), t.at(1), t.at(-2))
        return ((back + back.at(1)) * 7.0 - (back.at(-1) + back.at(2))) * (1.0 / 12.0), flux * face

    sides = [read_sides(row) for row in range(SUB)]
    west, east = Many(side[0] for side in sides), Many(side[1] for side in sides)
    u, t, st = (
        edge_rows(ref, west, east, levels, groups, name) for name, ref in (("u", u_ref), ("t", t_ref), ("st", st_ref))
    )
    edge_t, edge_u = (outer_columns(part) for part in along(numbers[groups], *counts(count_edge), u, t, st))
    own = counts(count)
    for q in range(groups):
        st = load_rows(st_ref, q, levels)
        from_x, to_u = along(numbers[q], *own, load_rows(u_ref, q, levels), load_rows(t_ref, q, levels), st)
        store_rows(dt_ref, q, levels, st + merge_edges(from_x, edge_t, q))
        store_rows(du_ref, q, levels, merge_edges(to_u, edge_u, q))
    flow = (u,) + tuple(
        edge_rows(ref, west, east, levels, groups, name) for name, ref in (("v", v_ref), ("su", su_ref), ("sv", sv_ref))
    )
    for n, rows in enumerate(flow):
        for row in range(SUB):
            edge_ref[(n * SUB + row) * SUB : (n * SUB + row + 1) * SUB, :] = rows[row]


def turns(ny):
    first_row = (lax.axis_index("ty") * SUB).astype(jnp.float32)
    scale = 0.5 / (ny * SUB)
    turn_u = Many(0.25 + (first_row + (row + 0.5)) * scale for row in range(-1, 8))
    return turn_u, Many(-0.25 - (first_row + row) * scale for row in range(0, 9))


def prepared(u, v, turn_u, turn_v):
    v_pair, u_pair = v[:-1] + v[1:], u[2:10] + u[1:9]
    return (
        (v_pair + v_pair.at(-1)) * 0.25,
        (u_pair + u_pair.at(1)) * 0.25,
        (u[:-2] - u[2:]) * 0.25 + turn_u,
        (v[1:10].at(-1) - v[1:10].at(1)) * 0.25 + turn_v,
        u[2:10].at(1) - u[2:10].at(-1),
        v[2:10] - v[0:8],
    )


def row_kernel(
    levels, ny, u_ref, v_ref, t_ref, st_ref, count_ref, y1_ref, y2_ref, dtx_ref, dt_hbm, dv_ref, made_ref, edge_ref, dt_ref, sems
):
    groups = group_count(levels)
    read_row, read_counts = slot_reader(y1_ref, y2_ref, groups)
    numbers = level_numbers(groups)
    zero = jnp.zeros((SUB, LANES), jnp.float32)
    count = count_ref[...].astype(jnp.float32)
    count_south, count_north = read_counts()
    counts = rows_of((count_south, count, count_north), -2, 9)
    counts_v = counts[1:].minimum(counts[:-1])
    out = []
    for n, (name, row) in enumerate(OUTER_ROWS):
        (edge,) = edges_of_groups([Many([read_row(name, row, q)]) for q in range(groups)]).items
        edge_ref[n * SUB : (n + 1) * SUB, :] = edge
    for q in range(groups):
        level = numbers[q]

        def rows(name, ref, first, last):
            south = [read_row(name, row, q) for row in range(first, 0)]
            north = [read_row(name, row, q) for row in range(SUB, last + 1)]
            return Many(south + load_rows(ref, q, levels).items + north)

        t, st, v = rows("t", t_ref, -2, 8), rows("st", st_ref, -2, 9), rows("v", v_ref, -1, 9)
        made = prepared(rows("u", u_ref, -2, 8), v, *turns(ny))
        for n, value in enumerate(value for values in made for value in values.items):
            place = pl.ds((q * MADE_ROWS + n) * SUB, SUB)
            made_ref[place, :] = value
        cell = (st * -ADVECT).where(counts > level, zero)
        flux = (cell[:-1] - cell[1:]).where(counts_v > level, zero)
        back = v * flux
        from_y = ((back[1:9] + back[2:10]) * 7.0 - (back[0:8] + back[3:11])) * (1.0 / 12.0)
        to_v = flux[1:9] * face_values(t[2:10], t[1:9], t[3:11], t[0:8])
        store_rows(dt_ref, q, levels, load_rows(dtx_ref, q, levels) + from_y)
        store_rows(dv_ref, q, levels, to_v)
        part = pl.ds(q * SUB * SUB, min(SUB, levels - q * SUB) * SUB)
        out.append(pltpu.make_async_copy(dt_ref.at[part, :], dt_hbm.at[part, :], sems.at[q]))
        out[-1].start()
    for copy in out:
        copy.wait()


def total(value):
    return jnp.sum(value, axis=(0, 1), keepdims=True)


def surface_solve(levels, ny, nx, read, count_ref, face_ref, r_refs, beside_setup, beside_sum):
    groups = group_count(levels)
    lanes, rows = lane_ids(), row_ids()
    numbers = level_numbers(groups)
    zero = jnp.zeros((SUB, LANES), jnp.float32)
    band = max(1, min(ny, BAND_BLOCKS // nx))
    while ny % band:
        band -= 1
    cells = [(dj, i) for dj in range(band) for i in range(nx)]

    def loop(body, init=0):
        if ny * nx <= 32:
            for j in range(0, ny, band):
                init = body(j, init)
            return init
        return lax.fori_loop(0, ny // band, lambda step, carry: body(step * band, carry), init)

    def get(ref, j):
        return Many(ref[j + dj, i] for dj, i in cells)

    def put(ref, j, values):
        for (dj, i), value in zip(cells, values.items):
            ref[j + dj, i] = value

    def beside(values, step):
        return Many(values[dj * nx + min(max(i + step, 0), nx - 1)] for dj, i in cells)

    def below(ref, j, values):
        outside = [ref[max(j - 1, 0) if isinstance(j, int) else jnp.maximum(j - 1, 0), i] for i in range(nx)]
        return Many(outside + values.items[:-nx])

    def above(ref, j, values):
        top = min(j + band, ny - 1) if isinstance(j, int) else jnp.minimum(j + band, ny - 1)
        outside = [ref[top, i] for i in range(nx)]
        return Many(values.items[nx:] + outside)

    def west_of(values):
        return beside(values, -1).where(lanes == LANES - 1, values).rolled(1)

    def east_of(values):
        return beside(values, 1).where(lanes == 0, values).rolled(-1)

    def south_of(ref, j, values):
        return below(ref, j, values).where(rows == SUB - 1, values).apply(lambda a: roll_rows(a, 1))

    def north_of(ref, j, values):
        return above(ref, j, values).where(rows == 0, values).apply(lambda a: roll_rows(a, -1))

    def depth(wet):
        return wet.apply(lambda m: m * (m * (GRAVITY_DT * 0.5 / levels) + GRAVITY_DT * (1.0 - 0.5 / levels)))

    def gather(j, carry):
        put(count_ref, j, Many(read(j + dj, i, 0) for dj, i in cells))
        return carry

    loop(gather)

    def faces(j, carry):
        count = get(count_ref, j)
        wet_u, wet_v = count.minimum(west_of(count)), count.minimum(south_of(count_ref, j, count))
        first_column = [(lanes == 0) if i == 0 else (lanes < 0) for dj, i in cells]
        first_row = [(rows == 0) & (j + dj == 0) for dj, i in cells]
        wet_u = Many([zero] * len(cells)).where(Many(first_column), wet_u)
        wet_v = Many([zero] * len(cells)).where(Many(first_row), wet_v)
        put(face_ref.at[0], j, depth(wet_u))
        put(face_ref.at[1], j, depth(wet_v))
        edge = Many(read(j + dj, i, CHUNK_EDGE) for dj, i in cells)
        wet_west = wet_u.apply(lambda a: jnp.broadcast_to(a[:, 0:1], (SUB, LANES)))
        place = lanes & (SEG - 1)
        number = (lanes >> 5) * EDGE_LEVELS + place
        reach = jnp.where((place < EDGE_LEVELS) & (number < levels), number.astype(jnp.float32), float(levels))
        inside = edge.where(wet_west > reach, zero)
        col_u = inside.apply(lambda a: jnp.broadcast_to(jnp.sum(a, axis=1, keepdims=True), (SUB, LANES)))
        put(face_ref.at[4], j, col_u * GRAVITY_DT)
        wet_south = wet_v.apply(lambda a: row_of(a, 0))
        col_v = Many([zero] * len(cells))
        for q in range(groups):
            south = Many(read(j + dj, i, CHUNK_ROW + q * SUB) for dj, i in cells)
            col_v = col_v + south.where(wet_south > numbers[q], zero)
        col_v = col_v.apply(lambda a: jnp.broadcast_to(jnp.sum(a, axis=0, keepdims=True), (SUB, LANES)))
        put(face_ref.at[5], j, col_v * GRAVITY_DT)
        return carry

    loop(faces)
    beside_setup()

    def start(j, carry):
        load = Many(read(j + dj, i, CHUNK_LOAD) for dj, i in cells)
        col_u, col_v = get(face_ref.at[4], j), get(face_ref.at[5], j)
        depth_u, depth_v = get(face_ref.at[0], j), get(face_ref.at[1], j)
        last_column = Many((lanes == LANES - 1) if i + 1 < nx else (lanes < 0) for dj, i in cells)
        at_end = Many((lanes == LANES - 1) if i + 1 == nx else (lanes < 0) for dj, i in cells)
        last_row = Many((rows == SUB - 1) & (j + dj + 1 < ny) for dj, i in cells)
        at_top = Many((rows == SUB - 1) & (j + dj + 1 == ny) for dj, i in cells)
        none = Many([zero] * len(cells))
        load = load - col_u.where(lanes == 0, zero) - col_v.where(rows == 0, zero)
        load = load + beside(col_u, 1).where(last_column, none) + above(face_ref.at[5], j, col_v).where(last_row, none)
        depth_east = none.where(at_end, east_of(depth_u))
        depth_north = none.where(at_top, north_of(face_ref.at[1], j, depth_v))
        put(face_ref.at[2], j, depth_east)
        put(face_ref.at[3], j, depth_north)
        put(face_ref.at[6], j, (depth_u + depth_east) + (depth_v + depth_north) + 1.0)
        put(r_refs.at[0], j, load)
        return carry

    def gathered(partial, values):
        items = list(values.items)
        while len(items) > 1:
            items = [a + b for a, b in zip(items[::2], items[1::2])] + items[len(items) // 2 * 2 :]
        return partial + items[0]

    loop(start)

    def products(k):
        r_ref = r_refs.at[k]

        def body(j, carry):
            r = get(r_ref, j)
            image = r * get(face_ref.at[6], j) - get(face_ref.at[0], j) * west_of(r) - get(face_ref.at[2], j) * east_of(r)
            image = image - get(face_ref.at[1], j) * south_of(r_ref, j, r)
            image = image - get(face_ref.at[3], j) * north_of(r_ref, j, r)
            put(face_ref.at[4], j, image)
            return gathered(carry[0], r * r), gathered(carry[1], r * image)

        return [total(part) for part in loop(body, (zero, zero))]

    norm, product = products(0)
    beside_sum(0)
    step = norm / product
    steps, ratios = [step], []

    for k in range(ITERS - 1):

        def advance(j, carry):
            image = get(face_ref.at[4], j)
            if k > 0:
                image = image + get(face_ref.at[5], j) * ratio
            if k + 2 < ITERS:
                put(face_ref.at[5], j, image)
            put(r_refs.at[k + 1], j, get(r_refs.at[k], j) - image * step)
            return carry

        loop(advance)
        new, product = products(k + 1)
        beside_sum(k + 1)
        ratio = new / norm
        step = new / (product - ratio * new / step)
        norm = new
        steps.append(step)
        ratios.append(ratio)

    weights = [steps[-1]]
    for k in reversed(range(ITERS - 1)):
        weights.append(steps[k] + ratios[k] * weights[-1])
    weights.reverse()
    return weights


def flow_kernel(
    levels, ny, nx, u_ref, v_ref, su_ref, sv_ref, ga_ref, gb_ref, y1_ref, y2_ref, edge_ref, outer_ref, made_ref, dut_ref, dvt_ref,
    du_hbm, dv_hbm, eta_hbm, count_s, face_s, r_s, eta_ref, du_ref, dv_ref, sems,
):
    groups = group_count(levels)
    lanes, rows_id = lane_ids(), row_ids()
    core = lax.axis_index("core")
    my_j = lax.axis_index("ty")
    my_i = lax.axis_index("y") * 2 + core
    numbers = level_numbers(groups)
    thick = [1.0 + number * (1.0 / levels) for number in numbers]
    read_row, _ = slot_reader(y1_ref, y2_ref, groups)
    zero = jnp.zeros((SUB, LANES), jnp.float32)

    def read(j, i, first):
        where = (j * (nx // 2) + i // 2, pl.ds(first, SUB), slice(None))
        return jnp.where(core == i % 2, ga_ref[where], gb_ref[where])

    def block(dj, di, get):
        return get(jnp.clip(my_j + dj, 0, ny - 1), jnp.clip(my_i + di, 0, nx - 1))

    def near(dj, di, get):
        j, i = jnp.clip(my_j + dj, 0, ny - 1), jnp.clip(my_i + di, 0, nx - 1)
        inside = (my_j + dj >= 0) & (my_j + dj < ny) & (my_i + di >= 0) & (my_i + di < nx)
        return jnp.where(inside, get(j, i), 0.0)

    corner_tiles = {
        name: near(dj, di, lambda j, i: read(j, i, CHUNK_EDGE))
        for name, dj, di in (("se", -1, 1), ("sw", -1, -1), ("nw", 1, -1), ("ne", 1, 1))
    }

    def insert_corners(edge, name, row):
        for which, value, target in CORNER_PLACES.get((name, row), ()):
            there = (lanes & (SEG - 1)) == target
            edge = jnp.where(there, roll_lanes(corner_tiles[which], target - EDGE_LEVELS - value), edge)
        return edge

    def rows(name, ref, q, first, last):
        south = [read_row(name, row, q) for row in range(first, 0)]
        north = [read_row(name, row, q) for row in range(SUB, last + 1)]
        return Many(south + load_rows(ref, q, levels).items + north)

    def edges(name):
        first, last = FLOW_ROWS[name]
        n = FLOW_FIELDS.index(name)

        def register(row):
            if 0 <= row < SUB:
                return edge_ref[(n * SUB + row) * SUB : (n * SUB + row + 1) * SUB, :]
            place = OUTER_ROWS.index((name, row)) * SUB
            return insert_corners(outer_ref[place : place + SUB, :], name, row)

        return Many(register(row) for row in range(first, last + 1))

    refs = {"u": u_ref, "v": v_ref, "su": su_ref, "sv": sv_ref}
    data, made = {}, {}

    def prepare(part):
        if part == groups:
            data[part] = [edges(name) for name in FLOW_FIELDS]
            made[part] = prepared(*data[part][:2], *turns(ny))
            return
        data[part] = [rows(name, refs[name], part, *FLOW_ROWS[name]) for name in FLOW_FIELDS]
        made[part], n = [], part * MADE_ROWS
        for size in MADE_SIZES:
            made[part].append(Many(made_ref[k * SUB : (k + 1) * SUB, :] for k in range(n, n + size)))
            n += size

    def pairs(get, operation):
        tiles = [[get(dj, di) for di in (-1, 0, 1)] for dj in (-1, 0, 1)]
        out = []
        for south, own, north in ([row[1] for row in tiles], [edge_of_tile(*row) for row in tiles]):
            outer = jnp.where(rows_id == SUB - 1, south, north)
            below = roll_rows(jnp.where(rows_id == SUB - 1, south, own), 1)
            below_outer = roll_rows(jnp.where(rows_id == SUB - 2, south, own), 1)
            out.append(
                (operation(own, at(own, -1)), operation(outer, at(outer, -1)), operation(own, below), operation(outer, below_outer))
            )
        return out

    def outer_and_own(own, outer):
        return Many([row_of(outer, SUB - 1)] + [row_of(own, row) for row in range(SUB)] + [row_of(outer, 0)])

    wet_counts, differences = [], []

    def beside_setup():
        wet_counts.extend(pairs(lambda dj, di: near(dj, di, lambda j, i: count_s[j, i]), jnp.minimum))
        prepare(groups)

    def beside_sum(k):
        differences.append(pairs(lambda dj, di: block(dj, di, lambda j, i: r_s[k, j, i]), lambda a, b: a - b))

    weights = surface_solve(levels, ny, nx, read, count_s, face_s, r_s, beside_setup, beside_sum)

    def weighted(parts):
        total_of = parts[0] * weights[0]
        for part, weight in zip(parts[1:], weights[1:]):
            total_of = total_of + part * weight
        return total_of

    slopes = [[weighted([d[kind][n] for d in differences]) for n in range(4)] for kind in range(2)]
    eta_ref[...] = weighted([r_s[k, my_j, my_i] for k in range(ITERS)])
    out = [pltpu.make_async_copy(eta_ref, eta_hbm, sems.at[0])]
    out[0].start()

    def adjoint(part):
        kind = 1 if part == groups else 0
        level = numbers[part]
        u, v, su, sv = data[part]
        v_bar, u_bar, from_v_bar, from_u_bar, u_across, v_across = made[part]
        wet_u = outer_and_own(*wet_counts[kind][:2]) > level
        wet_v = outer_and_own(*wet_counts[kind][2:]) > level
        u_cot = su + (outer_and_own(*slopes[kind][:2]) * thick[part]).where(wet_u, zero)
        v_cot = sv + (outer_and_own(*slopes[kind][2:]) * thick[part]).where(wet_v, zero)
        a, b = (u_cot * (0.5 * ADVECT)).where(wet_u, zero), (v_cot * (0.5 * ADVECT)).where(wet_v, zero)
        av, bu = a * v_bar, b[1:9] * u_bar
        au, bv = a[1:9] * u[2:10], b * v[:-1]
        to_v_bar, to_u_bar = a[:-1] * from_v_bar, b[1:] * from_u_bar
        near_u, near_v = to_u_bar[:-1] + to_u_bar[1:], to_v_bar[1:] + to_v_bar[:-1]
        du = u_cot[1:9] - a[1:9] * u_across + av[2:] - av[:-2] + near_u
        du = du + au.at(1) + (near_u - au).at(-1)
        dv = v_cot[1:9] - b[1:9] * v_across + bv[2:] - bv[:-2] + near_v
        dv = dv + (near_v + bu).at(1) - bu.at(-1)
        return du, dv

    edge_u, edge_v = (outer_columns(part) for part in adjoint(groups))
    for q in range(groups):
        prepare(q)
        du, dv = adjoint(q)
        store_rows(du_ref, q, levels, merge_edges(du, edge_u, q) + load_rows(dut_ref, q, levels))
        store_rows(dv_ref, q, levels, merge_edges(dv, edge_v, q) + load_rows(dvt_ref, q, levels))
        part = pl.ds(q * SUB * SUB, min(SUB, levels - q * SUB) * SUB)
        for target, source in ((du_hbm, du_ref), (dv_hbm, dv_ref)):
            out.append(pltpu.make_async_copy(source.at[part, :], target.at[part, :], sems.at[len(out)]))
            out[-1].start()
    for copy in out:
        copy.wait()


def swaps(mesh_shape, along, parity):
    ny, nx = mesh_shape
    pairs = []
    for j in range(ny):
        for i in range(nx):
            k, size = (j, ny) if along == "y" else (i, nx)
            other = k + 1 if k % 2 == parity else k - 1
            if 0 <= other < size:
                pairs.append((j * nx + i, other * nx + i if along == "y" else j * nx + other))
    return pairs


def call(kernel, outs, args, scratch=(), flops=0, size=0, far_in=False, far_out=(), limit=48):
    near, far = pl.BlockSpec(memory_space=pltpu.VMEM), pl.BlockSpec(memory_space=pltpu.HBM)
    outs = [out if isinstance(out, jax.ShapeDtypeStruct) else jax.ShapeDtypeStruct(out, jnp.float32) for out in outs]
    return pl.pallas_call(
        kernel,
        out_shape=outs,
        in_specs=[far if far_in else near] * len(args),
        out_specs=[far if n in far_out else near for n in range(len(outs))],
        scratch_shapes=list(scratch),
        compiler_params=pltpu.CompilerParams(vmem_limit_bytes=limit * 1024 * 1024),
        cost_estimate=pl.CostEstimate(flops=flops, bytes_accessed=size, transcendentals=0),
    )(*args)


def on_device(shape, u, v, t, count, su, sv, st, elev):
    ny, nx = shape
    levels = u.shape[0]
    groups = group_count(levels)
    flat = (levels * SUB, LANES)
    u, v, t, su, sv, st = (field.reshape(flat) for field in (u, v, t, su, sv, st))
    peers = ny * nx // 2
    row_packet = ((N_SLOTS * groups + 1) * SUB, LANES)
    column_packet = ((SUB + 1) * SUB, LANES)
    chunk = (peers, CHUNK_ROW + groups * SUB, LANES)
    tile = (SUB, LANES)
    (chunks,) = call(
        functools.partial(chunk_kernel, levels, peers),
        [chunk],
        (u, v, su, sv, count, elev),
        scratch=[pltpu.VMEM(flat, jnp.float32)] * 4
        + [pltpu.VMEM(tile, count.dtype), pltpu.VMEM(tile, jnp.float32), pltpu.SemaphoreType.DMA((6,))],
        flops=1 << 20,
        size=1 << 21,
        far_in=True,
        limit=60,
    )
    y1, y2, xp = call(
        functools.partial(packet_kernel, levels),
        [row_packet, row_packet, column_packet],
        (u, v, t, su, sv, st, count),
        flops=1 << 20,
        size=1 << 21,
    )
    axes = ("ty", "y", "core")
    ga = lax.all_to_all(chunks, ("ty", "y"), 0, 0)
    x1 = lax.ppermute(xp, axes, swaps(shape, "x", 0))
    x2 = lax.ppermute(xp, axes, swaps(shape, "x", 1))
    y1 = lax.ppermute(y1, axes, swaps(shape, "y", 0))
    y2 = lax.ppermute(y2, axes, swaps(shape, "y", 1))
    dtx, du_t, edge = call(
        functools.partial(column_kernel, levels),
        [flat, flat, (len(FLOW_FIELDS) * SUB * SUB, LANES)],
        (u, v, t, st, su, sv, count, x1, x2),
        flops=1 << 22,
        size=1 << 21,
    )
    ga, y1, y2, dtx = lax.optimization_barrier((ga, y1, y2, dtx))
    gb = lax.ppermute(ga, axes, swaps(shape, "x", 0))
    dt, dv_t, made, outer = call(
        functools.partial(row_kernel, levels, ny),
        [flat, flat, (groups * MADE_ROWS * SUB, LANES), (len(OUTER_ROWS) * SUB, LANES)],
        (u, v, t, st, count, y1, y2, dtx),
        scratch=(pltpu.VMEM(flat, jnp.float32), pltpu.SemaphoreType.DMA((groups,))),
        flops=1 << 22,
        size=1 << 21,
        far_out=(0,),
    )
    grid = pltpu.VMEM((ny, nx, SUB, LANES), jnp.float32)
    faces, residuals = (pltpu.VMEM((n, ny, nx, SUB, LANES), jnp.float32) for n in (7, ITERS))
    du, dv, eta = call(
        functools.partial(flow_kernel, levels, ny, nx),
        [flat, flat, (SUB, LANES)],
        (u, v, su, sv, ga, gb, y1, y2, edge, outer, made, du_t, dv_t),
        far_out=(0, 1, 2),
        scratch=(grid, faces, residuals)
        + tuple(pltpu.VMEM(shape, jnp.float32) for shape in (tile, flat, flat))
        + (pltpu.SemaphoreType.DMA((2 * groups + 1,)),),
        flops=1 << 23,
        size=1 << 22,
    )
    whole = (levels, SUB, LANES)
    return du.reshape(whole), dv.reshape(whole), dt.reshape(whole), eta


def solution(mesh):
    ny, nx = mesh.shape["ty"], mesh.shape["tx"]
    split = Mesh(mesh.devices.reshape(ny, nx // 2, 2), ("ty", "y", "core"))
    deep, flat = P(None, "ty", ("y", "core")), P("ty", ("y", "core"))
    return jax.shard_map(
        functools.partial(on_device, (ny, nx)),
        mesh=split,
        in_specs=(deep, deep, deep, flat, deep, deep, deep, flat),
        out_specs=(deep, deep, deep, flat),
        check_vma=False,
    )
```

```python
import functools

import jax
import jax.numpy as jnp
from jax import lax
from jax.experimental import pallas as pl
from jax.experimental.pallas import tpu as pltpu
from jax.sharding import Mesh, PartitionSpec as P

ITERS = 4
ADVECT = 0.1
GRAVITY_DT = 0.1

SUB = 8
LANES = 128
SEG = 32
FIELDS = ("u", "v", "t", "st", "su", "sv")
BAND_BLOCKS = 32
ADJOINT_PARTS = ((4, 0), (1, 2), (3,))
FLOW_FIELDS = ("u", "v", "su", "sv")
FLOW_ROWS = {"u": (-2, 8), "v": (-1, 9), "su": (-1, 8), "sv": (-1, 8)}
OUTER_ROWS = tuple((n, r) for n in FLOW_FIELDS for r in range(FLOW_ROWS[n][0], FLOW_ROWS[n][1] + 1) if not 0 <= r < 8)
MADE_SIZES = (10, 8, 9, 9, 8, 8)
MADE_ROWS = sum(MADE_SIZES)
SOUTH_SLOTS = {("u", -2): 0, ("u", -1): 1, ("v", -1): 2, ("t", -2): 3, ("t", -1): 4, ("st", -2): 5, ("st", -1): 6}
SOUTH_SLOTS.update({("su", -1): 7, ("sv", -1): 8})
NORTH_SLOTS = {("u", 8): 0, ("v", 8): 1, ("v", 9): 2, ("t", 8): 3, ("st", 8): 5, ("st", 9): 6, ("su", 8): 7, ("sv", 8): 8}
N_SLOTS = 9
CHUNK_LOAD = SUB
CHUNK_EDGE = 2 * SUB
CHUNK_ROW = 3 * SUB
EDGE_LEVELS = 20
CORNERS = (("u", 6, 0), ("u", 7, 0), ("u", 7, 1), ("su", 7, 0), ("v", 7, 127), ("u", 7, 127))
CORNERS += (("v", 0, 127), ("v", 1, 127), ("v", 0, 126), ("sv", 0, 127), ("v", 0, 0), ("u", 0, 0))
CORNER_PLACES = {
    ("u", -2): (("se", 0, 24),),
    ("u", -1): (("se", 1, 24), ("se", 2, 25), ("sw", 5, 7)),
    ("su", -1): (("se", 3, 24),),
    ("v", -1): (("sw", 4, 7),),
    ("v", 8): (("nw", 6, 7), ("nw", 8, 6), ("ne", 10, 24)),
    ("u", 8): (("ne", 11, 24),),
    ("v", 9): (("nw", 7, 7),),
    ("sv", 8): (("nw", 9, 7),),
}


def lane_ids():
    return lax.broadcasted_iota(jnp.int32, (SUB, LANES), 1)


def row_ids():
    return lax.broadcasted_iota(jnp.int32, (SUB, LANES), 0)


def roll_lanes(value, amount):
    amount %= LANES
    return value if amount == 0 else pltpu.roll(value, amount, 1)


def roll_rows(value, amount):
    amount %= SUB
    return value if amount == 0 else pltpu.roll(value, amount, 0)


def at(value, shift):
    return roll_lanes(value, -shift)


def row_of(tile, row):
    return jnp.broadcast_to(tile[row : row + 1, :], (SUB, LANES))


def group_count(levels):
    return -(-levels // SUB)


def load_group(ref, row, q, levels):
    first = min(q * SUB, levels - SUB)
    value = ref[pl.ds(first * SUB + row, SUB, stride=SUB), :]
    return roll_rows(value, first - q * SUB)


def store_group(ref, row, q, levels, value):
    count = min(SUB, levels - q * SUB)
    ref[pl.ds(q * SUB * SUB + row, count, stride=SUB), :] = value[:count]


def level_numbers(groups):
    rows = row_ids()
    numbers = [(rows + q * SUB).astype(jnp.float32) for q in range(groups)]
    return numbers + [(rows + (lane_ids() >> 5) * SUB).astype(jnp.float32)]


def edge_of_tile(west, centre, east):
    lanes = lane_ids()
    out = jnp.where(lanes < 8, roll_lanes(west, 8), roll_lanes(centre, 8))
    out = jnp.where(lanes >= 16, roll_lanes(centre, 24), out)
    out = jnp.where(lanes >= 24, roll_lanes(east, 24), out)
    out = jnp.where(lanes < SEG, out, roll_lanes(out, SEG))
    return jnp.where(lanes < 2 * SEG, out, roll_lanes(out, 2 * SEG))


def chunk_kernel(
    levels, peers, u_hbm, v_hbm, su_hbm, sv_hbm, count_hbm, elev_hbm, chunk_ref,
    u_ref, v_ref, su_ref, sv_ref, count_ref, elev_ref, sems,
):
    pairs = (
        (count_hbm, count_ref), (su_hbm, su_ref), (sv_hbm, sv_ref), (elev_hbm, elev_ref), (u_hbm, u_ref), (v_hbm, v_ref),
    )
    copies = [pltpu.make_async_copy(source, target, sems.at[n]) for n, (source, target) in enumerate(pairs)]
    for copy in copies:
        copy.start()
    groups = group_count(levels)
    lanes, rows = lane_ids(), row_ids()
    refs = {"u": u_ref, "v": v_ref, "su": su_ref, "sv": sv_ref}
    for copy in copies[:4]:
        copy.wait()
    count = count_ref[...].astype(jnp.float32)
    zero = jnp.zeros((SUB, LANES), jnp.float32)

    wet_u = jnp.where(lanes == 0, 0.0, jnp.minimum(count, roll_lanes(count, 1)))
    wet_v = jnp.where(rows == 0, 0.0, jnp.minimum(count, roll_rows(count, 1)))
    col_u, col_v, edge = [zero] * 4, [zero] * 4, zero
    for k in range(levels):
        su_level = su_ref[k * SUB : (k + 1) * SUB, :]
        col_u[k % 4] = col_u[k % 4] + jnp.where(wet_u > float(k), su_level, 0.0)
        col_v[k % 4] = col_v[k % 4] + jnp.where(wet_v > float(k), sv_ref[k * SUB : (k + 1) * SUB, :], 0.0)
        lane = SEG * (k // EDGE_LEVELS) + k % EDGE_LEVELS
        edge = jnp.where(lanes == lane, roll_lanes(su_level, lane), edge)
    col_u, col_v = ((col[0] + col[1]) + (col[2] + col[3]) for col in (col_u, col_v))
    load = elev_ref[...] + GRAVITY_DT * (at(col_u, 1) - col_u + roll_rows(col_v, -1) - col_v)

    for copy in copies[4:]:
        copy.wait()
    for place, (name, row, column) in enumerate(CORNERS):
        for q in range(groups):
            lane = SEG * q + EDGE_LEVELS + place
            edge = jnp.where(lanes == lane, roll_lanes(load_group(refs[name], row, q, levels), lane - column), edge)

    south_row = [load_group(sv_ref, 0, q, levels) for q in range(groups)]

    def put(peer, carry):
        chunk_ref[peer, 0:SUB, :] = count
        chunk_ref[peer, CHUNK_LOAD : CHUNK_LOAD + SUB, :] = load
        chunk_ref[peer, CHUNK_EDGE : CHUNK_EDGE + SUB, :] = edge
        for q in range(groups):
            chunk_ref[peer, CHUNK_ROW + q * SUB : CHUNK_ROW + (q + 1) * SUB, :] = south_row[q]
        return carry

    lax.fori_loop(0, peers, put, 0, unroll=4)


def packet_kernel(levels, u_ref, v_ref, t_ref, su_ref, sv_ref, st_ref, count_ref, y1_ref, y2_ref, x_ref):
    groups = group_count(levels)
    lanes = lane_ids()
    zero = jnp.zeros((SUB, LANES), jnp.float32)
    count = count_ref[...].astype(jnp.float32)
    even = lax.axis_index("ty") % 2 == 0
    refs = {"u": u_ref, "v": v_ref, "t": t_ref, "st": st_ref, "su": su_ref, "sv": sv_ref}
    loaded = {}
    for name in FIELDS:
        for row in range(SUB):
            for q in range(groups):
                loaded[name, row, q] = load_group(refs[name], row, q, levels)

    for slot in range(N_SLOTS):
        upper = [(name, row + SUB) for (name, row), place in SOUTH_SLOTS.items() if place == slot]
        lower = [(name, row - SUB) for (name, row), place in NORTH_SLOTS.items() if place == slot]
        for q in range(groups):
            to_north = loaded[(*upper[0], q)]
            to_south = loaded[(*lower[0], q)] if lower else zero
            place = pl.ds((slot * groups + q) * SUB, SUB)
            y1_ref[place, :] = jnp.where(even, to_north, to_south)
            y2_ref[place, :] = jnp.where(even, to_south, to_north)
    y1_ref[N_SLOTS * groups * SUB :, :] = count
    y2_ref[N_SLOTS * groups * SUB :, :] = count

    for row in range(SUB):
        packet = zero
        for field, name in enumerate(FIELDS):
            for q in range(groups):
                lane = SEG * q + 4 * field
                packet = jnp.where((lanes >= lane) & (lanes < lane + 4), roll_lanes(loaded[name, row, q], lane + 2), packet)
        x_ref[row * SUB : (row + 1) * SUB, :] = packet
    x_ref[SUB * SUB :, :] = count


def joined(parts):
    return Many([item for part in parts for item in part.items], len(parts))


class Many:
    def __init__(self, items, parts=1):
        self.items = list(items)
        self.parts = parts

    def __getitem__(self, where):
        if not isinstance(where, slice):
            return self.items[where]
        rows = len(self.items) // self.parts
        return Many([item for n in range(self.parts) for item in self.items[n * rows : (n + 1) * rows][where]], self.parts)

    def __len__(self):
        return len(self.items)

    def split(self):
        rows = len(self.items) // self.parts
        return [Many(self.items[n * rows : (n + 1) * rows]) for n in range(self.parts)]

    def apply(self, operation, *others):
        others = [other.items if isinstance(other, Many) else [other] * len(self) for other in others]
        assert all(len(other) == len(self) for other in others)
        return Many([operation(*parts) for parts in zip(self.items, *others)], self.parts)

    def __add__(self, other):
        return self.apply(lambda a, b: a + b, other)

    def __sub__(self, other):
        return self.apply(lambda a, b: a - b, other)

    def __mul__(self, other):
        return self.apply(lambda a, b: a * b, other)

    def __gt__(self, other):
        return self.apply(lambda a, b: a > b, other)

    def at(self, shift):
        return self.apply(lambda a: at(a, shift))

    def rolled(self, amount):
        return self.apply(lambda a: roll_lanes(a, amount))

    def minimum(self, other):
        return self.apply(jnp.minimum, other)

    def where(self, mask, other):
        return self.apply(lambda a, m, b: jnp.where(m, a, b), mask, other)


def edges_of_groups(parts):
    lanes = lane_ids()
    out = parts[0].rolled(8)
    for q in range(1, len(parts)):
        out = parts[q].rolled(SEG * q + 8).where(lanes >= SEG * q, out)
    return out.rolled(16).where((lanes & (SEG - 1)) >= 16, out)


def insert_sides(edge, west, east, field):
    place = lane_ids() & (SEG - 1)
    edge = west.rolled(6 - 4 * field).where((place == 6) | (place == 7), edge)
    return east.rolled(22 - 4 * field).where((place == 24) | (place == 25), edge)


def outer_columns(edge):
    return edge.rolled(-16).where((lane_ids() & (SEG - 1)) < 8, edge)


def merge_edges(values, outer, q):
    lanes = lane_ids()
    return outer.rolled(-(SEG * q + 8)).where((lanes < 2) | (lanes >= LANES - 2), values)


def load_rows(ref, q, levels):
    return Many(load_group(ref, row, q, levels) for row in range(SUB))


def store_rows(ref, q, levels, values):
    for row in range(SUB):
        store_group(ref, row, q, levels, values[row])


def rows_of(tiles, first, last):
    return Many(row_of(tiles[row // SUB + 1], row % SUB) for row in range(first, last + 1))


def slot_reader(y1_ref, y2_ref, groups):
    even = lax.axis_index("ty") % 2 == 0

    def read(name, row, q):
        slot = (SOUTH_SLOTS if row < 0 else NORTH_SLOTS)[name, row]
        place = pl.ds((slot * groups + q) * SUB, SUB)
        one, two = y1_ref[place, :], y2_ref[place, :]
        return jnp.where(even, two, one) if row < 0 else jnp.where(even, one, two)

    def counts():
        place = pl.ds(N_SLOTS * groups * SUB, SUB)
        one, two = y1_ref[place, :], y2_ref[place, :]
        return jnp.where(even, two, one), jnp.where(even, one, two)

    return read, counts


def side_reader(x1_ref, x2_ref):
    even = lax.axis_index("core") % 2 == 0

    def read(row):
        place = pl.ds(row * SUB, SUB)
        one, two = x1_ref[place, :], x2_ref[place, :]
        return jnp.where(even, two, one), jnp.where(even, one, two)

    return read


def face_values(t0, t_before, t_after, t_before2):
    return ((t0 + t_before) * 7.0 - (t_after + t_before2)) * (1.0 / 12.0)


def edge_rows(ref, west, east, levels, groups, name):
    own = edges_of_groups([load_rows(ref, q, levels) for q in range(groups)])
    return insert_sides(own, west, east, FIELDS.index(name))


def column_kernel(
    levels, u_ref, v_ref, t_ref, st_ref, su_ref, sv_ref, count_ref, x1_ref, x2_ref, dt_ref, du_ref, edge_ref
):
    groups = group_count(levels)
    read_sides = side_reader(x1_ref, x2_ref)
    numbers = level_numbers(groups)
    zero = jnp.zeros((SUB, LANES), jnp.float32)
    count = count_ref[...].astype(jnp.float32)
    count_west, count_east = read_sides(SUB)
    count_edge = edge_of_tile(count_west, count, count_east)

    def counts(tile):
        return tuple(rows_of((None, part, None), 0, 7) for part in (tile, jnp.minimum(tile, at(tile, -1))))

    def along(level, wet, wet_u, u, t, st):
        cell = (st * -ADVECT).where(wet > level, zero)
        flux = (cell.at(-1) - cell).where(wet_u > level, zero)
        back = u * flux
        face = face_values(t, t.at(-1), t.at(1), t.at(-2))
        return ((back + back.at(1)) * 7.0 - (back.at(-1) + back.at(2))) * (1.0 / 12.0), flux * face

    sides = [read_sides(row) for row in range(SUB)]
    west, east = Many(side[0] for side in sides), Many(side[1] for side in sides)
    u, t, st = (
        edge_rows(ref, west, east, levels, groups, name) for name, ref in (("u", u_ref), ("t", t_ref), ("st", st_ref))
    )
    edge_t, edge_u = (outer_columns(part) for part in along(numbers[groups], *counts(count_edge), u, t, st))
    own = counts(count)
    for q in range(groups):
        st = load_rows(st_ref, q, levels)
        from_x, to_u = along(numbers[q], *own, load_rows(u_ref, q, levels), load_rows(t_ref, q, levels), st)
        store_rows(dt_ref, q, levels, st + merge_edges(from_x, edge_t, q))
        store_rows(du_ref, q, levels, merge_edges(to_u, edge_u, q))
    flow = (u,) + tuple(
        edge_rows(ref, west, east, levels, groups, name) for name, ref in (("v", v_ref), ("su", su_ref), ("sv", sv_ref))
    )
    for n, rows in enumerate(flow):
        for row in range(SUB):
            edge_ref[(n * SUB + row) * SUB : (n * SUB + row + 1) * SUB, :] = rows[row]


def turns(ny):
    first_row = (lax.axis_index("ty") * SUB).astype(jnp.float32)
    scale = 0.5 / (ny * SUB)
    turn_u = Many(0.25 + (first_row + (row + 0.5)) * scale for row in range(-1, 8))
    return turn_u, Many(-0.25 - (first_row + row) * scale for row in range(0, 9))


def prepared(u, v, turn_u, turn_v):
    v_pair, u_pair = v[:-1] + v[1:], u[2:10] + u[1:9]
    return (
        (v_pair + v_pair.at(-1)) * 0.25,
        (u_pair + u_pair.at(1)) * 0.25,
        (u[:-2] - u[2:]) * 0.25 + turn_u,
        (v[1:10].at(-1) - v[1:10].at(1)) * 0.25 + turn_v,
        u[2:10].at(1) - u[2:10].at(-1),
        v[2:10] - v[0:8],
    )


def row_kernel(
    levels, ny, u_ref, v_ref, t_ref, st_ref, count_ref, y1_ref, y2_ref, dtx_ref, dt_hbm, dv_ref, made_ref, edge_ref, dt_ref, sems
):
    groups = group_count(levels)
    read_row, read_counts = slot_reader(y1_ref, y2_ref, groups)
    numbers = level_numbers(groups)
    zero = jnp.zeros((SUB, LANES), jnp.float32)
    count = count_ref[...].astype(jnp.float32)
    count_south, count_north = read_counts()
    counts = rows_of((count_south, count, count_north), -2, 9)
    counts_v = counts[1:].minimum(counts[:-1])
    out = []
    for n, (name, row) in enumerate(OUTER_ROWS):
        (edge,) = edges_of_groups([Many([read_row(name, row, q)]) for q in range(groups)]).items
        edge_ref[n * SUB : (n + 1) * SUB, :] = edge
    for q in range(groups):
        level = numbers[q]

        def rows(name, ref, first, last):
            south = [read_row(name, row, q) for row in range(first, 0)]
            north = [read_row(name, row, q) for row in range(SUB, last + 1)]
            return Many(south + load_rows(ref, q, levels).items + north)

        t, st, v = rows("t", t_ref, -2, 8), rows("st", st_ref, -2, 9), rows("v", v_ref, -1, 9)
        made = prepared(rows("u", u_ref, -2, 8), v, *turns(ny))
        for n, value in enumerate(value for values in made for value in values.items):
            place = pl.ds((q * MADE_ROWS + n) * SUB, SUB)
            made_ref[place, :] = value
        cell = (st * -ADVECT).where(counts > level, zero)
        flux = (cell[:-1] - cell[1:]).where(counts_v > level, zero)
        back = v * flux
        from_y = ((back[1:9] + back[2:10]) * 7.0 - (back[0:8] + back[3:11])) * (1.0 / 12.0)
        to_v = flux[1:9] * face_values(t[2:10], t[1:9], t[3:11], t[0:8])
        store_rows(dt_ref, q, levels, load_rows(dtx_ref, q, levels) + from_y)
        store_rows(dv_ref, q, levels, to_v)
        part = pl.ds(q * SUB * SUB, min(SUB, levels - q * SUB) * SUB)
        out.append(pltpu.make_async_copy(dt_ref.at[part, :], dt_hbm.at[part, :], sems.at[q]))
        out[-1].start()
    for copy in out:
        copy.wait()


def total(value):
    return jnp.sum(value, axis=(0, 1), keepdims=True)


def surface_solve(levels, ny, nx, read, count_ref, face_ref, r_refs, beside_setup, beside_sum):
    groups = group_count(levels)
    lanes, rows = lane_ids(), row_ids()
    numbers = level_numbers(groups)
    zero = jnp.zeros((SUB, LANES), jnp.float32)
    band = max(1, min(ny, BAND_BLOCKS // nx))
    while ny % band:
        band -= 1
    cells = [(dj, i) for dj in range(band) for i in range(nx)]

    def loop(body, init=0):
        if ny * nx <= 32:
            for j in range(0, ny, band):
                init = body(j, init)
            return init
        return lax.fori_loop(0, ny // band, lambda step, carry: body(step * band, carry), init)

    def get(ref, j):
        return Many(ref[j + dj, i] for dj, i in cells)

    def put(ref, j, values):
        for (dj, i), value in zip(cells, values.items):
            ref[j + dj, i] = value

    def beside(values, step):
        return Many(values[dj * nx + min(max(i + step, 0), nx - 1)] for dj, i in cells)

    def below(ref, j, values):
        outside = [ref[max(j - 1, 0) if isinstance(j, int) else jnp.maximum(j - 1, 0), i] for i in range(nx)]
        return Many(outside + values.items[:-nx])

    def above(ref, j, values):
        top = min(j + band, ny - 1) if isinstance(j, int) else jnp.minimum(j + band, ny - 1)
        outside = [ref[top, i] for i in range(nx)]
        return Many(values.items[nx:] + outside)

    def west_of(values):
        return beside(values, -1).where(lanes == LANES - 1, values).rolled(1)

    def east_of(values):
        return beside(values, 1).where(lanes == 0, values).rolled(-1)

    def south_of(ref, j, values):
        return below(ref, j, values).where(rows == SUB - 1, values).apply(lambda a: roll_rows(a, 1))

    def north_of(ref, j, values):
        return above(ref, j, values).where(rows == 0, values).apply(lambda a: roll_rows(a, -1))

    def depth(wet):
        return wet.apply(lambda m: m * (m * (GRAVITY_DT * 0.5 / levels) + GRAVITY_DT * (1.0 - 0.5 / levels)))

    def gather(j, carry):
        put(count_ref, j, Many(read(j + dj, i, 0) for dj, i in cells))
        return carry

    loop(gather)

    def faces(j, carry):
        count = get(count_ref, j)
        wet_u, wet_v = count.minimum(west_of(count)), count.minimum(south_of(count_ref, j, count))
        first_column = [(lanes == 0) if i == 0 else (lanes < 0) for dj, i in cells]
        first_row = [(rows == 0) & (j + dj == 0) for dj, i in cells]
        wet_u = Many([zero] * len(cells)).where(Many(first_column), wet_u)
        wet_v = Many([zero] * len(cells)).where(Many(first_row), wet_v)
        put(face_ref.at[0], j, depth(wet_u))
        put(face_ref.at[1], j, depth(wet_v))
        edge = Many(read(j + dj, i, CHUNK_EDGE) for dj, i in cells)
        wet_west = wet_u.apply(lambda a: jnp.broadcast_to(a[:, 0:1], (SUB, LANES)))
        place = lanes & (SEG - 1)
        number = (lanes >> 5) * EDGE_LEVELS + place
        reach = jnp.where((place < EDGE_LEVELS) & (number < levels), number.astype(jnp.float32), float(levels))
        inside = edge.where(wet_west > reach, zero)
        col_u = inside.apply(lambda a: jnp.broadcast_to(jnp.sum(a, axis=1, keepdims=True), (SUB, LANES)))
        put(face_ref.at[4], j, col_u * GRAVITY_DT)
        wet_south = wet_v.apply(lambda a: row_of(a, 0))
        col_v = Many([zero] * len(cells))
        for q in range(groups):
            south = Many(read(j + dj, i, CHUNK_ROW + q * SUB) for dj, i in cells)
            col_v = col_v + south.where(wet_south > numbers[q], zero)
        col_v = col_v.apply(lambda a: jnp.broadcast_to(jnp.sum(a, axis=0, keepdims=True), (SUB, LANES)))
        put(face_ref.at[5], j, col_v * GRAVITY_DT)
        return carry

    loop(faces)
    beside_setup()

    def start(j, carry):
        load = Many(read(j + dj, i, CHUNK_LOAD) for dj, i in cells)
        col_u, col_v = get(face_ref.at[4], j), get(face_ref.at[5], j)
        depth_u, depth_v = get(face_ref.at[0], j), get(face_ref.at[1], j)
        last_column = Many((lanes == LANES - 1) if i + 1 < nx else (lanes < 0) for dj, i in cells)
        at_end = Many((lanes == LANES - 1) if i + 1 == nx else (lanes < 0) for dj, i in cells)
        last_row = Many((rows == SUB - 1) & (j + dj + 1 < ny) for dj, i in cells)
        at_top = Many((rows == SUB - 1) & (j + dj + 1 == ny) for dj, i in cells)
        none = Many([zero] * len(cells))
        load = load - col_u.where(lanes == 0, zero) - col_v.where(rows == 0, zero)
        load = load + beside(col_u, 1).where(last_column, none) + above(face_ref.at[5], j, col_v).where(last_row, none)
        depth_east = none.where(at_end, east_of(depth_u))
        depth_north = none.where(at_top, north_of(face_ref.at[1], j, depth_v))
        put(face_ref.at[2], j, depth_east)
        put(face_ref.at[3], j, depth_north)
        put(face_ref.at[6], j, (depth_u + depth_east) + (depth_v + depth_north) + 1.0)
        put(r_refs.at[0], j, load)
        return carry

    def gathered(partial, values):
        items = list(values.items)
        while len(items) > 1:
            items = [a + b for a, b in zip(items[::2], items[1::2])] + items[len(items) // 2 * 2 :]
        return partial + items[0]

    loop(start)

    def products(k):
        r_ref = r_refs.at[k]

        def body(j, carry):
            r = get(r_ref, j)
            image = r * get(face_ref.at[6], j) - get(face_ref.at[0], j) * west_of(r) - get(face_ref.at[2], j) * east_of(r)
            image = image - get(face_ref.at[1], j) * south_of(r_ref, j, r)
            image = image - get(face_ref.at[3], j) * north_of(r_ref, j, r)
            put(face_ref.at[4], j, image)
            return gathered(carry[0], r * r), gathered(carry[1], r * image)

        return [total(part) for part in loop(body, (zero, zero))]

    norm, product = products(0)
    beside_sum(0)
    step = norm / product
    steps, ratios = [step], []

    for k in range(ITERS - 1):

        def advance(j, carry):
            image = get(face_ref.at[4], j)
            if k > 0:
                image = image + get(face_ref.at[5], j) * ratio
            if k + 2 < ITERS:
                put(face_ref.at[5], j, image)
            put(r_refs.at[k + 1], j, get(r_refs.at[k], j) - image * step)
            return carry

        loop(advance)
        new, product = products(k + 1)
        beside_sum(k + 1)
        ratio = new / norm
        step = new / (product - ratio * new / step)
        norm = new
        steps.append(step)
        ratios.append(ratio)

    weights = [steps[-1]]
    for k in reversed(range(ITERS - 1)):
        weights.append(steps[k] + ratios[k] * weights[-1])
    weights.reverse()
    return weights


def flow_kernel(
    levels, ny, nx, u_ref, v_ref, su_ref, sv_ref, ga_ref, gb_ref, y1_ref, y2_ref, edge_ref, outer_ref, made_ref, dut_ref, dvt_ref,
    du_hbm, dv_hbm, eta_hbm, count_s, face_s, r_s, eta_ref, du_ref, dv_ref, sems,
):
    groups = group_count(levels)
    lanes, rows_id = lane_ids(), row_ids()
    core = lax.axis_index("core")
    my_j = lax.axis_index("ty")
    my_i = lax.axis_index("y") * 2 + core
    numbers = level_numbers(groups)
    thick = [1.0 + number * (1.0 / levels) for number in numbers]
    read_row, _ = slot_reader(y1_ref, y2_ref, groups)
    zero = jnp.zeros((SUB, LANES), jnp.float32)

    def read(j, i, first):
        where = (j * (nx // 2) + i // 2, pl.ds(first, SUB), slice(None))
        return jnp.where(core == i % 2, ga_ref[where], gb_ref[where])

    def block(dj, di, get):
        return get(jnp.clip(my_j + dj, 0, ny - 1), jnp.clip(my_i + di, 0, nx - 1))

    def near(dj, di, get):
        j, i = jnp.clip(my_j + dj, 0, ny - 1), jnp.clip(my_i + di, 0, nx - 1)
        inside = (my_j + dj >= 0) & (my_j + dj < ny) & (my_i + di >= 0) & (my_i + di < nx)
        return jnp.where(inside, get(j, i), 0.0)

    corner_tiles = {
        name: near(dj, di, lambda j, i: read(j, i, CHUNK_EDGE))
        for name, dj, di in (("se", -1, 1), ("sw", -1, -1), ("nw", 1, -1), ("ne", 1, 1))
    }

    def insert_corners(edge, name, row):
        for which, value, target in CORNER_PLACES.get((name, row), ()):
            there = (lanes & (SEG - 1)) == target
            edge = jnp.where(there, roll_lanes(corner_tiles[which], target - EDGE_LEVELS - value), edge)
        return edge

    def rows(name, ref, q, first, last):
        south = [read_row(name, row, q) for row in range(first, 0)]
        north = [read_row(name, row, q) for row in range(SUB, last + 1)]
        return Many(south + load_rows(ref, q, levels).items + north)

    def edges(name):
        first, last = FLOW_ROWS[name]
        n = FLOW_FIELDS.index(name)

        def register(row):
            if 0 <= row < SUB:
                return edge_ref[(n * SUB + row) * SUB : (n * SUB + row + 1) * SUB, :]
            place = OUTER_ROWS.index((name, row)) * SUB
            return insert_corners(outer_ref[place : place + SUB, :], name, row)

        return Many(register(row) for row in range(first, last + 1))

    refs = {"u": u_ref, "v": v_ref, "su": su_ref, "sv": sv_ref}
    data, made = {}, {}

    def prepare(part):
        if part == groups:
            data[part] = [edges(name) for name in FLOW_FIELDS]
            made[part] = prepared(*data[part][:2], *turns(ny))
            return
        data[part] = [rows(name, refs[name], part, *FLOW_ROWS[name]) for name in FLOW_FIELDS]
        made[part], n = [], part * MADE_ROWS
        for size in MADE_SIZES:
            made[part].append(Many(made_ref[k * SUB : (k + 1) * SUB, :] for k in range(n, n + size)))
            n += size

    def pairs(get, operation):
        tiles = [[get(dj, di) for di in (-1, 0, 1)] for dj in (-1, 0, 1)]
        out = []
        for south, own, north in ([row[1] for row in tiles], [edge_of_tile(*row) for row in tiles]):
            outer = jnp.where(rows_id == SUB - 1, south, north)
            below = roll_rows(jnp.where(rows_id == SUB - 1, south, own), 1)
            below_outer = roll_rows(jnp.where(rows_id == SUB - 2, south, own), 1)
            out.append(
                (operation(own, at(own, -1)), operation(outer, at(outer, -1)), operation(own, below), operation(outer, below_outer))
            )
        return out

    def outer_and_own(own, outer):
        return Many([row_of(outer, SUB - 1)] + [row_of(own, row) for row in range(SUB)] + [row_of(outer, 0)])

    wet_counts, differences = [], []

    def beside_setup():
        wet_counts.extend(pairs(lambda dj, di: near(dj, di, lambda j, i: count_s[j, i]), jnp.minimum))

    def beside_sum(k):
        if k == ITERS - 1:
            prepare(groups)
        differences.append(pairs(lambda dj, di: block(dj, di, lambda j, i: r_s[k, j, i]), lambda a, b: a - b))

    weights = surface_solve(levels, ny, nx, read, count_s, face_s, r_s, beside_setup, beside_sum)

    def weighted(parts):
        total_of = parts[0] * weights[0]
        for part, weight in zip(parts[1:], weights[1:]):
            total_of = total_of + part * weight
        return total_of

    slopes = [[weighted([d[kind][n] for d in differences]) for n in range(4)] for kind in range(2)]
    eta_ref[...] = weighted([r_s[k, my_j, my_i] for k in range(ITERS)])
    out = [pltpu.make_async_copy(eta_ref, eta_hbm, sems.at[0])]
    out[0].start()

    def adjoint(parts):
        u, v, su, sv = (joined([data[part][n] for part in parts]) for n in range(4))
        v_bar, u_bar, from_v_bar, from_u_bar, u_across, v_across = (
            joined([made[part][n] for part in parts]) for n in range(len(MADE_SIZES))
        )

        def each(values):
            return Many([values[part] for part in parts for _ in range(SUB + 2)], len(parts))

        def around(of, n):
            return joined([outer_and_own(*of[1 if part == groups else 0][n : n + 2]) for part in parts])

        wet_u, wet_v = around(wet_counts, 0) > each(numbers), around(wet_counts, 2) > each(numbers)
        u_cot = su + (around(slopes, 0) * each(thick)).where(wet_u, zero)
        v_cot = sv + (around(slopes, 2) * each(thick)).where(wet_v, zero)
        a, b = (u_cot * (0.5 * ADVECT)).where(wet_u, zero), (v_cot * (0.5 * ADVECT)).where(wet_v, zero)
        av, bu = a * v_bar, b[1:9] * u_bar
        au, bv = a[1:9] * u[2:10], b * v[:-1]
        to_v_bar, to_u_bar = a[:-1] * from_v_bar, b[1:] * from_u_bar
        near_u, near_v = to_u_bar[:-1] + to_u_bar[1:], to_v_bar[1:] + to_v_bar[:-1]
        du = u_cot[1:9] - a[1:9] * u_across + av[2:] - av[:-2] + near_u
        du = du + au.at(1) + (near_u - au).at(-1)
        dv = v_cot[1:9] - b[1:9] * v_across + bv[2:] - bv[:-2] + near_v
        dv = dv + (near_v + bu).at(1) - bu.at(-1)
        return list(zip(du.split(), dv.split()))

    for part in range(groups):
        prepare(part)
    flow = {}
    for parts in ADJOINT_PARTS:
        flow.update(zip(parts, adjoint(parts)))
    edge_u, edge_v = (outer_columns(part) for part in flow[groups])
    for q in range(groups):
        du, dv = flow[q]
        store_rows(du_ref, q, levels, merge_edges(du, edge_u, q) + load_rows(dut_ref, q, levels))
        store_rows(dv_ref, q, levels, merge_edges(dv, edge_v, q) + load_rows(dvt_ref, q, levels))
        part = pl.ds(q * SUB * SUB, min(SUB, levels - q * SUB) * SUB)
        for target, source in ((du_hbm, du_ref), (dv_hbm, dv_ref)):
            out.append(pltpu.make_async_copy(source.at[part, :], target.at[part, :], sems.at[len(out)]))
            out[-1].start()
    for copy in out:
        copy.wait()


def swaps(mesh_shape, along, parity):
    ny, nx = mesh_shape
    pairs = []
    for j in range(ny):
        for i in range(nx):
            k, size = (j, ny) if along == "y" else (i, nx)
            other = k + 1 if k % 2 == parity else k - 1
            if 0 <= other < size:
                pairs.append((j * nx + i, other * nx + i if along == "y" else j * nx + other))
    return pairs


def call(kernel, outs, args, scratch=(), flops=0, size=0, far_in=False, far_out=(), limit=48):
    near, far = pl.BlockSpec(memory_space=pltpu.VMEM), pl.BlockSpec(memory_space=pltpu.HBM)
    outs = [out if isinstance(out, jax.ShapeDtypeStruct) else jax.ShapeDtypeStruct(out, jnp.float32) for out in outs]
    return pl.pallas_call(
        kernel,
        out_shape=outs,
        in_specs=[far if far_in else near] * len(args),
        out_specs=[far if n in far_out else near for n in range(len(outs))],
        scratch_shapes=list(scratch),
        compiler_params=pltpu.CompilerParams(vmem_limit_bytes=limit * 1024 * 1024),
        cost_estimate=pl.CostEstimate(flops=flops, bytes_accessed=size, transcendentals=0),
    )(*args)


def on_device(shape, u, v, t, count, su, sv, st, elev):
    ny, nx = shape
    levels = u.shape[0]
    groups = group_count(levels)
    flat = (levels * SUB, LANES)
    u, v, t, su, sv, st = (field.reshape(flat) for field in (u, v, t, su, sv, st))
    peers = ny * nx // 2
    row_packet = ((N_SLOTS * groups + 1) * SUB, LANES)
    column_packet = ((SUB + 1) * SUB, LANES)
    chunk = (peers, CHUNK_ROW + groups * SUB, LANES)
    tile = (SUB, LANES)
    (chunks,) = call(
        functools.partial(chunk_kernel, levels, peers),
        [chunk],
        (u, v, su, sv, count, elev),
        scratch=[pltpu.VMEM(flat, jnp.float32)] * 4
        + [pltpu.VMEM(tile, count.dtype), pltpu.VMEM(tile, jnp.float32), pltpu.SemaphoreType.DMA((6,))],
        flops=1 << 20,
        size=1 << 21,
        far_in=True,
        limit=60,
    )
    y1, y2, xp = call(
        functools.partial(packet_kernel, levels),
        [row_packet, row_packet, column_packet],
        (u, v, t, su, sv, st, count),
        flops=1 << 20,
        size=1 << 21,
    )
    axes = ("ty", "y", "core")
    ga = lax.all_to_all(chunks, ("ty", "y"), 0, 0)
    x1 = lax.ppermute(xp, axes, swaps(shape, "x", 0))
    x2 = lax.ppermute(xp, axes, swaps(shape, "x", 1))
    y1 = lax.ppermute(y1, axes, swaps(shape, "y", 0))
    y2 = lax.ppermute(y2, axes, swaps(shape, "y", 1))
    dtx, du_t, edge = call(
        functools.partial(column_kernel, levels),
        [flat, flat, (len(FLOW_FIELDS) * SUB * SUB, LANES)],
        (u, v, t, st, su, sv, count, x1, x2),
        flops=1 << 22,
        size=1 << 21,
    )
    ga, y1, y2, dtx = lax.optimization_barrier((ga, y1, y2, dtx))
    gb = lax.ppermute(ga, axes, swaps(shape, "x", 0))
    dt, dv_t, made, outer = call(
        functools.partial(row_kernel, levels, ny),
        [flat, flat, (groups * MADE_ROWS * SUB, LANES), (len(OUTER_ROWS) * SUB, LANES)],
        (u, v, t, st, count, y1, y2, dtx),
        scratch=(pltpu.VMEM(flat, jnp.float32), pltpu.SemaphoreType.DMA((groups,))),
        flops=1 << 22,
        size=1 << 21,
        far_out=(0,),
    )
    grid = pltpu.VMEM((ny, nx, SUB, LANES), jnp.float32)
    faces, residuals = (pltpu.VMEM((n, ny, nx, SUB, LANES), jnp.float32) for n in (7, ITERS))
    du, dv, eta = call(
        functools.partial(flow_kernel, levels, ny, nx),
        [flat, flat, (SUB, LANES)],
        (u, v, su, sv, ga, gb, y1, y2, edge, outer, made, du_t, dv_t),
        far_out=(0, 1, 2),
        scratch=(grid, faces, residuals)
        + tuple(pltpu.VMEM(shape, jnp.float32) for shape in (tile, flat, flat))
        + (pltpu.SemaphoreType.DMA((2 * groups + 1,)),),
        flops=1 << 23,
        size=1 << 22,
    )
    whole = (levels, SUB, LANES)
    return du.reshape(whole), dv.reshape(whole), dt.reshape(whole), eta


def solution(mesh):
    ny, nx = mesh.shape["ty"], mesh.shape["tx"]
    split = Mesh(mesh.devices.reshape(ny, nx // 2, 2), ("ty", "y", "core"))
    deep, flat = P(None, "ty", ("y", "core")), P("ty", ("y", "core"))
    return jax.shard_map(
        functools.partial(on_device, (ny, nx)),
        mesh=split,
        in_specs=(deep, deep, deep, flat, deep, deep, deep, flat),
        out_specs=(deep, deep, deep, flat),
        check_vma=False,
    )
```

```python
import functools

import jax
import jax.numpy as jnp
from jax import lax
from jax.experimental import pallas as pl
from jax.experimental.pallas import tpu as pltpu
from jax.sharding import Mesh, PartitionSpec as P

ITERS = 4
ADVECT = 0.1
GRAVITY_DT = 0.1

SUB = 8
LANES = 128
SEG = 32
FIELDS = ("u", "v", "t", "st", "su", "sv")
BAND_BLOCKS = 32
ADJOINT_PARTS = ((4, 0), (1, 2), (3,))
FLOW_FIELDS = ("u", "v", "su", "sv")
FLOW_ROWS = {"u": (-2, 8), "v": (-1, 9), "su": (-1, 8), "sv": (-1, 8)}
OUTER_ROWS = tuple((n, r) for n in FLOW_FIELDS for r in range(FLOW_ROWS[n][0], FLOW_ROWS[n][1] + 1) if not 0 <= r < 8)
MADE_SIZES = (10, 8, 9, 9, 8, 8)
MADE_ROWS = sum(MADE_SIZES)
SOUTH_SLOTS = {("u", -2): 0, ("u", -1): 1, ("v", -1): 2, ("t", -2): 3, ("t", -1): 4, ("st", -2): 5, ("st", -1): 6}
SOUTH_SLOTS.update({("su", -1): 7, ("sv", -1): 8})
NORTH_SLOTS = {("u", 8): 0, ("v", 8): 1, ("v", 9): 2, ("t", 8): 3, ("st", 8): 5, ("st", 9): 6, ("su", 8): 7, ("sv", 8): 8}
N_SLOTS = 9
TILE = SUB * LANES
CHUNK_LOAD = TILE
CHUNK_ROW = 2 * TILE
WEST_LEVELS = LANES // SUB
CORNERS_PER_ROW = 4
CORNERS = (("u", 6, 0), ("u", 7, 0), ("u", 7, 1), ("su", 7, 0), ("v", 7, 127), ("u", 7, 127))
CORNERS += (("v", 0, 127), ("v", 1, 127), ("v", 0, 126), ("sv", 0, 127), ("v", 0, 0), ("u", 0, 0))
CORNER_PLACES = {
    ("u", -2): (("se", 0, 24),),
    ("u", -1): (("se", 1, 24), ("se", 2, 25), ("sw", 5, 7)),
    ("su", -1): (("se", 3, 24),),
    ("v", -1): (("sw", 4, 7),),
    ("v", 8): (("nw", 6, 7), ("nw", 8, 6), ("ne", 10, 24)),
    ("u", 8): (("ne", 11, 24),),
    ("v", 9): (("nw", 7, 7),),
    ("sv", 8): (("nw", 9, 7),),
}


def lane_ids():
    return lax.broadcasted_iota(jnp.int32, (SUB, LANES), 1)


def row_ids():
    return lax.broadcasted_iota(jnp.int32, (SUB, LANES), 0)


def roll_lanes(value, amount):
    amount %= LANES
    return value if amount == 0 else pltpu.roll(value, amount, 1)


def roll_rows(value, amount):
    amount %= SUB
    return value if amount == 0 else pltpu.roll(value, amount, 0)


def at(value, shift):
    return roll_lanes(value, -shift)


def row_of(tile, row):
    return jnp.broadcast_to(tile[row : row + 1, :], (SUB, LANES))


def group_count(levels):
    return -(-levels // SUB)


def load_group(ref, row, q, levels):
    first = min(q * SUB, levels - SUB)
    value = ref[pl.ds(first * SUB + row, SUB, stride=SUB), :]
    return roll_rows(value, first - q * SUB)


def store_group(ref, row, q, levels, value):
    count = min(SUB, levels - q * SUB)
    ref[pl.ds(q * SUB * SUB + row, count, stride=SUB), :] = value[:count]


def level_numbers(groups):
    rows = row_ids()
    numbers = [(rows + q * SUB).astype(jnp.float32) for q in range(groups)]
    return numbers + [(rows + (lane_ids() >> 5) * SUB).astype(jnp.float32)]


def edge_of_tile(west, centre, east):
    lanes = lane_ids()
    out = jnp.where(lanes < 8, roll_lanes(west, 8), roll_lanes(centre, 8))
    out = jnp.where(lanes >= 16, roll_lanes(centre, 24), out)
    out = jnp.where(lanes >= 24, roll_lanes(east, 24), out)
    out = jnp.where(lanes < SEG, out, roll_lanes(out, SEG))
    return jnp.where(lanes < 2 * SEG, out, roll_lanes(out, 2 * SEG))


def chunk_kernel(
    levels, peers, u_hbm, v_hbm, su_hbm, sv_hbm, count_hbm, elev_hbm, chunk_ref,
    u_ref, v_ref, su_ref, sv_ref, count_ref, elev_ref, sems,
):
    pairs = (
        (count_hbm, count_ref), (su_hbm, su_ref), (sv_hbm, sv_ref), (elev_hbm, elev_ref), (u_hbm, u_ref), (v_hbm, v_ref),
    )
    copies = [pltpu.make_async_copy(source, target, sems.at[n]) for n, (source, target) in enumerate(pairs)]
    for copy in copies:
        copy.start()
    groups = group_count(levels)
    lanes, rows = lane_ids(), row_ids()
    refs = {"u": u_ref, "v": v_ref, "su": su_ref, "sv": sv_ref}
    for copy in copies[:4]:
        copy.wait()
    count = count_ref[...].astype(jnp.float32)
    zero = jnp.zeros((SUB, LANES), jnp.float32)

    wet_u = jnp.where(lanes == 0, 0.0, jnp.minimum(count, roll_lanes(count, 1)))
    wet_v = jnp.where(rows == 0, 0.0, jnp.minimum(count, roll_rows(count, 1)))
    col_u, col_v = [zero] * 4, [zero] * 4
    west = [zero] * (levels // WEST_LEVELS + 1)
    for k in range(levels):
        su_level = su_ref[k * SUB : (k + 1) * SUB, :]
        col_u[k % 4] = col_u[k % 4] + jnp.where(wet_u > float(k), su_level, 0.0)
        col_v[k % 4] = col_v[k % 4] + jnp.where(wet_v > float(k), sv_ref[k * SUB : (k + 1) * SUB, :], 0.0)
        n = k // WEST_LEVELS
        there = lanes == rows + k % WEST_LEVELS * SUB
        west[n] = jnp.where(there, jnp.broadcast_to(su_level[:, 0:1], (SUB, LANES)), west[n])
    col_u, col_v = ((col[0] + col[1]) + (col[2] + col[3]) for col in (col_u, col_v))
    load = elev_ref[...] + GRAVITY_DT * (at(col_u, 1) - col_u + roll_rows(col_v, -1) - col_v)

    for copy in copies[4:]:
        copy.wait()
    corners = [zero] * (len(CORNERS) // CORNERS_PER_ROW)
    for place, (name, row, column) in enumerate(CORNERS):
        n, base = place // CORNERS_PER_ROW, place % CORNERS_PER_ROW * SUB
        for q in range(groups):
            value = load_group(refs[name], row, q, levels)[:, column : column + 1]
            there = lanes == SEG * q + base + SUB - 1 - rows
            corners[n] = jnp.where(there, jnp.broadcast_to(value, (SUB, LANES)), corners[n])

    def in_a_row(tile):
        return jnp.broadcast_to(jnp.sum(tile, axis=0, keepdims=True), (SUB, LANES))

    tiles = [count, load] + [load_group(sv_ref, 0, q, levels) for q in range(groups)]
    for n, part in enumerate(west):
        tiles[-1] = jnp.where(rows == SUB - len(west) + n, in_a_row(part), tiles[-1])
    last = zero
    for n, part in enumerate(corners):
        last = jnp.where(rows == n, in_a_row(part), last)
    tiles = [tile.reshape(1, TILE) for tile in tiles + [last]]
    tiles[-1] = tiles[-1][:, : len(corners) * LANES]

    def put(peer, carry):
        first = 0
        for tile in tiles:
            chunk_ref[peer, :, first : first + tile.shape[1]] = tile
            first += tile.shape[1]
        return carry

    lax.fori_loop(0, peers, put, 0, unroll=4)


def packet_kernel(levels, u_ref, v_ref, t_ref, su_ref, sv_ref, st_ref, count_ref, y1_ref, y2_ref, x_ref):
    groups = group_count(levels)
    lanes = lane_ids()
    zero = jnp.zeros((SUB, LANES), jnp.float32)
    count = count_ref[...].astype(jnp.float32)
    even = lax.axis_index("ty") % 2 == 0
    refs = {"u": u_ref, "v": v_ref, "t": t_ref, "st": st_ref, "su": su_ref, "sv": sv_ref}
    loaded = {}
    for name in FIELDS:
        for row in range(SUB):
            for q in range(groups):
                loaded[name, row, q] = load_group(refs[name], row, q, levels)

    for slot in range(N_SLOTS):
        upper = [(name, row + SUB) for (name, row), place in SOUTH_SLOTS.items() if place == slot]
        lower = [(name, row - SUB) for (name, row), place in NORTH_SLOTS.items() if place == slot]
        for q in range(groups):
            to_north = loaded[(*upper[0], q)]
            to_south = loaded[(*lower[0], q)] if lower else zero
            place = pl.ds((slot * groups + q) * SUB, SUB)
            y1_ref[place, :] = jnp.where(even, to_north, to_south)
            y2_ref[place, :] = jnp.where(even, to_south, to_north)
    y1_ref[N_SLOTS * groups * SUB :, :] = count
    y2_ref[N_SLOTS * groups * SUB :, :] = count

    for row in range(SUB):
        packet = zero
        for field, name in enumerate(FIELDS):
            for q in range(groups):
                lane = SEG * q + 4 * field
                packet = jnp.where((lanes >= lane) & (lanes < lane + 4), roll_lanes(loaded[name, row, q], lane + 2), packet)
        x_ref[row * SUB : (row + 1) * SUB, :] = packet
    x_ref[SUB * SUB :, :] = count


def joined(parts):
    return Many([item for part in parts for item in part.items], len(parts))


class Many:
    def __init__(self, items, parts=1):
        self.items = list(items)
        self.parts = parts

    def __getitem__(self, where):
        if not isinstance(where, slice):
            return self.items[where]
        rows = len(self.items) // self.parts
        return Many([item for n in range(self.parts) for item in self.items[n * rows : (n + 1) * rows][where]], self.parts)

    def __len__(self):
        return len(self.items)

    def split(self):
        rows = len(self.items) // self.parts
        return [Many(self.items[n * rows : (n + 1) * rows]) for n in range(self.parts)]

    def apply(self, operation, *others):
        others = [other.items if isinstance(other, Many) else [other] * len(self) for other in others]
        assert all(len(other) == len(self) for other in others)
        return Many([operation(*parts) for parts in zip(self.items, *others)], self.parts)

    def __add__(self, other):
        return self.apply(lambda a, b: a + b, other)

    def __sub__(self, other):
        return self.apply(lambda a, b: a - b, other)

    def __mul__(self, other):
        return self.apply(lambda a, b: a * b, other)

    def __gt__(self, other):
        return self.apply(lambda a, b: a > b, other)

    def at(self, shift):
        return self.apply(lambda a: at(a, shift))

    def rolled(self, amount):
        return self.apply(lambda a: roll_lanes(a, amount))

    def minimum(self, other):
        return self.apply(jnp.minimum, other)

    def where(self, mask, other):
        return self.apply(lambda a, m, b: jnp.where(m, a, b), mask, other)


def edges_of_groups(parts):
    lanes = lane_ids()
    out = parts[0].rolled(8)
    for q in range(1, len(parts)):
        out = parts[q].rolled(SEG * q + 8).where(lanes >= SEG * q, out)
    return out.rolled(16).where((lanes & (SEG - 1)) >= 16, out)


def insert_sides(edge, west, east, field):
    place = lane_ids() & (SEG - 1)
    edge = west.rolled(6 - 4 * field).where((place == 6) | (place == 7), edge)
    return east.rolled(22 - 4 * field).where((place == 24) | (place == 25), edge)


def outer_columns(edge):
    return edge.rolled(-16).where((lane_ids() & (SEG - 1)) < 8, edge)


def merge_edges(values, outer, q):
    lanes = lane_ids()
    return outer.rolled(-(SEG * q + 8)).where((lanes < 2) | (lanes >= LANES - 2), values)


def load_rows(ref, q, levels):
    return Many(load_group(ref, row, q, levels) for row in range(SUB))


def store_rows(ref, q, levels, values):
    for row in range(SUB):
        store_group(ref, row, q, levels, values[row])


def rows_of(tiles, first, last):
    return Many(row_of(tiles[row // SUB + 1], row % SUB) for row in range(first, last + 1))


def slot_reader(y1_ref, y2_ref, groups):
    even = lax.axis_index("ty") % 2 == 0

    def read(name, row, q):
        slot = (SOUTH_SLOTS if row < 0 else NORTH_SLOTS)[name, row]
        place = pl.ds((slot * groups + q) * SUB, SUB)
        one, two = y1_ref[place, :], y2_ref[place, :]
        return jnp.where(even, two, one) if row < 0 else jnp.where(even, one, two)

    def counts():
        place = pl.ds(N_SLOTS * groups * SUB, SUB)
        one, two = y1_ref[place, :], y2_ref[place, :]
        return jnp.where(even, two, one), jnp.where(even, one, two)

    return read, counts


def side_reader(x1_ref, x2_ref):
    even = lax.axis_index("core") % 2 == 0

    def read(row):
        place = pl.ds(row * SUB, SUB)
        one, two = x1_ref[place, :], x2_ref[place, :]
        return jnp.where(even, two, one), jnp.where(even, one, two)

    return read


def face_values(t0, t_before, t_after, t_before2):
    return ((t0 + t_before) * 7.0 - (t_after + t_before2)) * (1.0 / 12.0)


def edge_rows(ref, west, east, levels, groups, name):
    own = edges_of_groups([load_rows(ref, q, levels) for q in range(groups)])
    return insert_sides(own, west, east, FIELDS.index(name))


def column_kernel(
    levels, u_ref, v_ref, t_ref, st_ref, su_ref, sv_ref, count_ref, x1_ref, x2_ref, dt_ref, du_ref, edge_ref
):
    groups = group_count(levels)
    read_sides = side_reader(x1_ref, x2_ref)
    numbers = level_numbers(groups)
    zero = jnp.zeros((SUB, LANES), jnp.float32)
    count = count_ref[...].astype(jnp.float32)
    count_west, count_east = read_sides(SUB)
    count_edge = edge_of_tile(count_west, count, count_east)

    def counts(tile):
        return tuple(rows_of((None, part, None), 0, 7) for part in (tile, jnp.minimum(tile, at(tile, -1))))

    def along(level, wet, wet_u, u, t, st):
        cell = (st * -ADVECT).where(wet > level, zero)
        flux = (cell.at(-1) - cell).where(wet_u > level, zero)
        back = u * flux
        face = face_values(t, t.at(-1), t.at(1), t.at(-2))
        return ((back + back.at(1)) * 7.0 - (back.at(-1) + back.at(2))) * (1.0 / 12.0), flux * face

    sides = [read_sides(row) for row in range(SUB)]
    west, east = Many(side[0] for side in sides), Many(side[1] for side in sides)
    u, t, st = (
        edge_rows(ref, west, east, levels, groups, name) for name, ref in (("u", u_ref), ("t", t_ref), ("st", st_ref))
    )
    edge_t, edge_u = (outer_columns(part) for part in along(numbers[groups], *counts(count_edge), u, t, st))
    own = counts(count)
    for q in range(groups):
        st = load_rows(st_ref, q, levels)
        from_x, to_u = along(numbers[q], *own, load_rows(u_ref, q, levels), load_rows(t_ref, q, levels), st)
        store_rows(dt_ref, q, levels, st + merge_edges(from_x, edge_t, q))
        store_rows(du_ref, q, levels, merge_edges(to_u, edge_u, q))
    flow = (u,) + tuple(
        edge_rows(ref, west, east, levels, groups, name) for name, ref in (("v", v_ref), ("su", su_ref), ("sv", sv_ref))
    )
    for n, rows in enumerate(flow):
        for row in range(SUB):
            edge_ref[(n * SUB + row) * SUB : (n * SUB + row + 1) * SUB, :] = rows[row]


def turns(ny):
    first_row = (lax.axis_index("ty") * SUB).astype(jnp.float32)
    scale = 0.5 / (ny * SUB)
    turn_u = Many(0.25 + (first_row + (row + 0.5)) * scale for row in range(-1, 8))
    return turn_u, Many(-0.25 - (first_row + row) * scale for row in range(0, 9))


def prepared(u, v, turn_u, turn_v):
    v_pair, u_pair = v[:-1] + v[1:], u[2:10] + u[1:9]
    return (
        (v_pair + v_pair.at(-1)) * 0.25,
        (u_pair + u_pair.at(1)) * 0.25,
        (u[:-2] - u[2:]) * 0.25 + turn_u,
        (v[1:10].at(-1) - v[1:10].at(1)) * 0.25 + turn_v,
        u[2:10].at(1) - u[2:10].at(-1),
        v[2:10] - v[0:8],
    )


def row_kernel(
    levels, ny, u_ref, v_ref, t_ref, st_ref, count_ref, y1_ref, y2_ref, dtx_ref, dt_hbm, dv_ref, made_ref, edge_ref, dt_ref, sems
):
    groups = group_count(levels)
    read_row, read_counts = slot_reader(y1_ref, y2_ref, groups)
    numbers = level_numbers(groups)
    zero = jnp.zeros((SUB, LANES), jnp.float32)
    count = count_ref[...].astype(jnp.float32)
    count_south, count_north = read_counts()
    counts = rows_of((count_south, count, count_north), -2, 9)
    counts_v = counts[1:].minimum(counts[:-1])
    out = []
    for n, (name, row) in enumerate(OUTER_ROWS):
        (edge,) = edges_of_groups([Many([read_row(name, row, q)]) for q in range(groups)]).items
        edge_ref[n * SUB : (n + 1) * SUB, :] = edge
    for q in range(groups):
        level = numbers[q]

        def rows(name, ref, first, last):
            south = [read_row(name, row, q) for row in range(first, 0)]
            north = [read_row(name, row, q) for row in range(SUB, last + 1)]
            return Many(south + load_rows(ref, q, levels).items + north)

        t, st, v = rows("t", t_ref, -2, 8), rows("st", st_ref, -2, 9), rows("v", v_ref, -1, 9)
        made = prepared(rows("u", u_ref, -2, 8), v, *turns(ny))
        for n, value in enumerate(value for values in made for value in values.items):
            place = pl.ds((q * MADE_ROWS + n) * SUB, SUB)
            made_ref[place, :] = value
        cell = (st * -ADVECT).where(counts > level, zero)
        flux = (cell[:-1] - cell[1:]).where(counts_v > level, zero)
        back = v * flux
        from_y = ((back[1:9] + back[2:10]) * 7.0 - (back[0:8] + back[3:11])) * (1.0 / 12.0)
        to_v = flux[1:9] * face_values(t[2:10], t[1:9], t[3:11], t[0:8])
        store_rows(dt_ref, q, levels, load_rows(dtx_ref, q, levels) + from_y)
        store_rows(dv_ref, q, levels, to_v)
        part = pl.ds(q * SUB * SUB, min(SUB, levels - q * SUB) * SUB)
        out.append(pltpu.make_async_copy(dt_ref.at[part, :], dt_hbm.at[part, :], sems.at[q]))
        out[-1].start()
    for copy in out:
        copy.wait()


def total(value):
    return jnp.sum(value, axis=(0, 1), keepdims=True)


def surface_solve(levels, ny, nx, read, count_ref, face_ref, r_refs, beside_setup, beside_sum):
    groups = group_count(levels)
    lanes, rows = lane_ids(), row_ids()
    numbers = level_numbers(groups)
    zero = jnp.zeros((SUB, LANES), jnp.float32)
    band = max(1, min(ny, BAND_BLOCKS // nx))
    while ny % band:
        band -= 1
    cells = [(dj, i) for dj in range(band) for i in range(nx)]

    def loop(body, init=0):
        if ny * nx <= 32:
            for j in range(0, ny, band):
                init = body(j, init)
            return init
        return lax.fori_loop(0, ny // band, lambda step, carry: body(step * band, carry), init)

    def get(ref, j):
        return Many(ref[j + dj, i] for dj, i in cells)

    def put(ref, j, values):
        for (dj, i), value in zip(cells, values.items):
            ref[j + dj, i] = value

    def beside(values, step):
        return Many(values[dj * nx + min(max(i + step, 0), nx - 1)] for dj, i in cells)

    def below(ref, j, values):
        outside = [ref[max(j - 1, 0) if isinstance(j, int) else jnp.maximum(j - 1, 0), i] for i in range(nx)]
        return Many(outside + values.items[:-nx])

    def above(ref, j, values):
        top = min(j + band, ny - 1) if isinstance(j, int) else jnp.minimum(j + band, ny - 1)
        outside = [ref[top, i] for i in range(nx)]
        return Many(values.items[nx:] + outside)

    def west_of(values):
        return beside(values, -1).where(lanes == LANES - 1, values).rolled(1)

    def east_of(values):
        return beside(values, 1).where(lanes == 0, values).rolled(-1)

    def south_of(ref, j, values):
        return below(ref, j, values).where(rows == SUB - 1, values).apply(lambda a: roll_rows(a, 1))

    def north_of(ref, j, values):
        return above(ref, j, values).where(rows == 0, values).apply(lambda a: roll_rows(a, -1))

    def depth(wet):
        return wet.apply(lambda m: m * (m * (GRAVITY_DT * 0.5 / levels) + GRAVITY_DT * (1.0 - 0.5 / levels)))

    def gather(j, carry):
        put(count_ref, j, Many(read(j + dj, i, 0) for dj, i in cells))
        return carry

    loop(gather)

    def faces(j, carry):
        count = get(count_ref, j)
        wet_u, wet_v = count.minimum(west_of(count)), count.minimum(south_of(count_ref, j, count))
        first_column = [(lanes == 0) if i == 0 else (lanes < 0) for dj, i in cells]
        first_row = [(rows == 0) & (j + dj == 0) for dj, i in cells]
        wet_u = Many([zero] * len(cells)).where(Many(first_column), wet_u)
        wet_v = Many([zero] * len(cells)).where(Many(first_row), wet_v)
        put(face_ref.at[0], j, depth(wet_u))
        put(face_ref.at[1], j, depth(wet_v))
        wet_west = wet_u.apply(lambda a: jnp.broadcast_to(a[:, 0:1], (SUB, LANES)))
        souths = [Many(read(j + dj, i, CHUNK_ROW + q * TILE) for dj, i in cells) for q in range(groups)]
        inside = Many([zero] * len(cells))
        for n in range(levels // WEST_LEVELS + 1):
            reach = jnp.where((lanes & (SUB - 1)) == rows, (lanes >> 3) + n * WEST_LEVELS, levels).astype(jnp.float32)
            west = souths[-1].apply(lambda a: row_of(a, SUB - 1 - levels // WEST_LEVELS + n))
            inside = inside + west.where(wet_west > reach, zero)
        col_u = inside.apply(lambda a: jnp.broadcast_to(jnp.sum(a, axis=1, keepdims=True), (SUB, LANES)))
        put(face_ref.at[4], j, col_u * GRAVITY_DT)
        wet_south = wet_v.apply(lambda a: row_of(a, 0))
        col_v = Many([zero] * len(cells))
        for q in range(groups):
            col_v = col_v + souths[q].where(wet_south > numbers[q], zero)
        col_v = col_v.apply(lambda a: jnp.broadcast_to(jnp.sum(a, axis=0, keepdims=True), (SUB, LANES)))
        put(face_ref.at[5], j, col_v * GRAVITY_DT)
        return carry

    loop(faces)
    beside_setup()

    def start(j, carry):
        load = Many(read(j + dj, i, CHUNK_LOAD) for dj, i in cells)
        col_u, col_v = get(face_ref.at[4], j), get(face_ref.at[5], j)
        depth_u, depth_v = get(face_ref.at[0], j), get(face_ref.at[1], j)
        last_column = Many((lanes == LANES - 1) if i + 1 < nx else (lanes < 0) for dj, i in cells)
        at_end = Many((lanes == LANES - 1) if i + 1 == nx else (lanes < 0) for dj, i in cells)
        last_row = Many((rows == SUB - 1) & (j + dj + 1 < ny) for dj, i in cells)
        at_top = Many((rows == SUB - 1) & (j + dj + 1 == ny) for dj, i in cells)
        none = Many([zero] * len(cells))
        load = load - col_u.where(lanes == 0, zero) - col_v.where(rows == 0, zero)
        load = load + beside(col_u, 1).where(last_column, none) + above(face_ref.at[5], j, col_v).where(last_row, none)
        depth_east = none.where(at_end, east_of(depth_u))
        depth_north = none.where(at_top, north_of(face_ref.at[1], j, depth_v))
        put(face_ref.at[2], j, depth_east)
        put(face_ref.at[3], j, depth_north)
        put(face_ref.at[6], j, (depth_u + depth_east) + (depth_v + depth_north) + 1.0)
        put(r_refs.at[0], j, load)
        return carry

    def gathered(partial, values):
        items = list(values.items)
        while len(items) > 1:
            items = [a + b for a, b in zip(items[::2], items[1::2])] + items[len(items) // 2 * 2 :]
        return partial + items[0]

    loop(start)

    def products(k):
        r_ref = r_refs.at[k]

        def body(j, carry):
            r = get(r_ref, j)
            image = r * get(face_ref.at[6], j) - get(face_ref.at[0], j) * west_of(r) - get(face_ref.at[2], j) * east_of(r)
            image = image - get(face_ref.at[1], j) * south_of(r_ref, j, r)
            image = image - get(face_ref.at[3], j) * north_of(r_ref, j, r)
            put(face_ref.at[4], j, image)
            return gathered(carry[0], r * r), gathered(carry[1], r * image)

        return [total(part) for part in loop(body, (zero, zero))]

    norm, product = products(0)
    beside_sum(0)
    step = norm / product
    steps, ratios = [step], []

    for k in range(ITERS - 1):

        def advance(j, carry):
            image = get(face_ref.at[4], j)
            if k > 0:
                image = image + get(face_ref.at[5], j) * ratio
            if k + 2 < ITERS:
                put(face_ref.at[5], j, image)
            put(r_refs.at[k + 1], j, get(r_refs.at[k], j) - image * step)
            return carry

        loop(advance)
        new, product = products(k + 1)
        beside_sum(k + 1)
        ratio = new / norm
        step = new / (product - ratio * new / step)
        norm = new
        steps.append(step)
        ratios.append(ratio)

    weights = [steps[-1]]
    for k in reversed(range(ITERS - 1)):
        weights.append(steps[k] + ratios[k] * weights[-1])
    weights.reverse()
    return weights


def flow_kernel(
    levels, ny, nx, u_ref, v_ref, su_ref, sv_ref, ga_ref, gb_ref, y1_ref, y2_ref, edge_ref, outer_ref, made_ref, dut_ref, dvt_ref,
    du_hbm, dv_hbm, eta_hbm, count_s, face_s, r_s, eta_ref, du_ref, dv_ref, sems,
):
    groups = group_count(levels)
    lanes, rows_id = lane_ids(), row_ids()
    core = lax.axis_index("core")
    my_j = lax.axis_index("ty")
    my_i = lax.axis_index("y") * 2 + core
    numbers = level_numbers(groups)
    thick = [1.0 + number * (1.0 / levels) for number in numbers]
    read_row, _ = slot_reader(y1_ref, y2_ref, groups)
    zero = jnp.zeros((SUB, LANES), jnp.float32)

    def read(j, i, first):
        where = (j * (nx // 2) + i // 2, slice(None), pl.ds(first, TILE))
        return jnp.where(core == i % 2, ga_ref[where].reshape(SUB, LANES), gb_ref[where].reshape(SUB, LANES))

    def read_corners(n, j, i):
        where = (j * (nx // 2) + i // 2, slice(None), pl.ds(CHUNK_ROW + groups * TILE + n * LANES, LANES))
        row = jnp.broadcast_to(jnp.where(core == i % 2, ga_ref[where], gb_ref[where]), (SUB, LANES))
        return pltpu.roll(row, LANES - SUB + 1, 1, stride=1, stride_axis=0)

    def block(dj, di, get):
        return get(jnp.clip(my_j + dj, 0, ny - 1), jnp.clip(my_i + di, 0, nx - 1))

    def near(dj, di, get):
        j, i = jnp.clip(my_j + dj, 0, ny - 1), jnp.clip(my_i + di, 0, nx - 1)
        inside = (my_j + dj >= 0) & (my_j + dj < ny) & (my_i + di >= 0) & (my_i + di < nx)
        return jnp.where(inside, get(j, i), 0.0)

    diagonal = {"se": (-1, 1), "sw": (-1, -1), "nw": (1, -1), "ne": (1, 1)}
    corner_tiles = {}
    for places in CORNER_PLACES.values():
        for which, value, _ in places:
            n = value // CORNERS_PER_ROW
            if (which, n) not in corner_tiles:
                corner_tiles[which, n] = near(*diagonal[which], functools.partial(read_corners, n))

    def insert_corners(edge, name, row):
        for which, value, target in CORNER_PLACES.get((name, row), ()):
            there = (lanes & (SEG - 1)) == target
            tile = corner_tiles[which, value // CORNERS_PER_ROW]
            edge = jnp.where(there, roll_lanes(tile, target - value % CORNERS_PER_ROW * SUB), edge)
        return edge

    def rows(name, ref, q, first, last):
        south = [read_row(name, row, q) for row in range(first, 0)]
        north = [read_row(name, row, q) for row in range(SUB, last + 1)]
        return Many(south + load_rows(ref, q, levels).items + north)

    def edges(name):
        first, last = FLOW_ROWS[name]
        n = FLOW_FIELDS.index(name)

        def register(row):
            if 0 <= row < SUB:
                return edge_ref[(n * SUB + row) * SUB : (n * SUB + row + 1) * SUB, :]
            place = OUTER_ROWS.index((name, row)) * SUB
            return insert_corners(outer_ref[place : place + SUB, :], name, row)

        return Many(register(row) for row in range(first, last + 1))

    refs = {"u": u_ref, "v": v_ref, "su": su_ref, "sv": sv_ref}
    data, made = {}, {}

    def prepare(part):
        if part == groups:
            data[part] = [edges(name) for name in FLOW_FIELDS]
            made[part] = prepared(*data[part][:2], *turns(ny))
            return
        data[part] = [rows(name, refs[name], part, *FLOW_ROWS[name]) for name in FLOW_FIELDS]
        made[part], n = [], part * MADE_ROWS
        for size in MADE_SIZES:
            made[part].append(Many(made_ref[k * SUB : (k + 1) * SUB, :] for k in range(n, n + size)))
            n += size

    def pairs(get, operation):
        tiles = [[get(dj, di) for di in (-1, 0, 1)] for dj in (-1, 0, 1)]
        out = []
        for south, own, north in ([row[1] for row in tiles], [edge_of_tile(*row) for row in tiles]):
            outer = jnp.where(rows_id == SUB - 1, south, north)
            below = roll_rows(jnp.where(rows_id == SUB - 1, south, own), 1)
            below_outer = roll_rows(jnp.where(rows_id == SUB - 2, south, own), 1)
            out.append(
                (operation(own, at(own, -1)), operation(outer, at(outer, -1)), operation(own, below), operation(outer, below_outer))
            )
        return out

    def outer_and_own(own, outer):
        return Many([row_of(outer, SUB - 1)] + [row_of(own, row) for row in range(SUB)] + [row_of(outer, 0)])

    wet_counts, differences = [], []

    def beside_setup():
        wet_counts.extend(pairs(lambda dj, di: near(dj, di, lambda j, i: count_s[j, i]), jnp.minimum))

    def beside_sum(k):
        if k == ITERS - 1:
            prepare(groups)
        differences.append(pairs(lambda dj, di: block(dj, di, lambda j, i: r_s[k, j, i]), lambda a, b: a - b))

    weights = surface_solve(levels, ny, nx, read, count_s, face_s, r_s, beside_setup, beside_sum)

    def weighted(parts):
        total_of = parts[0] * weights[0]
        for part, weight in zip(parts[1:], weights[1:]):
            total_of = total_of + part * weight
        return total_of

    slopes = [[weighted([d[kind][n] for d in differences]) for n in range(4)] for kind in range(2)]
    eta_ref[...] = weighted([r_s[k, my_j, my_i] for k in range(ITERS)])
    out = [pltpu.make_async_copy(eta_ref, eta_hbm, sems.at[0])]
    out[0].start()

    def adjoint(parts):
        u, v, su, sv = (joined([data[part][n] for part in parts]) for n in range(4))
        v_bar, u_bar, from_v_bar, from_u_bar, u_across, v_across = (
            joined([made[part][n] for part in parts]) for n in range(len(MADE_SIZES))
        )

        def each(values):
            return Many([values[part] for part in parts for _ in range(SUB + 2)], len(parts))

        def around(of, n):
            return joined([outer_and_own(*of[1 if part == groups else 0][n : n + 2]) for part in parts])

        wet_u, wet_v = around(wet_counts, 0) > each(numbers), around(wet_counts, 2) > each(numbers)
        u_cot = su + (around(slopes, 0) * each(thick)).where(wet_u, zero)
        v_cot = sv + (around(slopes, 2) * each(thick)).where(wet_v, zero)
        a, b = (u_cot * (0.5 * ADVECT)).where(wet_u, zero), (v_cot * (0.5 * ADVECT)).where(wet_v, zero)
        av, bu = a * v_bar, b[1:9] * u_bar
        au, bv = a[1:9] * u[2:10], b * v[:-1]
        to_v_bar, to_u_bar = a[:-1] * from_v_bar, b[1:] * from_u_bar
        near_u, near_v = to_u_bar[:-1] + to_u_bar[1:], to_v_bar[1:] + to_v_bar[:-1]
        du = u_cot[1:9] - a[1:9] * u_across + av[2:] - av[:-2] + near_u
        du = du + au.at(1) + (near_u - au).at(-1)
        dv = v_cot[1:9] - b[1:9] * v_across + bv[2:] - bv[:-2] + near_v
        dv = dv + (near_v + bu).at(1) - bu.at(-1)
        return list(zip(du.split(), dv.split()))

    for part in range(groups):
        prepare(part)
    flow = {}
    for parts in ADJOINT_PARTS:
        flow.update(zip(parts, adjoint(parts)))
    edge_u, edge_v = (outer_columns(part) for part in flow[groups])
    for q in range(groups):
        du, dv = flow[q]
        store_rows(du_ref, q, levels, merge_edges(du, edge_u, q) + load_rows(dut_ref, q, levels))
        store_rows(dv_ref, q, levels, merge_edges(dv, edge_v, q) + load_rows(dvt_ref, q, levels))
        part = pl.ds(q * SUB * SUB, min(SUB, levels - q * SUB) * SUB)
        for target, source in ((du_hbm, du_ref), (dv_hbm, dv_ref)):
            out.append(pltpu.make_async_copy(source.at[part, :], target.at[part, :], sems.at[len(out)]))
            out[-1].start()
    for copy in out:
        copy.wait()


def swaps(mesh_shape, along, parity):
    ny, nx = mesh_shape
    pairs = []
    for j in range(ny):
        for i in range(nx):
            k, size = (j, ny) if along == "y" else (i, nx)
            other = k + 1 if k % 2 == parity else k - 1
            if 0 <= other < size:
                pairs.append((j * nx + i, other * nx + i if along == "y" else j * nx + other))
    return pairs


def call(kernel, outs, args, scratch=(), flops=0, size=0, far_in=False, far_out=(), limit=48):
    near, far = pl.BlockSpec(memory_space=pltpu.VMEM), pl.BlockSpec(memory_space=pltpu.HBM)
    outs = [out if isinstance(out, jax.ShapeDtypeStruct) else jax.ShapeDtypeStruct(out, jnp.float32) for out in outs]
    return pl.pallas_call(
        kernel,
        out_shape=outs,
        in_specs=[far if far_in else near] * len(args),
        out_specs=[far if n in far_out else near for n in range(len(outs))],
        scratch_shapes=list(scratch),
        compiler_params=pltpu.CompilerParams(vmem_limit_bytes=limit * 1024 * 1024),
        cost_estimate=pl.CostEstimate(flops=flops, bytes_accessed=size, transcendentals=0),
    )(*args)


def on_device(shape, u, v, t, count, su, sv, st, elev):
    ny, nx = shape
    levels = u.shape[0]
    groups = group_count(levels)
    flat = (levels * SUB, LANES)
    u, v, t, su, sv, st = (field.reshape(flat) for field in (u, v, t, su, sv, st))
    peers = ny * nx // 2
    row_packet = ((N_SLOTS * groups + 1) * SUB, LANES)
    column_packet = ((SUB + 1) * SUB, LANES)
    chunk = (peers, 1, CHUNK_ROW + groups * TILE + len(CORNERS) // CORNERS_PER_ROW * LANES)
    tile = (SUB, LANES)
    (chunks,) = call(
        functools.partial(chunk_kernel, levels, peers),
        [chunk],
        (u, v, su, sv, count, elev),
        scratch=[pltpu.VMEM(flat, jnp.float32)] * 4
        + [pltpu.VMEM(tile, count.dtype), pltpu.VMEM(tile, jnp.float32), pltpu.SemaphoreType.DMA((6,))],
        flops=1 << 20,
        size=1 << 21,
        far_in=True,
        limit=60,
    )
    y1, y2, xp = call(
        functools.partial(packet_kernel, levels),
        [row_packet, row_packet, column_packet],
        (u, v, t, su, sv, st, count),
        flops=1 << 20,
        size=1 << 21,
    )
    axes = ("ty", "y", "core")
    ga = lax.all_to_all(chunks, ("ty", "y"), 0, 0)
    x1 = lax.ppermute(xp, axes, swaps(shape, "x", 0))
    x2 = lax.ppermute(xp, axes, swaps(shape, "x", 1))
    y1 = lax.ppermute(y1, axes, swaps(shape, "y", 0))
    y2 = lax.ppermute(y2, axes, swaps(shape, "y", 1))
    dtx, du_t, edge = call(
        functools.partial(column_kernel, levels),
        [flat, flat, (len(FLOW_FIELDS) * SUB * SUB, LANES)],
        (u, v, t, st, su, sv, count, x1, x2),
        flops=1 << 22,
        size=1 << 21,
    )
    ga, y1, y2, dtx = lax.optimization_barrier((ga, y1, y2, dtx))
    gb = lax.ppermute(ga, axes, swaps(shape, "x", 0))
    dt, dv_t, made, outer = call(
        functools.partial(row_kernel, levels, ny),
        [flat, flat, (groups * MADE_ROWS * SUB, LANES), (len(OUTER_ROWS) * SUB, LANES)],
        (u, v, t, st, count, y1, y2, dtx),
        scratch=(pltpu.VMEM(flat, jnp.float32), pltpu.SemaphoreType.DMA((groups,))),
        flops=1 << 22,
        size=1 << 21,
        far_out=(0,),
    )
    grid = pltpu.VMEM((ny, nx, SUB, LANES), jnp.float32)
    faces, residuals = (pltpu.VMEM((n, ny, nx, SUB, LANES), jnp.float32) for n in (7, ITERS))
    du, dv, eta = call(
        functools.partial(flow_kernel, levels, ny, nx),
        [flat, flat, (SUB, LANES)],
        (u, v, su, sv, ga, gb, y1, y2, edge, outer, made, du_t, dv_t),
        far_out=(0, 1, 2),
        scratch=(grid, faces, residuals)
        + tuple(pltpu.VMEM(shape, jnp.float32) for shape in (tile, flat, flat))
        + (pltpu.SemaphoreType.DMA((2 * groups + 1,)),),
        flops=1 << 23,
        size=1 << 22,
    )
    whole = (levels, SUB, LANES)
    return du.reshape(whole), dv.reshape(whole), dt.reshape(whole), eta


def solution(mesh):
    ny, nx = mesh.shape["ty"], mesh.shape["tx"]
    split = Mesh(mesh.devices.reshape(ny, nx // 2, 2), ("ty", "y", "core"))
    deep, flat = P(None, "ty", ("y", "core")), P("ty", ("y", "core"))
    return jax.shard_map(
        functools.partial(on_device, (ny, nx)),
        mesh=split,
        in_specs=(deep, deep, deep, flat, deep, deep, deep, flat),
        out_specs=(deep, deep, deep, flat),
        check_vma=False,
    )
```

```python
import functools

import jax
import jax.numpy as jnp
from jax import lax
from jax.experimental import pallas as pl
from jax.experimental.pallas import tpu as pltpu
from jax.sharding import Mesh, PartitionSpec as P

ITERS = 4
ADVECT = 0.1
GRAVITY_DT = 0.1

SUB = 8
LANES = 128
SEG = 32
FIELDS = ("u", "v", "t", "st", "su", "sv")
BAND_BLOCKS = 32
ADJOINT_PARTS = ((4, 0), (1, 2), (3,))
FLOW_FIELDS = ("u", "v", "su", "sv")
FLOW_ROWS = {"u": (-2, 8), "v": (-1, 9), "su": (-1, 8), "sv": (-1, 8)}
OUTER_ROWS = tuple((n, r) for n in FLOW_FIELDS for r in range(FLOW_ROWS[n][0], FLOW_ROWS[n][1] + 1) if not 0 <= r < 8)
MADE_SIZES = (10, 8, 9, 9, 8, 8)
MADE_ROWS = sum(MADE_SIZES)
SOUTH_SLOTS = {("u", -2): 0, ("u", -1): 1, ("v", -1): 2, ("t", -2): 3, ("t", -1): 4, ("st", -2): 5, ("st", -1): 6}
SOUTH_SLOTS.update({("su", -1): 7, ("sv", -1): 8})
NORTH_SLOTS = {("u", 8): 0, ("v", 8): 1, ("v", 9): 2, ("t", 8): 3, ("st", 8): 5, ("st", 9): 6, ("su", 8): 7, ("sv", 8): 8}
N_SLOTS = 9
TILE = SUB * LANES
CHUNK_LOAD = TILE
CHUNK_ROW = 2 * TILE
WEST_LEVELS = LANES // SUB
CORNERS_PER_ROW = 4
CORNERS = (("u", 6, 0), ("u", 7, 0), ("u", 7, 1), ("su", 7, 0), ("v", 7, 127), ("u", 7, 127))
CORNERS += (("v", 0, 127), ("v", 1, 127), ("v", 0, 126), ("sv", 0, 127), ("v", 0, 0), ("u", 0, 0))
CORNER_PLACES = {
    ("u", -2): (("se", 0, 24),),
    ("u", -1): (("se", 1, 24), ("se", 2, 25), ("sw", 5, 7)),
    ("su", -1): (("se", 3, 24),),
    ("v", -1): (("sw", 4, 7),),
    ("v", 8): (("nw", 6, 7), ("nw", 8, 6), ("ne", 10, 24)),
    ("u", 8): (("ne", 11, 24),),
    ("v", 9): (("nw", 7, 7),),
    ("sv", 8): (("nw", 9, 7),),
}


def lane_ids():
    return lax.broadcasted_iota(jnp.int32, (SUB, LANES), 1)


def row_ids():
    return lax.broadcasted_iota(jnp.int32, (SUB, LANES), 0)


def roll_lanes(value, amount):
    amount %= LANES
    return value if amount == 0 else pltpu.roll(value, amount, 1)


def roll_rows(value, amount):
    amount %= SUB
    return value if amount == 0 else pltpu.roll(value, amount, 0)


def at(value, shift):
    return roll_lanes(value, -shift)


def row_of(tile, row):
    return jnp.broadcast_to(tile[row : row + 1, :], (SUB, LANES))


def group_count(levels):
    return -(-levels // SUB)


def load_group(ref, row, q, levels):
    first = min(q * SUB, levels - SUB)
    value = ref[pl.ds(first * SUB + row, SUB, stride=SUB), :]
    return roll_rows(value, first - q * SUB)


def store_group(ref, row, q, levels, value):
    count = min(SUB, levels - q * SUB)
    ref[pl.ds(q * SUB * SUB + row, count, stride=SUB), :] = value[:count]


def level_numbers(groups):
    rows = row_ids()
    numbers = [(rows + q * SUB).astype(jnp.float32) for q in range(groups)]
    return numbers + [(rows + (lane_ids() >> 5) * SUB).astype(jnp.float32)]


def edge_of_tile(west, centre, east):
    lanes = lane_ids()
    out = jnp.where(lanes < 8, roll_lanes(west, 8), roll_lanes(centre, 8))
    out = jnp.where(lanes >= 16, roll_lanes(centre, 24), out)
    out = jnp.where(lanes >= 24, roll_lanes(east, 24), out)
    out = jnp.where(lanes < SEG, out, roll_lanes(out, SEG))
    return jnp.where(lanes < 2 * SEG, out, roll_lanes(out, 2 * SEG))


def chunk_kernel(
    levels, peers, u_hbm, v_hbm, su_hbm, sv_hbm, count_hbm, elev_hbm, chunk_ref,
    u_ref, v_ref, su_ref, sv_ref, count_ref, elev_ref, sems,
):
    pairs = (
        (count_hbm, count_ref), (su_hbm, su_ref), (sv_hbm, sv_ref), (elev_hbm, elev_ref), (u_hbm, u_ref), (v_hbm, v_ref),
    )
    copies = [pltpu.make_async_copy(source, target, sems.at[n]) for n, (source, target) in enumerate(pairs)]
    for copy in copies:
        copy.start()
    groups = group_count(levels)
    lanes, rows = lane_ids(), row_ids()
    refs = {"u": u_ref, "v": v_ref, "su": su_ref, "sv": sv_ref}
    for copy in copies[:4]:
        copy.wait()
    count = count_ref[...].astype(jnp.float32)
    zero = jnp.zeros((SUB, LANES), jnp.float32)

    wet_u = jnp.where(lanes == 0, 0.0, jnp.minimum(count, roll_lanes(count, 1)))
    wet_v = jnp.where(rows == 0, 0.0, jnp.minimum(count, roll_rows(count, 1)))
    col_u, col_v = [zero] * 4, [zero] * 4
    west = [zero] * (levels // WEST_LEVELS + 1)
    for k in range(levels):
        su_level = su_ref[k * SUB : (k + 1) * SUB, :]
        col_u[k % 4] = col_u[k % 4] + jnp.where(wet_u > float(k), su_level, 0.0)
        col_v[k % 4] = col_v[k % 4] + jnp.where(wet_v > float(k), sv_ref[k * SUB : (k + 1) * SUB, :], 0.0)
        n = k // WEST_LEVELS
        there = lanes == rows + k % WEST_LEVELS * SUB
        west[n] = jnp.where(there, jnp.broadcast_to(su_level[:, 0:1], (SUB, LANES)), west[n])
    col_u, col_v = ((col[0] + col[1]) + (col[2] + col[3]) for col in (col_u, col_v))
    load = elev_ref[...] + GRAVITY_DT * (at(col_u, 1) - col_u + roll_rows(col_v, -1) - col_v)

    for copy in copies[4:]:
        copy.wait()
    corners = [zero] * (len(CORNERS) // CORNERS_PER_ROW)
    for place, (name, row, column) in enumerate(CORNERS):
        n, base = place // CORNERS_PER_ROW, place % CORNERS_PER_ROW * SUB
        for q in range(groups):
            value = load_group(refs[name], row, q, levels)[:, column : column + 1]
            there = lanes == SEG * q + base + SUB - 1 - rows
            corners[n] = jnp.where(there, jnp.broadcast_to(value, (SUB, LANES)), corners[n])

    def in_a_row(tile):
        return jnp.broadcast_to(jnp.sum(tile, axis=0, keepdims=True), (SUB, LANES))

    tiles = [count, load] + [load_group(sv_ref, 0, q, levels) for q in range(groups)]
    for n, part in enumerate(west):
        tiles[-1] = jnp.where(rows == SUB - len(west) + n, in_a_row(part), tiles[-1])
    last = zero
    for n, part in enumerate(corners):
        last = jnp.where(rows == n, in_a_row(part), last)
    tiles = [tile.reshape(1, TILE) for tile in tiles + [last]]
    tiles[-1] = tiles[-1][:, : len(corners) * LANES]

    def put(peer, carry):
        first = 0
        for tile in tiles:
            chunk_ref[peer, :, first : first + tile.shape[1]] = tile
            first += tile.shape[1]
        return carry

    lax.fori_loop(0, peers, put, 0, unroll=4)


def packet_kernel(levels, u_ref, v_ref, t_ref, su_ref, sv_ref, st_ref, count_ref, y1_ref, y2_ref, x_ref):
    groups = group_count(levels)
    lanes = lane_ids()
    zero = jnp.zeros((SUB, LANES), jnp.float32)
    count = count_ref[...].astype(jnp.float32)
    even = lax.axis_index("ty") % 2 == 0
    refs = {"u": u_ref, "v": v_ref, "t": t_ref, "st": st_ref, "su": su_ref, "sv": sv_ref}
    loaded = {}
    for name in FIELDS:
        for row in range(SUB):
            for q in range(groups):
                loaded[name, row, q] = load_group(refs[name], row, q, levels)

    for slot in range(N_SLOTS):
        upper = [(name, row + SUB) for (name, row), place in SOUTH_SLOTS.items() if place == slot]
        lower = [(name, row - SUB) for (name, row), place in NORTH_SLOTS.items() if place == slot]
        for q in range(groups):
            to_north = loaded[(*upper[0], q)]
            to_south = loaded[(*lower[0], q)] if lower else zero
            place = pl.ds((slot * groups + q) * SUB, SUB)
            y1_ref[place, :] = jnp.where(even, to_north, to_south)
            y2_ref[place, :] = jnp.where(even, to_south, to_north)
    y1_ref[N_SLOTS * groups * SUB :, :] = count
    y2_ref[N_SLOTS * groups * SUB :, :] = count

    for row in range(SUB):
        packet = zero
        for field, name in enumerate(FIELDS):
            for q in range(groups):
                lane = SEG * q + 4 * field
                packet = jnp.where((lanes >= lane) & (lanes < lane + 4), roll_lanes(loaded[name, row, q], lane + 2), packet)
        x_ref[row * SUB : (row + 1) * SUB, :] = packet
    x_ref[SUB * SUB :, :] = count


def joined(parts):
    return Many([item for part in parts for item in part.items], len(parts))


class Many:
    def __init__(self, items, parts=1):
        self.items = list(items)
        self.parts = parts

    def __getitem__(self, where):
        if not isinstance(where, slice):
            return self.items[where]
        rows = len(self.items) // self.parts
        return Many([item for n in range(self.parts) for item in self.items[n * rows : (n + 1) * rows][where]], self.parts)

    def __len__(self):
        return len(self.items)

    def split(self):
        rows = len(self.items) // self.parts
        return [Many(self.items[n * rows : (n + 1) * rows]) for n in range(self.parts)]

    def apply(self, operation, *others):
        others = [other.items if isinstance(other, Many) else [other] * len(self) for other in others]
        assert all(len(other) == len(self) for other in others)
        return Many([operation(*parts) for parts in zip(self.items, *others)], self.parts)

    def __add__(self, other):
        return self.apply(lambda a, b: a + b, other)

    def __sub__(self, other):
        return self.apply(lambda a, b: a - b, other)

    def __mul__(self, other):
        return self.apply(lambda a, b: a * b, other)

    def __gt__(self, other):
        return self.apply(lambda a, b: a > b, other)

    def at(self, shift):
        return self.apply(lambda a: at(a, shift))

    def rolled(self, amount):
        return self.apply(lambda a: roll_lanes(a, amount))

    def minimum(self, other):
        return self.apply(jnp.minimum, other)

    def where(self, mask, other):
        return self.apply(lambda a, m, b: jnp.where(m, a, b), mask, other)


def edges_of_groups(parts):
    lanes = lane_ids()
    out = parts[0].rolled(8)
    for q in range(1, len(parts)):
        out = parts[q].rolled(SEG * q + 8).where(lanes >= SEG * q, out)
    return out.rolled(16).where((lanes & (SEG - 1)) >= 16, out)


def insert_sides(edge, west, east, field):
    place = lane_ids() & (SEG - 1)
    edge = west.rolled(6 - 4 * field).where((place == 6) | (place == 7), edge)
    return east.rolled(22 - 4 * field).where((place == 24) | (place == 25), edge)


def outer_columns(edge):
    return edge.rolled(-16).where((lane_ids() & (SEG - 1)) < 8, edge)


def merge_edges(values, outer, q):
    lanes = lane_ids()
    return outer.rolled(-(SEG * q + 8)).where((lanes < 2) | (lanes >= LANES - 2), values)


def load_rows(ref, q, levels):
    return Many(load_group(ref, row, q, levels) for row in range(SUB))


def store_rows(ref, q, levels, values):
    for row in range(SUB):
        store_group(ref, row, q, levels, values[row])


def rows_of(tiles, first, last):
    return Many(row_of(tiles[row // SUB + 1], row % SUB) for row in range(first, last + 1))


def slot_reader(y1_ref, y2_ref, groups):
    even = lax.axis_index("ty") % 2 == 0

    def read(name, row, q):
        slot = (SOUTH_SLOTS if row < 0 else NORTH_SLOTS)[name, row]
        place = pl.ds((slot * groups + q) * SUB, SUB)
        one, two = y1_ref[place, :], y2_ref[place, :]
        return jnp.where(even, two, one) if row < 0 else jnp.where(even, one, two)

    def counts():
        place = pl.ds(N_SLOTS * groups * SUB, SUB)
        one, two = y1_ref[place, :], y2_ref[place, :]
        return jnp.where(even, two, one), jnp.where(even, one, two)

    return read, counts


def side_reader(x1_ref, x2_ref):
    even = lax.axis_index("core") % 2 == 0

    def read(row):
        place = pl.ds(row * SUB, SUB)
        one, two = x1_ref[place, :], x2_ref[place, :]
        return jnp.where(even, two, one), jnp.where(even, one, two)

    return read


def face_values(t0, t_before, t_after, t_before2):
    return ((t0 + t_before) * 7.0 - (t_after + t_before2)) * (1.0 / 12.0)


def edge_rows(ref, west, east, levels, groups, name):
    own = edges_of_groups([load_rows(ref, q, levels) for q in range(groups)])
    return insert_sides(own, west, east, FIELDS.index(name))


def column_kernel(
    levels, u_ref, v_ref, t_ref, st_ref, su_ref, sv_ref, count_ref, x1_ref, x2_ref, dt_ref, du_ref, edge_ref
):
    groups = group_count(levels)
    read_sides = side_reader(x1_ref, x2_ref)
    numbers = level_numbers(groups)
    zero = jnp.zeros((SUB, LANES), jnp.float32)
    count = count_ref[...].astype(jnp.float32)
    count_west, count_east = read_sides(SUB)
    count_edge = edge_of_tile(count_west, count, count_east)

    def counts(tile):
        return tuple(rows_of((None, part, None), 0, 7) for part in (tile, jnp.minimum(tile, at(tile, -1))))

    def along(level, wet, wet_u, u, t, st):
        cell = (st * -ADVECT).where(wet > level, zero)
        flux = (cell.at(-1) - cell).where(wet_u > level, zero)
        back = u * flux
        face = face_values(t, t.at(-1), t.at(1), t.at(-2))
        return ((back + back.at(1)) * 7.0 - (back.at(-1) + back.at(2))) * (1.0 / 12.0), flux * face

    sides = [read_sides(row) for row in range(SUB)]
    west, east = Many(side[0] for side in sides), Many(side[1] for side in sides)
    u, t, st = (
        edge_rows(ref, west, east, levels, groups, name) for name, ref in (("u", u_ref), ("t", t_ref), ("st", st_ref))
    )
    edge_t, edge_u = (outer_columns(part) for part in along(numbers[groups], *counts(count_edge), u, t, st))
    own = counts(count)
    for q in range(groups):
        st = load_rows(st_ref, q, levels)
        from_x, to_u = along(numbers[q], *own, load_rows(u_ref, q, levels), load_rows(t_ref, q, levels), st)
        store_rows(dt_ref, q, levels, st + merge_edges(from_x, edge_t, q))
        store_rows(du_ref, q, levels, merge_edges(to_u, edge_u, q))
    flow = (u,) + tuple(
        edge_rows(ref, west, east, levels, groups, name) for name, ref in (("v", v_ref), ("su", su_ref), ("sv", sv_ref))
    )
    for n, rows in enumerate(flow):
        for row in range(SUB):
            edge_ref[(n * SUB + row) * SUB : (n * SUB + row + 1) * SUB, :] = rows[row]


def turns(ny):
    first_row = (lax.axis_index("ty") * SUB).astype(jnp.float32)
    scale = 0.5 / (ny * SUB)
    turn_u = Many(0.25 + (first_row + (row + 0.5)) * scale for row in range(-1, 8))
    return turn_u, Many(-0.25 - (first_row + row) * scale for row in range(0, 9))


def prepared(u, v, turn_u, turn_v):
    v_pair, u_pair = v[:-1] + v[1:], u[2:10] + u[1:9]
    return (
        (v_pair + v_pair.at(-1)) * 0.25,
        (u_pair + u_pair.at(1)) * 0.25,
        (u[:-2] - u[2:]) * 0.25 + turn_u,
        (v[1:10].at(-1) - v[1:10].at(1)) * 0.25 + turn_v,
        u[2:10].at(1) - u[2:10].at(-1),
        v[2:10] - v[0:8],
    )


def row_kernel(
    levels, ny, u_ref, v_ref, t_ref, st_ref, count_ref, y1_ref, y2_ref, dtx_ref, dt_hbm, dv_ref, made_ref, edge_ref, dt_ref, sems
):
    groups = group_count(levels)
    read_row, read_counts = slot_reader(y1_ref, y2_ref, groups)
    numbers = level_numbers(groups)
    zero = jnp.zeros((SUB, LANES), jnp.float32)
    count = count_ref[...].astype(jnp.float32)
    count_south, count_north = read_counts()
    counts = rows_of((count_south, count, count_north), -2, 9)
    counts_v = counts[1:].minimum(counts[:-1])
    out = []
    for n, (name, row) in enumerate(OUTER_ROWS):
        (edge,) = edges_of_groups([Many([read_row(name, row, q)]) for q in range(groups)]).items
        edge_ref[n * SUB : (n + 1) * SUB, :] = edge
    for q in range(groups):
        level = numbers[q]

        def rows(name, ref, first, last):
            south = [read_row(name, row, q) for row in range(first, 0)]
            north = [read_row(name, row, q) for row in range(SUB, last + 1)]
            return Many(south + load_rows(ref, q, levels).items + north)

        t, st, v = rows("t", t_ref, -2, 8), rows("st", st_ref, -2, 9), rows("v", v_ref, -1, 9)
        made = prepared(rows("u", u_ref, -2, 8), v, *turns(ny))
        for n, value in enumerate(value for values in made for value in values.items):
            place = pl.ds((q * MADE_ROWS + n) * SUB, SUB)
            made_ref[place, :] = value
        cell = (st * -ADVECT).where(counts > level, zero)
        flux = (cell[:-1] - cell[1:]).where(counts_v > level, zero)
        back = v * flux
        from_y = ((back[1:9] + back[2:10]) * 7.0 - (back[0:8] + back[3:11])) * (1.0 / 12.0)
        to_v = flux[1:9] * face_values(t[2:10], t[1:9], t[3:11], t[0:8])
        store_rows(dt_ref, q, levels, load_rows(dtx_ref, q, levels) + from_y)
        store_rows(dv_ref, q, levels, to_v)
        part = pl.ds(q * SUB * SUB, min(SUB, levels - q * SUB) * SUB)
        out.append(pltpu.make_async_copy(dt_ref.at[part, :], dt_hbm.at[part, :], sems.at[q]))
        out[-1].start()
    for copy in out:
        copy.wait()


def total(value):
    return jnp.sum(value, axis=(0, 1), keepdims=True)


def surface_solve(levels, ny, nx, read, count_ref, face_ref, r_refs, beside_setup, beside_sum):
    groups = group_count(levels)
    lanes, rows = lane_ids(), row_ids()
    numbers = level_numbers(groups)
    zero = jnp.zeros((SUB, LANES), jnp.float32)
    band = max(1, min(ny, BAND_BLOCKS // nx))
    while ny % band:
        band -= 1
    cells = [(dj, i) for dj in range(band) for i in range(nx)]

    def loop(body, init=0):
        if ny * nx <= 32:
            for j in range(0, ny, band):
                init = body(j, init)
            return init
        return lax.fori_loop(0, ny // band, lambda step, carry: body(step * band, carry), init)

    def get(ref, j):
        return Many(ref[j + dj, i] for dj, i in cells)

    def put(ref, j, values):
        for (dj, i), value in zip(cells, values.items):
            ref[j + dj, i] = value

    def beside(values, step):
        return Many(values[dj * nx + min(max(i + step, 0), nx - 1)] for dj, i in cells)

    def below(ref, j, values):
        outside = [ref[max(j - 1, 0) if isinstance(j, int) else jnp.maximum(j - 1, 0), i] for i in range(nx)]
        return Many(outside + values.items[:-nx])

    def above(ref, j, values):
        top = min(j + band, ny - 1) if isinstance(j, int) else jnp.minimum(j + band, ny - 1)
        outside = [ref[top, i] for i in range(nx)]
        return Many(values.items[nx:] + outside)

    def west_of(values):
        return beside(values, -1).where(lanes == LANES - 1, values).rolled(1)

    def east_of(values):
        return beside(values, 1).where(lanes == 0, values).rolled(-1)

    def south_of(ref, j, values):
        return below(ref, j, values).where(rows == SUB - 1, values).apply(lambda a: roll_rows(a, 1))

    def north_of(ref, j, values):
        return above(ref, j, values).where(rows == 0, values).apply(lambda a: roll_rows(a, -1))

    def depth(wet):
        return wet.apply(lambda m: m * (m * (GRAVITY_DT * 0.5 / levels) + GRAVITY_DT * (1.0 - 0.5 / levels)))

    def gather(j, carry):
        put(count_ref, j, Many(read(j + dj, i, 0) for dj, i in cells))
        return carry

    loop(gather)

    def faces(j, carry):
        count = get(count_ref, j)
        wet_u, wet_v = count.minimum(west_of(count)), count.minimum(south_of(count_ref, j, count))
        first_column = [(lanes == 0) if i == 0 else (lanes < 0) for dj, i in cells]
        first_row = [(rows == 0) & (j + dj == 0) for dj, i in cells]
        wet_u = Many([zero] * len(cells)).where(Many(first_column), wet_u)
        wet_v = Many([zero] * len(cells)).where(Many(first_row), wet_v)
        put(face_ref.at[0], j, depth(wet_u))
        put(face_ref.at[1], j, depth(wet_v))
        wet_west = wet_u.apply(lambda a: jnp.broadcast_to(a[:, 0:1], (SUB, LANES)))
        souths = [Many(read(j + dj, i, CHUNK_ROW + q * TILE) for dj, i in cells) for q in range(groups)]
        inside = Many([zero] * len(cells))
        for n in range(levels // WEST_LEVELS + 1):
            reach = jnp.where((lanes & (SUB - 1)) == rows, (lanes >> 3) + n * WEST_LEVELS, levels).astype(jnp.float32)
            west = souths[-1].apply(lambda a: row_of(a, SUB - 1 - levels // WEST_LEVELS + n))
            inside = inside + west.where(wet_west > reach, zero)
        col_u = inside.apply(lambda a: jnp.broadcast_to(jnp.sum(a, axis=1, keepdims=True), (SUB, LANES)))
        put(face_ref.at[4], j, col_u * GRAVITY_DT)
        wet_south = wet_v.apply(lambda a: row_of(a, 0))
        col_v = Many([zero] * len(cells))
        for q in range(groups):
            col_v = col_v + souths[q].where(wet_south > numbers[q], zero)
        col_v = col_v.apply(lambda a: jnp.broadcast_to(jnp.sum(a, axis=0, keepdims=True), (SUB, LANES)))
        put(face_ref.at[5], j, col_v * GRAVITY_DT)
        return carry

    loop(faces)
    beside_setup()

    def start(j, carry):
        load = Many(read(j + dj, i, CHUNK_LOAD) for dj, i in cells)
        col_u, col_v = get(face_ref.at[4], j), get(face_ref.at[5], j)
        depth_u, depth_v = get(face_ref.at[0], j), get(face_ref.at[1], j)
        last_column = Many((lanes == LANES - 1) if i + 1 < nx else (lanes < 0) for dj, i in cells)
        at_end = Many((lanes == LANES - 1) if i + 1 == nx else (lanes < 0) for dj, i in cells)
        last_row = Many((rows == SUB - 1) & (j + dj + 1 < ny) for dj, i in cells)
        at_top = Many((rows == SUB - 1) & (j + dj + 1 == ny) for dj, i in cells)
        none = Many([zero] * len(cells))
        load = load - col_u.where(lanes == 0, zero) - col_v.where(rows == 0, zero)
        load = load + beside(col_u, 1).where(last_column, none) + above(face_ref.at[5], j, col_v).where(last_row, none)
        depth_east = none.where(at_end, east_of(depth_u))
        depth_north = none.where(at_top, north_of(face_ref.at[1], j, depth_v))
        put(face_ref.at[2], j, depth_east)
        put(face_ref.at[3], j, depth_north)
        put(face_ref.at[6], j, (depth_u + depth_east) + (depth_v + depth_north) + 1.0)
        put(r_refs.at[0], j, load)
        return carry

    def gathered(partial, values):
        items = list(values.items)
        while len(items) > 1:
            items = [a + b for a, b in zip(items[::2], items[1::2])] + items[len(items) // 2 * 2 :]
        return partial + items[0]

    loop(start)

    def products(k):
        r_ref = r_refs.at[k]

        def body(j, carry):
            r = get(r_ref, j)
            image = r * get(face_ref.at[6], j) - get(face_ref.at[0], j) * west_of(r) - get(face_ref.at[2], j) * east_of(r)
            image = image - get(face_ref.at[1], j) * south_of(r_ref, j, r)
            image = image - get(face_ref.at[3], j) * north_of(r_ref, j, r)
            put(face_ref.at[4], j, image)
            return gathered(carry[0], r * r), gathered(carry[1], r * image)

        return [total(part) for part in loop(body, (zero, zero))]

    norm, product = products(0)
    beside_sum(0)
    step = norm / product
    steps, ratios = [step], []

    for k in range(ITERS - 1):

        def advance(j, carry):
            image = get(face_ref.at[4], j)
            if k > 0:
                image = image + get(face_ref.at[5], j) * ratio
            if k + 2 < ITERS:
                put(face_ref.at[5], j, image)
            put(r_refs.at[k + 1], j, get(r_refs.at[k], j) - image * step)
            return carry

        loop(advance)
        new, product = products(k + 1)
        beside_sum(k + 1)
        ratio = new / norm
        step = new / (product - ratio * new / step)
        norm = new
        steps.append(step)
        ratios.append(ratio)

    weights = [steps[-1]]
    for k in reversed(range(ITERS - 1)):
        weights.append(steps[k] + ratios[k] * weights[-1])
    weights.reverse()
    return weights


def flow_kernel(
    levels, ny, nx, u_ref, v_ref, su_ref, sv_ref, ga_ref, gb_ref, y1_ref, y2_ref, edge_ref, outer_ref, made_ref, dut_ref, dvt_ref,
    du_hbm, dv_hbm, eta_hbm, count_s, face_s, r_s, eta_ref, du_ref, dv_ref, sems,
):
    groups = group_count(levels)
    lanes, rows_id = lane_ids(), row_ids()
    core = lax.axis_index("core")
    my_j = lax.axis_index("ty")
    my_i = lax.axis_index("y") * 2 + core
    numbers = level_numbers(groups)
    thick = [1.0 + number * (1.0 / levels) for number in numbers]
    read_row, _ = slot_reader(y1_ref, y2_ref, groups)
    zero = jnp.zeros((SUB, LANES), jnp.float32)

    def read(j, i, first):
        where = (j * (nx // 2) + i // 2, slice(None), pl.ds(first, TILE))
        return jnp.where(core == i % 2, ga_ref[where].reshape(SUB, LANES), gb_ref[where].reshape(SUB, LANES))

    def read_corners(n, j, i):
        where = (j * (nx // 2) + i // 2, slice(None), pl.ds(CHUNK_ROW + groups * TILE + n * LANES, LANES))
        row = jnp.broadcast_to(jnp.where(core == i % 2, ga_ref[where], gb_ref[where]), (SUB, LANES))
        return pltpu.roll(row, LANES - SUB + 1, 1, stride=1, stride_axis=0)

    def block(dj, di, get):
        return get(jnp.clip(my_j + dj, 0, ny - 1), jnp.clip(my_i + di, 0, nx - 1))

    def near(dj, di, get):
        j, i = jnp.clip(my_j + dj, 0, ny - 1), jnp.clip(my_i + di, 0, nx - 1)
        inside = (my_j + dj >= 0) & (my_j + dj < ny) & (my_i + di >= 0) & (my_i + di < nx)
        return jnp.where(inside, get(j, i), 0.0)

    diagonal = {"se": (-1, 1), "sw": (-1, -1), "nw": (1, -1), "ne": (1, 1)}
    corner_tiles = {}
    for places in CORNER_PLACES.values():
        for which, value, _ in places:
            n = value // CORNERS_PER_ROW
            if (which, n) not in corner_tiles:
                corner_tiles[which, n] = near(*diagonal[which], functools.partial(read_corners, n))

    def insert_corners(edge, name, row):
        for which, value, target in CORNER_PLACES.get((name, row), ()):
            there = (lanes & (SEG - 1)) == target
            tile = corner_tiles[which, value // CORNERS_PER_ROW]
            edge = jnp.where(there, roll_lanes(tile, target - value % CORNERS_PER_ROW * SUB), edge)
        return edge

    def rows(name, ref, q, first, last):
        south = [read_row(name, row, q) for row in range(first, 0)]
        north = [read_row(name, row, q) for row in range(SUB, last + 1)]
        return Many(south + load_rows(ref, q, levels).items + north)

    def edges(name):
        first, last = FLOW_ROWS[name]
        n = FLOW_FIELDS.index(name)

        def register(row):
            if 0 <= row < SUB:
                return edge_ref[(n * SUB + row) * SUB : (n * SUB + row + 1) * SUB, :]
            place = OUTER_ROWS.index((name, row)) * SUB
            return insert_corners(outer_ref[place : place + SUB, :], name, row)

        return Many(register(row) for row in range(first, last + 1))

    refs = {"u": u_ref, "v": v_ref, "su": su_ref, "sv": sv_ref}
    data, made = {}, {}

    def prepare(part):
        if part == groups:
            data[part] = [edges(name) for name in FLOW_FIELDS]
            made[part] = prepared(*data[part][:2], *turns(ny))
            return
        data[part] = [rows(name, refs[name], part, *FLOW_ROWS[name]) for name in FLOW_FIELDS]
        made[part], n = [], part * MADE_ROWS
        for size in MADE_SIZES:
            made[part].append(Many(made_ref[k * SUB : (k + 1) * SUB, :] for k in range(n, n + size)))
            n += size

    def pairs(get, operation):
        tiles = [[get(dj, di) for di in (-1, 0, 1)] for dj in (-1, 0, 1)]
        out = []
        for south, own, north in ([row[1] for row in tiles], [edge_of_tile(*row) for row in tiles]):
            outer = jnp.where(rows_id == SUB - 1, south, north)
            below = roll_rows(jnp.where(rows_id == SUB - 1, south, own), 1)
            below_outer = roll_rows(jnp.where(rows_id == SUB - 2, south, own), 1)
            out.append(
                (operation(own, at(own, -1)), operation(outer, at(outer, -1)), operation(own, below), operation(outer, below_outer))
            )
        return out

    def outer_and_own(own, outer):
        return Many([row_of(outer, SUB - 1)] + [row_of(own, row) for row in range(SUB)] + [row_of(outer, 0)])

    wet_counts, differences = [], []

    def beside_setup():
        wet_counts.extend(pairs(lambda dj, di: near(dj, di, lambda j, i: count_s[j, i]), jnp.minimum))

    def beside_sum(k):
        if k == ITERS - 1:
            prepare(groups)
        differences.append(pairs(lambda dj, di: block(dj, di, lambda j, i: r_s[k, j, i]), lambda a, b: a - b))

    weights = surface_solve(levels, ny, nx, read, count_s, face_s, r_s, beside_setup, beside_sum)

    def weighted(parts):
        total_of = parts[0] * weights[0]
        for part, weight in zip(parts[1:], weights[1:]):
            total_of = total_of + part * weight
        return total_of

    slopes = [[weighted([d[kind][n] for d in differences]) for n in range(4)] for kind in range(2)]
    eta_ref[...] = weighted([r_s[k, my_j, my_i] for k in range(ITERS)])
    out = [pltpu.make_async_copy(eta_ref, eta_hbm, sems.at[0])]
    out[0].start()

    def adjoint(parts):
        u, v, su, sv = (joined([data[part][n] for part in parts]) for n in range(4))
        v_bar, u_bar, from_v_bar, from_u_bar, u_across, v_across = (
            joined([made[part][n] for part in parts]) for n in range(len(MADE_SIZES))
        )

        def each(values):
            return Many([values[part] for part in parts for _ in range(SUB + 2)], len(parts))

        def around(of, n):
            return joined([outer_and_own(*of[1 if part == groups else 0][n : n + 2]) for part in parts])

        wet_u, wet_v = around(wet_counts, 0) > each(numbers), around(wet_counts, 2) > each(numbers)
        u_cot = su + (around(slopes, 0) * each(thick)).where(wet_u, zero)
        v_cot = sv + (around(slopes, 2) * each(thick)).where(wet_v, zero)
        a, b = (u_cot * (0.5 * ADVECT)).where(wet_u, zero), (v_cot * (0.5 * ADVECT)).where(wet_v, zero)
        av, bu = a * v_bar, b[1:9] * u_bar
        au, bv = a[1:9] * u[2:10], b * v[:-1]
        to_v_bar, to_u_bar = a[:-1] * from_v_bar, b[1:] * from_u_bar
        near_u, near_v = to_u_bar[:-1] + to_u_bar[1:], to_v_bar[1:] + to_v_bar[:-1]
        du = u_cot[1:9] - a[1:9] * u_across + av[2:] - av[:-2] + near_u
        du = du + au.at(1) + (near_u - au).at(-1)
        dv = v_cot[1:9] - b[1:9] * v_across + bv[2:] - bv[:-2] + near_v
        dv = dv + (near_v + bu).at(1) - bu.at(-1)
        return list(zip(du.split(), dv.split()))

    for part in range(groups):
        prepare(part)
    flow = {}
    for parts in ADJOINT_PARTS:
        flow.update(zip(parts, adjoint(parts)))
    edge_u, edge_v = (outer_columns(part) for part in flow[groups])
    for q in range(groups):
        du, dv = flow[q]
        store_rows(du_ref, q, levels, merge_edges(du, edge_u, q) + load_rows(dut_ref, q, levels))
        store_rows(dv_ref, q, levels, merge_edges(dv, edge_v, q) + load_rows(dvt_ref, q, levels))
        part = pl.ds(q * SUB * SUB, min(SUB, levels - q * SUB) * SUB)
        for target, source in ((du_hbm, du_ref), (dv_hbm, dv_ref)):
            out.append(pltpu.make_async_copy(source.at[part, :], target.at[part, :], sems.at[len(out)]))
            out[-1].start()
    for copy in out:
        copy.wait()


def swaps(mesh_shape, along, parity):
    ny, nx = mesh_shape
    pairs = []
    for j in range(ny):
        for i in range(nx):
            k, size = (j, ny) if along == "y" else (i, nx)
            other = k + 1 if k % 2 == parity else k - 1
            if 0 <= other < size:
                pairs.append((j * nx + i, other * nx + i if along == "y" else j * nx + other))
    return pairs


def call(kernel, outs, args, scratch=(), flops=0, size=0, far_in=False, far_out=(), limit=48):
    near, far = pl.BlockSpec(memory_space=pltpu.VMEM), pl.BlockSpec(memory_space=pltpu.HBM)
    outs = [out if isinstance(out, jax.ShapeDtypeStruct) else jax.ShapeDtypeStruct(out, jnp.float32) for out in outs]
    return pl.pallas_call(
        kernel,
        out_shape=outs,
        in_specs=[far if far_in else near] * len(args),
        out_specs=[far if n in far_out else near for n in range(len(outs))],
        scratch_shapes=list(scratch),
        compiler_params=pltpu.CompilerParams(vmem_limit_bytes=limit * 1024 * 1024),
        cost_estimate=pl.CostEstimate(flops=flops, bytes_accessed=size, transcendentals=0),
    )(*args)


def on_device(shape, u, v, t, count, su, sv, st, elev):
    ny, nx = shape
    levels = u.shape[0]
    groups = group_count(levels)
    flat = (levels * SUB, LANES)
    room = (groups * SUB * SUB, LANES)
    u, v, t, su, sv, st = (field.reshape(flat) for field in (u, v, t, su, sv, st))
    peers = ny * nx // 2
    row_packet = ((N_SLOTS * groups + 1) * SUB, LANES)
    column_packet = ((SUB + 1) * SUB, LANES)
    chunk = (peers, 1, CHUNK_ROW + groups * TILE + len(CORNERS) // CORNERS_PER_ROW * LANES)
    tile = (SUB, LANES)
    (chunks,) = call(
        functools.partial(chunk_kernel, levels, peers),
        [chunk],
        (u, v, su, sv, count, elev),
        scratch=[pltpu.VMEM(flat, jnp.float32)] * 4
        + [pltpu.VMEM(tile, count.dtype), pltpu.VMEM(tile, jnp.float32), pltpu.SemaphoreType.DMA((6,))],
        flops=1 << 20,
        size=1 << 21,
        far_in=True,
        limit=60,
    )
    y1, y2, xp = call(
        functools.partial(packet_kernel, levels),
        [row_packet, row_packet, column_packet],
        (u, v, t, su, sv, st, count),
        flops=1 << 20,
        size=1 << 21,
    )
    axes = ("ty", "y", "core")
    ga = lax.all_to_all(chunks, ("ty", "y"), 0, 0)
    x1 = lax.ppermute(xp, axes, swaps(shape, "x", 0))
    x2 = lax.ppermute(xp, axes, swaps(shape, "x", 1))
    y1 = lax.ppermute(y1, axes, swaps(shape, "y", 0))
    y2 = lax.ppermute(y2, axes, swaps(shape, "y", 1))
    dtx, du_t, edge = call(
        functools.partial(column_kernel, levels),
        [room, room, (len(FLOW_FIELDS) * SUB * SUB, LANES)],
        (u, v, t, st, su, sv, count, x1, x2),
        flops=1 << 22,
        size=1 << 21,
    )
    ga, y1, y2, dtx = lax.optimization_barrier((ga, y1, y2, dtx))
    gb = lax.ppermute(ga, axes, swaps(shape, "x", 0))
    dt, dv_t, made, outer = call(
        functools.partial(row_kernel, levels, ny),
        [flat, room, (groups * MADE_ROWS * SUB, LANES), (len(OUTER_ROWS) * SUB, LANES)],
        (u, v, t, st, count, y1, y2, dtx),
        scratch=(pltpu.VMEM(room, jnp.float32), pltpu.SemaphoreType.DMA((groups,))),
        flops=1 << 22,
        size=1 << 21,
        far_out=(0,),
    )
    grid = pltpu.VMEM((ny, nx, SUB, LANES), jnp.float32)
    faces, residuals = (pltpu.VMEM((n, ny, nx, SUB, LANES), jnp.float32) for n in (7, ITERS))
    du, dv, eta = call(
        functools.partial(flow_kernel, levels, ny, nx),
        [flat, flat, (SUB, LANES)],
        (u, v, su, sv, ga, gb, y1, y2, edge, outer, made, du_t, dv_t),
        far_out=(0, 1, 2),
        scratch=(grid, faces, residuals)
        + tuple(pltpu.VMEM(shape, jnp.float32) for shape in (tile, room, room))
        + (pltpu.SemaphoreType.DMA((2 * groups + 1,)),),
        flops=1 << 23,
        size=1 << 22,
    )
    whole = (levels, SUB, LANES)
    return du.reshape(whole), dv.reshape(whole), dt.reshape(whole), eta


def solution(mesh):
    ny, nx = mesh.shape["ty"], mesh.shape["tx"]
    split = Mesh(mesh.devices.reshape(ny, nx // 2, 2), ("ty", "y", "core"))
    deep, flat = P(None, "ty", ("y", "core")), P("ty", ("y", "core"))
    return jax.shard_map(
        functools.partial(on_device, (ny, nx)),
        mesh=split,
        in_specs=(deep, deep, deep, flat, deep, deep, deep, flat),
        out_specs=(deep, deep, deep, flat),
        check_vma=False,
    )
```

```python
import functools

import jax
import jax.numpy as jnp
from jax import lax
from jax.experimental import pallas as pl
from jax.experimental.pallas import tpu as pltpu
from jax.sharding import Mesh, PartitionSpec as P

ITERS = 4
ADVECT = 0.1
GRAVITY_DT = 0.1

SUB = 8
LANES = 128
SEG = 32
FIELDS = ("u", "v", "t", "st", "su", "sv")
BAND_BLOCKS = 32
ADJOINT_PARTS = ((4, 0), (1, 2), (3,))
FLOW_FIELDS = ("u", "v", "su", "sv")
FLOW_ROWS = {"u": (-2, 8), "v": (-1, 9), "su": (-1, 8), "sv": (-1, 8)}
OUTER_ROWS = tuple((n, r) for n in FLOW_FIELDS for r in range(FLOW_ROWS[n][0], FLOW_ROWS[n][1] + 1) if not 0 <= r < 8)
MADE_SIZES = (10, 8, 9, 9, 8, 8)
MADE_ROWS = sum(MADE_SIZES)
SOUTH_SLOTS = {("u", -2): 0, ("u", -1): 1, ("v", -1): 2, ("t", -2): 3, ("t", -1): 4, ("st", -2): 5, ("st", -1): 6}
SOUTH_SLOTS.update({("su", -1): 7, ("sv", -1): 8})
NORTH_SLOTS = {("u", 8): 0, ("v", 8): 1, ("v", 9): 2, ("t", 8): 3, ("st", 8): 5, ("st", 9): 6, ("su", 8): 7, ("sv", 8): 8}
N_SLOTS = 9
TILE = SUB * LANES
CHUNK_LOAD = TILE
CHUNK_ROW = 2 * TILE
WEST_LEVELS = LANES // SUB
CORNERS_PER_ROW = 4
CORNERS = (("u", 6, 0), ("u", 7, 0), ("u", 7, 1), ("su", 7, 0), ("v", 7, 127), ("u", 7, 127))
CORNERS += (("v", 0, 127), ("v", 1, 127), ("v", 0, 126), ("sv", 0, 127), ("v", 0, 0), ("u", 0, 0))
CORNER_PLACES = {
    ("u", -2): (("se", 0, 24),),
    ("u", -1): (("se", 1, 24), ("se", 2, 25), ("sw", 5, 7)),
    ("su", -1): (("se", 3, 24),),
    ("v", -1): (("sw", 4, 7),),
    ("v", 8): (("nw", 6, 7), ("nw", 8, 6), ("ne", 10, 24)),
    ("u", 8): (("ne", 11, 24),),
    ("v", 9): (("nw", 7, 7),),
    ("sv", 8): (("nw", 9, 7),),
}


def lane_ids():
    return lax.broadcasted_iota(jnp.int32, (SUB, LANES), 1)


def row_ids():
    return lax.broadcasted_iota(jnp.int32, (SUB, LANES), 0)


def roll_lanes(value, amount):
    amount %= LANES
    return value if amount == 0 else pltpu.roll(value, amount, 1)


def roll_rows(value, amount):
    amount %= SUB
    return value if amount == 0 else pltpu.roll(value, amount, 0)


def at(value, shift):
    return roll_lanes(value, -shift)


def row_of(tile, row):
    return jnp.broadcast_to(tile[row : row + 1, :], (SUB, LANES))


def group_count(levels):
    return -(-levels // SUB)


def load_group(ref, row, q, levels):
    first = min(q * SUB, levels - SUB)
    value = ref[pl.ds(first * SUB + row, SUB, stride=SUB), :]
    return roll_rows(value, first - q * SUB)


def store_group(ref, row, q, levels, value):
    count = min(SUB, levels - q * SUB)
    ref[pl.ds(q * SUB * SUB + row, count, stride=SUB), :] = value[:count]


def level_numbers(groups):
    rows = row_ids()
    numbers = [(rows + q * SUB).astype(jnp.float32) for q in range(groups)]
    return numbers + [(rows + (lane_ids() >> 5) * SUB).astype(jnp.float32)]


def edge_of_tile(west, centre, east):
    lanes = lane_ids()
    out = jnp.where(lanes < 8, roll_lanes(west, 8), roll_lanes(centre, 8))
    out = jnp.where(lanes >= 16, roll_lanes(centre, 24), out)
    out = jnp.where(lanes >= 24, roll_lanes(east, 24), out)
    out = jnp.where(lanes < SEG, out, roll_lanes(out, SEG))
    return jnp.where(lanes < 2 * SEG, out, roll_lanes(out, 2 * SEG))


def chunk_kernel(
    levels, peers, u_hbm, v_hbm, su_hbm, sv_hbm, count_hbm, elev_hbm, chunk_ref,
    u_ref, v_ref, su_ref, sv_ref, count_ref, elev_ref, sems,
):
    pairs = (
        (count_hbm, count_ref), (su_hbm, su_ref), (sv_hbm, sv_ref), (elev_hbm, elev_ref), (u_hbm, u_ref), (v_hbm, v_ref),
    )
    copies = [pltpu.make_async_copy(source, target, sems.at[n]) for n, (source, target) in enumerate(pairs)]
    for copy in copies:
        copy.start()
    groups = group_count(levels)
    lanes, rows = lane_ids(), row_ids()
    refs = {"u": u_ref, "v": v_ref, "su": su_ref, "sv": sv_ref}
    for copy in copies[:4]:
        copy.wait()
    count = count_ref[...].astype(jnp.float32)
    zero = jnp.zeros((SUB, LANES), jnp.float32)

    wet_u = jnp.where(lanes == 0, 0.0, jnp.minimum(count, roll_lanes(count, 1)))
    wet_v = jnp.where(rows == 0, 0.0, jnp.minimum(count, roll_rows(count, 1)))
    col_u, col_v = [zero] * 4, [zero] * 4
    west = [zero] * (levels // WEST_LEVELS + 1)
    for k in range(levels):
        su_level = su_ref[k * SUB : (k + 1) * SUB, :]
        col_u[k % 4] = col_u[k % 4] + jnp.where(wet_u > float(k), su_level, 0.0)
        col_v[k % 4] = col_v[k % 4] + jnp.where(wet_v > float(k), sv_ref[k * SUB : (k + 1) * SUB, :], 0.0)
        n = k // WEST_LEVELS
        there = lanes == rows + k % WEST_LEVELS * SUB
        west[n] = jnp.where(there, jnp.broadcast_to(su_level[:, 0:1], (SUB, LANES)), west[n])
    col_u, col_v = ((col[0] + col[1]) + (col[2] + col[3]) for col in (col_u, col_v))
    load = elev_ref[...] + GRAVITY_DT * (at(col_u, 1) - col_u + roll_rows(col_v, -1) - col_v)

    for copy in copies[4:]:
        copy.wait()
    corners = [zero] * (len(CORNERS) // CORNERS_PER_ROW)
    for place, (name, row, column) in enumerate(CORNERS):
        n, base = place // CORNERS_PER_ROW, place % CORNERS_PER_ROW * SUB
        for q in range(groups):
            value = load_group(refs[name], row, q, levels)[:, column : column + 1]
            there = lanes == SEG * q + base + SUB - 1 - rows
            corners[n] = jnp.where(there, jnp.broadcast_to(value, (SUB, LANES)), corners[n])

    def in_a_row(tile):
        return jnp.broadcast_to(jnp.sum(tile, axis=0, keepdims=True), (SUB, LANES))

    tiles = [count, load] + [load_group(sv_ref, 0, q, levels) for q in range(groups)]
    for n, part in enumerate(west):
        tiles[-1] = jnp.where(rows == SUB - len(west) + n, in_a_row(part), tiles[-1])
    last = zero
    for n, part in enumerate(corners):
        last = jnp.where(rows == n, in_a_row(part), last)
    tiles = [tile.reshape(1, TILE) for tile in tiles + [last]]
    tiles[-1] = tiles[-1][:, : len(corners) * LANES]

    def put(peer, carry):
        first = 0
        for tile in tiles:
            chunk_ref[peer, :, first : first + tile.shape[1]] = tile
            first += tile.shape[1]
        return carry

    lax.fori_loop(0, peers, put, 0, unroll=4)


def packet_kernel(levels, u_ref, v_ref, t_ref, su_ref, sv_ref, st_ref, count_ref, y1_ref, y2_ref, x_ref):
    groups = group_count(levels)
    lanes = lane_ids()
    zero = jnp.zeros((SUB, LANES), jnp.float32)
    count = count_ref[...].astype(jnp.float32)
    even = lax.axis_index("ty") % 2 == 0
    refs = {"u": u_ref, "v": v_ref, "t": t_ref, "st": st_ref, "su": su_ref, "sv": sv_ref}
    loaded = {}
    for name in FIELDS:
        for row in range(SUB):
            for q in range(groups):
                loaded[name, row, q] = load_group(refs[name], row, q, levels)

    for slot in range(N_SLOTS):
        upper = [(name, row + SUB) for (name, row), place in SOUTH_SLOTS.items() if place == slot]
        lower = [(name, row - SUB) for (name, row), place in NORTH_SLOTS.items() if place == slot]
        for q in range(groups):
            to_north = loaded[(*upper[0], q)]
            to_south = loaded[(*lower[0], q)] if lower else zero
            place = pl.ds((slot * groups + q) * SUB, SUB)
            y1_ref[place, :] = jnp.where(even, to_north, to_south)
            y2_ref[place, :] = jnp.where(even, to_south, to_north)
    y1_ref[N_SLOTS * groups * SUB :, :] = count
    y2_ref[N_SLOTS * groups * SUB :, :] = count

    for row in range(SUB):
        packet = zero
        for field, name in enumerate(FIELDS):
            for q in range(groups):
                lane = SEG * q + 4 * field
                packet = jnp.where((lanes >= lane) & (lanes < lane + 4), roll_lanes(loaded[name, row, q], lane + 2), packet)
        x_ref[row * SUB : (row + 1) * SUB, :] = packet
    x_ref[SUB * SUB :, :] = count


def joined(parts):
    return Many([item for part in parts for item in part.items], len(parts))


class Many:
    def __init__(self, items, parts=1):
        self.items = list(items)
        self.parts = parts

    def __getitem__(self, where):
        if not isinstance(where, slice):
            return self.items[where]
        rows = len(self.items) // self.parts
        return Many([item for n in range(self.parts) for item in self.items[n * rows : (n + 1) * rows][where]], self.parts)

    def __len__(self):
        return len(self.items)

    def split(self):
        rows = len(self.items) // self.parts
        return [Many(self.items[n * rows : (n + 1) * rows]) for n in range(self.parts)]

    def apply(self, operation, *others):
        others = [other.items if isinstance(other, Many) else [other] * len(self) for other in others]
        assert all(len(other) == len(self) for other in others)
        return Many([operation(*parts) for parts in zip(self.items, *others)], self.parts)

    def __add__(self, other):
        return self.apply(lambda a, b: a + b, other)

    def __sub__(self, other):
        return self.apply(lambda a, b: a - b, other)

    def __mul__(self, other):
        return self.apply(lambda a, b: a * b, other)

    def __gt__(self, other):
        return self.apply(lambda a, b: a > b, other)

    def at(self, shift):
        return self.apply(lambda a: at(a, shift))

    def rolled(self, amount):
        return self.apply(lambda a: roll_lanes(a, amount))

    def minimum(self, other):
        return self.apply(jnp.minimum, other)

    def where(self, mask, other):
        return self.apply(lambda a, m, b: jnp.where(m, a, b), mask, other)


def edges_of_groups(parts):
    lanes = lane_ids()
    out = parts[0].rolled(8)
    for q in range(1, len(parts)):
        out = parts[q].rolled(SEG * q + 8).where(lanes >= SEG * q, out)
    return out.rolled(16).where((lanes & (SEG - 1)) >= 16, out)


def insert_sides(edge, west, east, field):
    place = lane_ids() & (SEG - 1)
    edge = west.rolled(6 - 4 * field).where((place == 6) | (place == 7), edge)
    return east.rolled(22 - 4 * field).where((place == 24) | (place == 25), edge)


def outer_columns(edge):
    return edge.rolled(-16).where((lane_ids() & (SEG - 1)) < 8, edge)


def merge_edges(values, outer, q):
    lanes = lane_ids()
    return outer.rolled(-(SEG * q + 8)).where((lanes < 2) | (lanes >= LANES - 2), values)


def load_rows(ref, q, levels):
    return Many(load_group(ref, row, q, levels) for row in range(SUB))


def store_rows(ref, q, levels, values):
    for row in range(SUB):
        store_group(ref, row, q, levels, values[row])


def rows_of(tiles, first, last):
    return Many(row_of(tiles[row // SUB + 1], row % SUB) for row in range(first, last + 1))


def slot_reader(y1_ref, y2_ref, groups):
    even = lax.axis_index("ty") % 2 == 0

    def read(name, row, q):
        slot = (SOUTH_SLOTS if row < 0 else NORTH_SLOTS)[name, row]
        place = pl.ds((slot * groups + q) * SUB, SUB)
        one, two = y1_ref[place, :], y2_ref[place, :]
        return jnp.where(even, two, one) if row < 0 else jnp.where(even, one, two)

    def counts():
        place = pl.ds(N_SLOTS * groups * SUB, SUB)
        one, two = y1_ref[place, :], y2_ref[place, :]
        return jnp.where(even, two, one), jnp.where(even, one, two)

    return read, counts


def side_reader(x1_ref, x2_ref):
    even = lax.axis_index("core") % 2 == 0

    def read(row):
        place = pl.ds(row * SUB, SUB)
        one, two = x1_ref[place, :], x2_ref[place, :]
        return jnp.where(even, two, one), jnp.where(even, one, two)

    return read


def face_values(t0, t_before, t_after, t_before2):
    return ((t0 + t_before) * 7.0 - (t_after + t_before2)) * (1.0 / 12.0)


def edge_rows(ref, west, east, levels, groups, name):
    own = edges_of_groups([load_rows(ref, q, levels) for q in range(groups)])
    return insert_sides(own, west, east, FIELDS.index(name))


def column_kernel(
    levels, u_ref, v_ref, t_ref, st_ref, su_ref, sv_ref, count_ref, x1_ref, x2_ref, dt_ref, du_ref, edge_ref
):
    groups = group_count(levels)
    read_sides = side_reader(x1_ref, x2_ref)
    numbers = level_numbers(groups)
    zero = jnp.zeros((SUB, LANES), jnp.float32)
    count = count_ref[...].astype(jnp.float32)
    count_west, count_east = read_sides(SUB)
    count_edge = edge_of_tile(count_west, count, count_east)

    def counts(tile):
        return tuple(rows_of((None, part, None), 0, 7) for part in (tile, jnp.minimum(tile, at(tile, -1))))

    def along(level, wet, wet_u, u, t, st):
        cell = (st * -ADVECT).where(wet > level, zero)
        flux = (cell.at(-1) - cell).where(wet_u > level, zero)
        back = u * flux
        face = face_values(t, t.at(-1), t.at(1), t.at(-2))
        return ((back + back.at(1)) * 7.0 - (back.at(-1) + back.at(2))) * (1.0 / 12.0), flux * face

    sides = [read_sides(row) for row in range(SUB)]
    west, east = Many(side[0] for side in sides), Many(side[1] for side in sides)
    u, t, st = (
        edge_rows(ref, west, east, levels, groups, name) for name, ref in (("u", u_ref), ("t", t_ref), ("st", st_ref))
    )
    edge_t, edge_u = (outer_columns(part) for part in along(numbers[groups], *counts(count_edge), u, t, st))
    own = counts(count)
    for q in range(groups):
        st = load_rows(st_ref, q, levels)
        from_x, to_u = along(numbers[q], *own, load_rows(u_ref, q, levels), load_rows(t_ref, q, levels), st)
        store_rows(dt_ref, q, levels, st + merge_edges(from_x, edge_t, q))
        store_rows(du_ref, q, levels, merge_edges(to_u, edge_u, q))
    flow = (u,) + tuple(
        edge_rows(ref, west, east, levels, groups, name) for name, ref in (("v", v_ref), ("su", su_ref), ("sv", sv_ref))
    )
    for n, rows in enumerate(flow):
        for row in range(SUB):
            edge_ref[(n * SUB + row) * SUB : (n * SUB + row + 1) * SUB, :] = rows[row]


def turns(ny):
    first_row = (lax.axis_index("ty") * SUB).astype(jnp.float32)
    scale = 0.5 / (ny * SUB)
    turn_u = Many(0.25 + (first_row + (row + 0.5)) * scale for row in range(-1, 8))
    return turn_u, Many(-0.25 - (first_row + row) * scale for row in range(0, 9))


def prepared(u, v, turn_u, turn_v):
    v_pair, u_pair = v[:-1] + v[1:], u[2:10] + u[1:9]
    return (
        (v_pair + v_pair.at(-1)) * 0.25,
        (u_pair + u_pair.at(1)) * 0.25,
        (u[:-2] - u[2:]) * 0.25 + turn_u,
        (v[1:10].at(-1) - v[1:10].at(1)) * 0.25 + turn_v,
        u[2:10].at(1) - u[2:10].at(-1),
        v[2:10] - v[0:8],
    )


def row_kernel(
    levels, ny, u_ref, v_ref, t_ref, st_ref, count_ref, y1_ref, y2_ref, dtx_ref, dt_hbm, dv_ref, made_ref, edge_ref, dt_ref, sems
):
    groups = group_count(levels)
    read_row, read_counts = slot_reader(y1_ref, y2_ref, groups)
    numbers = level_numbers(groups)
    zero = jnp.zeros((SUB, LANES), jnp.float32)
    count = count_ref[...].astype(jnp.float32)
    count_south, count_north = read_counts()
    counts = rows_of((count_south, count, count_north), -2, 9)
    counts_v = counts[1:].minimum(counts[:-1])
    out = []
    for n, (name, row) in enumerate(OUTER_ROWS):
        (edge,) = edges_of_groups([Many([read_row(name, row, q)]) for q in range(groups)]).items
        edge_ref[n * SUB : (n + 1) * SUB, :] = edge
    for q in range(groups):
        level = numbers[q]

        def rows(name, ref, first, last):
            south = [read_row(name, row, q) for row in range(first, 0)]
            north = [read_row(name, row, q) for row in range(SUB, last + 1)]
            return Many(south + load_rows(ref, q, levels).items + north)

        t, st, v = rows("t", t_ref, -2, 8), rows("st", st_ref, -2, 9), rows("v", v_ref, -1, 9)
        made = prepared(rows("u", u_ref, -2, 8), v, *turns(ny))
        for n, value in enumerate(value for values in made for value in values.items):
            place = pl.ds((q * MADE_ROWS + n) * SUB, SUB)
            made_ref[place, :] = value
        cell = (st * -ADVECT).where(counts > level, zero)
        flux = (cell[:-1] - cell[1:]).where(counts_v > level, zero)
        back = v * flux
        from_y = ((back[1:9] + back[2:10]) * 7.0 - (back[0:8] + back[3:11])) * (1.0 / 12.0)
        to_v = flux[1:9] * face_values(t[2:10], t[1:9], t[3:11], t[0:8])
        store_rows(dt_ref, q, levels, load_rows(dtx_ref, q, levels) + from_y)
        store_rows(dv_ref, q, levels, to_v)
        part = pl.ds(q * SUB * SUB, min(SUB, levels - q * SUB) * SUB)
        out.append(pltpu.make_async_copy(dt_ref.at[part, :], dt_hbm.at[part, :], sems.at[q]))
        out[-1].start()
    for copy in out:
        copy.wait()


def total(value):
    return jnp.sum(value, axis=(0, 1), keepdims=True)


def surface_solve(levels, ny, nx, read, count_ref, face_ref, r_refs, beside_setup, beside_sum):
    groups = group_count(levels)
    lanes, rows = lane_ids(), row_ids()
    numbers = level_numbers(groups)
    zero = jnp.zeros((SUB, LANES), jnp.float32)
    band = max(1, min(ny, BAND_BLOCKS // nx))
    while ny % band:
        band -= 1
    cells = [(dj, i) for dj in range(band) for i in range(nx)]

    def loop(body, init=0):
        if ny * nx <= 32:
            for j in range(0, ny, band):
                init = body(j, init)
            return init
        return lax.fori_loop(0, ny // band, lambda step, carry: body(step * band, carry), init)

    def get(ref, j):
        return Many(ref[j + dj, i] for dj, i in cells)

    def put(ref, j, values):
        for (dj, i), value in zip(cells, values.items):
            ref[j + dj, i] = value

    def beside(values, step):
        return Many(values[dj * nx + min(max(i + step, 0), nx - 1)] for dj, i in cells)

    def below(ref, j, values):
        outside = [ref[max(j - 1, 0) if isinstance(j, int) else jnp.maximum(j - 1, 0), i] for i in range(nx)]
        return Many(outside + values.items[:-nx])

    def above(ref, j, values):
        top = min(j + band, ny - 1) if isinstance(j, int) else jnp.minimum(j + band, ny - 1)
        outside = [ref[top, i] for i in range(nx)]
        return Many(values.items[nx:] + outside)

    def west_of(values):
        return beside(values, -1).where(lanes == LANES - 1, values).rolled(1)

    def east_of(values):
        return beside(values, 1).where(lanes == 0, values).rolled(-1)

    def south_of(ref, j, values):
        return below(ref, j, values).where(rows == SUB - 1, values).apply(lambda a: roll_rows(a, 1))

    def north_of(ref, j, values):
        return above(ref, j, values).where(rows == 0, values).apply(lambda a: roll_rows(a, -1))

    def depth(wet):
        return wet.apply(lambda m: m * (m * (GRAVITY_DT * 0.5 / levels) + GRAVITY_DT * (1.0 - 0.5 / levels)))

    def gather(j, carry):
        put(count_ref, j, Many(read(j + dj, i, 0) for dj, i in cells))
        return carry

    loop(gather)

    def faces(j, carry):
        count = get(count_ref, j)
        wet_u, wet_v = count.minimum(west_of(count)), count.minimum(south_of(count_ref, j, count))
        first_column = [(lanes == 0) if i == 0 else (lanes < 0) for dj, i in cells]
        first_row = [(rows == 0) & (j + dj == 0) for dj, i in cells]
        wet_u = Many([zero] * len(cells)).where(Many(first_column), wet_u)
        wet_v = Many([zero] * len(cells)).where(Many(first_row), wet_v)
        put(face_ref.at[0], j, depth(wet_u))
        put(face_ref.at[1], j, depth(wet_v))
        wet_west = wet_u.apply(lambda a: jnp.broadcast_to(a[:, 0:1], (SUB, LANES)))
        souths = [Many(read(j + dj, i, CHUNK_ROW + q * TILE) for dj, i in cells) for q in range(groups)]
        inside = Many([zero] * len(cells))
        for n in range(levels // WEST_LEVELS + 1):
            reach = jnp.where((lanes & (SUB - 1)) == rows, (lanes >> 3) + n * WEST_LEVELS, levels).astype(jnp.float32)
            west = souths[-1].apply(lambda a: row_of(a, SUB - 1 - levels // WEST_LEVELS + n))
            inside = inside + west.where(wet_west > reach, zero)
        col_u = inside.apply(lambda a: jnp.broadcast_to(jnp.sum(a, axis=1, keepdims=True), (SUB, LANES)))
        put(face_ref.at[4], j, col_u * GRAVITY_DT)
        wet_south = wet_v.apply(lambda a: row_of(a, 0))
        col_v = Many([zero] * len(cells))
        for q in range(groups):
            col_v = col_v + souths[q].where(wet_south > numbers[q], zero)
        col_v = col_v.apply(lambda a: jnp.broadcast_to(jnp.sum(a, axis=0, keepdims=True), (SUB, LANES)))
        put(face_ref.at[5], j, col_v * GRAVITY_DT)
        return carry

    loop(faces)
    beside_setup()

    def start(j, carry):
        load = Many(read(j + dj, i, CHUNK_LOAD) for dj, i in cells)
        col_u, col_v = get(face_ref.at[4], j), get(face_ref.at[5], j)
        depth_u, depth_v = get(face_ref.at[0], j), get(face_ref.at[1], j)
        last_column = Many((lanes == LANES - 1) if i + 1 < nx else (lanes < 0) for dj, i in cells)
        at_end = Many((lanes == LANES - 1) if i + 1 == nx else (lanes < 0) for dj, i in cells)
        last_row = Many((rows == SUB - 1) & (j + dj + 1 < ny) for dj, i in cells)
        at_top = Many((rows == SUB - 1) & (j + dj + 1 == ny) for dj, i in cells)
        none = Many([zero] * len(cells))
        load = load - col_u.where(lanes == 0, zero) - col_v.where(rows == 0, zero)
        load = load + beside(col_u, 1).where(last_column, none) + above(face_ref.at[5], j, col_v).where(last_row, none)
        depth_east = none.where(at_end, east_of(depth_u))
        depth_north = none.where(at_top, north_of(face_ref.at[1], j, depth_v))
        put(face_ref.at[2], j, depth_east)
        put(face_ref.at[3], j, depth_north)
        put(face_ref.at[6], j, (depth_u + depth_east) + (depth_v + depth_north) + 1.0)
        put(r_refs.at[0], j, load)
        return carry

    def gathered(partial, values):
        items = list(values.items)
        while len(items) > 1:
            items = [a + b for a, b in zip(items[::2], items[1::2])] + items[len(items) // 2 * 2 :]
        return partial + items[0]

    loop(start)

    def products(k):
        r_ref = r_refs.at[k]

        def body(j, carry):
            r = get(r_ref, j)
            if k + 1 == ITERS:
                half = get(face_ref.at[0], j) * west_of(r) + get(face_ref.at[1], j) * south_of(r_ref, j, r)
                image = r * get(face_ref.at[6], j) - (half + half)
                return gathered(carry[0], r * r), gathered(carry[1], r * image)
            image = r * get(face_ref.at[6], j) - get(face_ref.at[0], j) * west_of(r) - get(face_ref.at[2], j) * east_of(r)
            image = image - get(face_ref.at[1], j) * south_of(r_ref, j, r)
            image = image - get(face_ref.at[3], j) * north_of(r_ref, j, r)
            put(face_ref.at[4], j, image)
            return gathered(carry[0], r * r), gathered(carry[1], r * image)

        return [total(part) for part in loop(body, (zero, zero))]

    norm, product = products(0)
    beside_sum(0)
    step = norm / product
    steps, ratios = [step], []

    for k in range(ITERS - 1):

        def advance(j, carry):
            image = get(face_ref.at[4], j)
            if k > 0:
                image = image + get(face_ref.at[5], j) * ratio
            if k + 2 < ITERS:
                put(face_ref.at[5], j, image)
            put(r_refs.at[k + 1], j, get(r_refs.at[k], j) - image * step)
            return carry

        loop(advance)
        new, product = products(k + 1)
        beside_sum(k + 1)
        ratio = new / norm
        step = new / (product - ratio * new / step)
        norm = new
        steps.append(step)
        ratios.append(ratio)

    weights = [steps[-1]]
    for k in reversed(range(ITERS - 1)):
        weights.append(steps[k] + ratios[k] * weights[-1])
    weights.reverse()
    return weights


def flow_kernel(
    levels, ny, nx, u_ref, v_ref, su_ref, sv_ref, ga_ref, gb_ref, y1_ref, y2_ref, edge_ref, outer_ref, made_ref, dut_ref, dvt_ref,
    du_hbm, dv_hbm, eta_hbm, count_s, face_s, r_s, eta_ref, du_ref, dv_ref, sems,
):
    groups = group_count(levels)
    lanes, rows_id = lane_ids(), row_ids()
    core = lax.axis_index("core")
    my_j = lax.axis_index("ty")
    my_i = lax.axis_index("y") * 2 + core
    numbers = level_numbers(groups)
    thick = [1.0 + number * (1.0 / levels) for number in numbers]
    read_row, _ = slot_reader(y1_ref, y2_ref, groups)
    zero = jnp.zeros((SUB, LANES), jnp.float32)

    def read(j, i, first):
        where = (j * (nx // 2) + i // 2, slice(None), pl.ds(first, TILE))
        return jnp.where(core == i % 2, ga_ref[where].reshape(SUB, LANES), gb_ref[where].reshape(SUB, LANES))

    def read_corners(n, j, i):
        where = (j * (nx // 2) + i // 2, slice(None), pl.ds(CHUNK_ROW + groups * TILE + n * LANES, LANES))
        row = jnp.broadcast_to(jnp.where(core == i % 2, ga_ref[where], gb_ref[where]), (SUB, LANES))
        return pltpu.roll(row, LANES - SUB + 1, 1, stride=1, stride_axis=0)

    def block(dj, di, get):
        return get(jnp.clip(my_j + dj, 0, ny - 1), jnp.clip(my_i + di, 0, nx - 1))

    def near(dj, di, get):
        j, i = jnp.clip(my_j + dj, 0, ny - 1), jnp.clip(my_i + di, 0, nx - 1)
        inside = (my_j + dj >= 0) & (my_j + dj < ny) & (my_i + di >= 0) & (my_i + di < nx)
        return jnp.where(inside, get(j, i), 0.0)

    diagonal = {"se": (-1, 1), "sw": (-1, -1), "nw": (1, -1), "ne": (1, 1)}
    corner_tiles = {}
    for places in CORNER_PLACES.values():
        for which, value, _ in places:
            n = value // CORNERS_PER_ROW
            if (which, n) not in corner_tiles:
                corner_tiles[which, n] = near(*diagonal[which], functools.partial(read_corners, n))

    def insert_corners(edge, name, row):
        for which, value, target in CORNER_PLACES.get((name, row), ()):
            there = (lanes & (SEG - 1)) == target
            tile = corner_tiles[which, value // CORNERS_PER_ROW]
            edge = jnp.where(there, roll_lanes(tile, target - value % CORNERS_PER_ROW * SUB), edge)
        return edge

    def rows(name, ref, q, first, last):
        south = [read_row(name, row, q) for row in range(first, 0)]
        north = [read_row(name, row, q) for row in range(SUB, last + 1)]
        return Many(south + load_rows(ref, q, levels).items + north)

    def edges(name):
        first, last = FLOW_ROWS[name]
        n = FLOW_FIELDS.index(name)

        def register(row):
            if 0 <= row < SUB:
                return edge_ref[(n * SUB + row) * SUB : (n * SUB + row + 1) * SUB, :]
            place = OUTER_ROWS.index((name, row)) * SUB
            return insert_corners(outer_ref[place : place + SUB, :], name, row)

        return Many(register(row) for row in range(first, last + 1))

    refs = {"u": u_ref, "v": v_ref, "su": su_ref, "sv": sv_ref}
    data, made = {}, {}

    def prepare(part):
        if part == groups:
            data[part] = [edges(name) for name in FLOW_FIELDS]
            made[part] = prepared(*data[part][:2], *turns(ny))
            return
        data[part] = [rows(name, refs[name], part, *FLOW_ROWS[name]) for name in FLOW_FIELDS]
        made[part], n = [], part * MADE_ROWS
        for size in MADE_SIZES:
            made[part].append(Many(made_ref[k * SUB : (k + 1) * SUB, :] for k in range(n, n + size)))
            n += size

    def pairs(get, operation):
        tiles = [[get(dj, di) for di in (-1, 0, 1)] for dj in (-1, 0, 1)]
        out = []
        for south, own, north in ([row[1] for row in tiles], [edge_of_tile(*row) for row in tiles]):
            outer = jnp.where(rows_id == SUB - 1, south, north)
            below = roll_rows(jnp.where(rows_id == SUB - 1, south, own), 1)
            below_outer = roll_rows(jnp.where(rows_id == SUB - 2, south, own), 1)
            out.append(
                (operation(own, at(own, -1)), operation(outer, at(outer, -1)), operation(own, below), operation(outer, below_outer))
            )
        return out

    def outer_and_own(own, outer):
        return Many([row_of(outer, SUB - 1)] + [row_of(own, row) for row in range(SUB)] + [row_of(outer, 0)])

    wet_counts, differences = [], []

    def beside_setup():
        wet_counts.extend(pairs(lambda dj, di: near(dj, di, lambda j, i: count_s[j, i]), jnp.minimum))

    def beside_sum(k):
        if k == ITERS - 1:
            prepare(groups)
        differences.append(pairs(lambda dj, di: block(dj, di, lambda j, i: r_s[k, j, i]), lambda a, b: a - b))

    weights = surface_solve(levels, ny, nx, read, count_s, face_s, r_s, beside_setup, beside_sum)

    def weighted(parts):
        total_of = parts[0] * weights[0]
        for part, weight in zip(parts[1:], weights[1:]):
            total_of = total_of + part * weight
        return total_of

    slopes = [[weighted([d[kind][n] for d in differences]) for n in range(4)] for kind in range(2)]
    eta_ref[...] = weighted([r_s[k, my_j, my_i] for k in range(ITERS)])
    out = [pltpu.make_async_copy(eta_ref, eta_hbm, sems.at[0])]
    out[0].start()

    def adjoint(parts):
        u, v, su, sv = (joined([data[part][n] for part in parts]) for n in range(4))
        v_bar, u_bar, from_v_bar, from_u_bar, u_across, v_across = (
            joined([made[part][n] for part in parts]) for n in range(len(MADE_SIZES))
        )

        def each(values):
            return Many([values[part] for part in parts for _ in range(SUB + 2)], len(parts))

        def around(of, n):
            return joined([outer_and_own(*of[1 if part == groups else 0][n : n + 2]) for part in parts])

        wet_u, wet_v = around(wet_counts, 0) > each(numbers), around(wet_counts, 2) > each(numbers)
        u_cot = su + (around(slopes, 0) * each(thick)).where(wet_u, zero)
        v_cot = sv + (around(slopes, 2) * each(thick)).where(wet_v, zero)
        a, b = (u_cot * (0.5 * ADVECT)).where(wet_u, zero), (v_cot * (0.5 * ADVECT)).where(wet_v, zero)
        av, bu = a * v_bar, b[1:9] * u_bar
        au, bv = a[1:9] * u[2:10], b * v[:-1]
        to_v_bar, to_u_bar = a[:-1] * from_v_bar, b[1:] * from_u_bar
        near_u, near_v = to_u_bar[:-1] + to_u_bar[1:], to_v_bar[1:] + to_v_bar[:-1]
        du = u_cot[1:9] - a[1:9] * u_across + av[2:] - av[:-2] + near_u
        du = du + au.at(1) + (near_u - au).at(-1)
        dv = v_cot[1:9] - b[1:9] * v_across + bv[2:] - bv[:-2] + near_v
        dv = dv + (near_v + bu).at(1) - bu.at(-1)
        return list(zip(du.split(), dv.split()))

    for part in range(groups):
        prepare(part)
    flow = {}
    for parts in ADJOINT_PARTS:
        flow.update(zip(parts, adjoint(parts)))
    edge_u, edge_v = (outer_columns(part) for part in flow[groups])
    for q in range(groups):
        du, dv = flow[q]
        store_rows(du_ref, q, levels, merge_edges(du, edge_u, q) + load_rows(dut_ref, q, levels))
        store_rows(dv_ref, q, levels, merge_edges(dv, edge_v, q) + load_rows(dvt_ref, q, levels))
        part = pl.ds(q * SUB * SUB, min(SUB, levels - q * SUB) * SUB)
        for target, source in ((du_hbm, du_ref), (dv_hbm, dv_ref)):
            out.append(pltpu.make_async_copy(source.at[part, :], target.at[part, :], sems.at[len(out)]))
            out[-1].start()
    for copy in out:
        copy.wait()


def swaps(mesh_shape, along, parity):
    ny, nx = mesh_shape
    pairs = []
    for j in range(ny):
        for i in range(nx):
            k, size = (j, ny) if along == "y" else (i, nx)
            other = k + 1 if k % 2 == parity else k - 1
            if 0 <= other < size:
                pairs.append((j * nx + i, other * nx + i if along == "y" else j * nx + other))
    return pairs


def call(kernel, outs, args, scratch=(), flops=0, size=0, far_in=False, far_out=(), limit=48):
    near, far = pl.BlockSpec(memory_space=pltpu.VMEM), pl.BlockSpec(memory_space=pltpu.HBM)
    outs = [out if isinstance(out, jax.ShapeDtypeStruct) else jax.ShapeDtypeStruct(out, jnp.float32) for out in outs]
    return pl.pallas_call(
        kernel,
        out_shape=outs,
        in_specs=[far if far_in else near] * len(args),
        out_specs=[far if n in far_out else near for n in range(len(outs))],
        scratch_shapes=list(scratch),
        compiler_params=pltpu.CompilerParams(vmem_limit_bytes=limit * 1024 * 1024),
        cost_estimate=pl.CostEstimate(flops=flops, bytes_accessed=size, transcendentals=0),
    )(*args)


def on_device(shape, u, v, t, count, su, sv, st, elev):
    ny, nx = shape
    levels = u.shape[0]
    groups = group_count(levels)
    flat = (levels * SUB, LANES)
    room = (groups * SUB * SUB, LANES)
    u, v, t, su, sv, st = (field.reshape(flat) for field in (u, v, t, su, sv, st))
    peers = ny * nx // 2
    row_packet = ((N_SLOTS * groups + 1) * SUB, LANES)
    column_packet = ((SUB + 1) * SUB, LANES)
    chunk = (peers, 1, CHUNK_ROW + groups * TILE + len(CORNERS) // CORNERS_PER_ROW * LANES)
    tile = (SUB, LANES)
    (chunks,) = call(
        functools.partial(chunk_kernel, levels, peers),
        [chunk],
        (u, v, su, sv, count, elev),
        scratch=[pltpu.VMEM(flat, jnp.float32)] * 4
        + [pltpu.VMEM(tile, count.dtype), pltpu.VMEM(tile, jnp.float32), pltpu.SemaphoreType.DMA((6,))],
        flops=1 << 20,
        size=1 << 21,
        far_in=True,
        limit=60,
    )
    y1, y2, xp = call(
        functools.partial(packet_kernel, levels),
        [row_packet, row_packet, column_packet],
        (u, v, t, su, sv, st, count),
        flops=1 << 20,
        size=1 << 21,
    )
    axes = ("ty", "y", "core")
    ga = lax.all_to_all(chunks, ("ty", "y"), 0, 0)
    x1 = lax.ppermute(xp, axes, swaps(shape, "x", 0))
    x2 = lax.ppermute(xp, axes, swaps(shape, "x", 1))
    y1 = lax.ppermute(y1, axes, swaps(shape, "y", 0))
    y2 = lax.ppermute(y2, axes, swaps(shape, "y", 1))
    dtx, du_t, edge = call(
        functools.partial(column_kernel, levels),
        [room, room, (len(FLOW_FIELDS) * SUB * SUB, LANES)],
        (u, v, t, st, su, sv, count, x1, x2),
        flops=1 << 22,
        size=1 << 21,
    )
    ga, y1, y2, dtx = lax.optimization_barrier((ga, y1, y2, dtx))
    gb = lax.ppermute(ga, axes, swaps(shape, "x", 0))
    dt, dv_t, made, outer = call(
        functools.partial(row_kernel, levels, ny),
        [flat, room, (groups * MADE_ROWS * SUB, LANES), (len(OUTER_ROWS) * SUB, LANES)],
        (u, v, t, st, count, y1, y2, dtx),
        scratch=(pltpu.VMEM(room, jnp.float32), pltpu.SemaphoreType.DMA((groups,))),
        flops=1 << 22,
        size=1 << 21,
        far_out=(0,),
    )
    grid = pltpu.VMEM((ny, nx, SUB, LANES), jnp.float32)
    faces, residuals = (pltpu.VMEM((n, ny, nx, SUB, LANES), jnp.float32) for n in (7, ITERS))
    du, dv, eta = call(
        functools.partial(flow_kernel, levels, ny, nx),
        [flat, flat, (SUB, LANES)],
        (u, v, su, sv, ga, gb, y1, y2, edge, outer, made, du_t, dv_t),
        far_out=(0, 1, 2),
        scratch=(grid, faces, residuals)
        + tuple(pltpu.VMEM(shape, jnp.float32) for shape in (tile, room, room))
        + (pltpu.SemaphoreType.DMA((2 * groups + 1,)),),
        flops=1 << 23,
        size=1 << 22,
    )
    whole = (levels, SUB, LANES)
    return du.reshape(whole), dv.reshape(whole), dt.reshape(whole), eta


def solution(mesh):
    ny, nx = mesh.shape["ty"], mesh.shape["tx"]
    split = Mesh(mesh.devices.reshape(ny, nx // 2, 2), ("ty", "y", "core"))
    deep, flat = P(None, "ty", ("y", "core")), P("ty", ("y", "core"))
    return jax.shard_map(
        functools.partial(on_device, (ny, nx)),
        mesh=split,
        in_specs=(deep, deep, deep, flat, deep, deep, deep, flat),
        out_specs=(deep, deep, deep, flat),
        check_vma=False,
    )
```

```python
import functools

import jax
import jax.numpy as jnp
from jax import lax
from jax.experimental import pallas as pl
from jax.experimental.pallas import tpu as pltpu
from jax.sharding import Mesh, PartitionSpec as P

ITERS = 4
ADVECT = 0.1
GRAVITY_DT = 0.1

SUB = 8
LANES = 128
SEG = 32
FIELDS = ("u", "v", "t", "st", "su", "sv")
BAND_BLOCKS = 32
ADJOINT_PARTS = ((4, 0), (1, 2), (3,))
FLOW_FIELDS = ("u", "v", "su", "sv")
FLOW_ROWS = {"u": (-2, 8), "v": (-1, 9), "su": (-1, 8), "sv": (-1, 8)}
OUTER_ROWS = tuple((n, r) for n in FLOW_FIELDS for r in range(FLOW_ROWS[n][0], FLOW_ROWS[n][1] + 1) if not 0 <= r < 8)
MADE_SIZES = (10, 8, 9, 9, 8, 8)
MADE_ROWS = sum(MADE_SIZES)
SOUTH_SLOTS = {("u", -2): 0, ("u", -1): 1, ("v", -1): 2, ("t", -2): 3, ("t", -1): 4, ("st", -2): 5, ("st", -1): 6}
SOUTH_SLOTS.update({("su", -1): 7, ("sv", -1): 8})
NORTH_SLOTS = {("u", 8): 0, ("v", 8): 1, ("v", 9): 2, ("t", 8): 3, ("st", 8): 5, ("st", 9): 6, ("su", 8): 7, ("sv", 8): 8}
N_SLOTS = 9
TILE = SUB * LANES
CHUNK_LOAD = TILE
CHUNK_ROW = 2 * TILE
WEST_LEVELS = LANES // SUB
CORNERS_PER_ROW = 4
CORNERS = (("u", 6, 0), ("u", 7, 0), ("u", 7, 1), ("su", 7, 0), ("v", 7, 127), ("u", 7, 127))
CORNERS += (("v", 0, 127), ("v", 1, 127), ("v", 0, 126), ("sv", 0, 127), ("v", 0, 0), ("u", 0, 0))
CORNER_PLACES = {
    ("u", -2): (("se", 0, 24),),
    ("u", -1): (("se", 1, 24), ("se", 2, 25), ("sw", 5, 7)),
    ("su", -1): (("se", 3, 24),),
    ("v", -1): (("sw", 4, 7),),
    ("v", 8): (("nw", 6, 7), ("nw", 8, 6), ("ne", 10, 24)),
    ("u", 8): (("ne", 11, 24),),
    ("v", 9): (("nw", 7, 7),),
    ("sv", 8): (("nw", 9, 7),),
}


def lane_ids():
    return lax.broadcasted_iota(jnp.int32, (SUB, LANES), 1)


def row_ids():
    return lax.broadcasted_iota(jnp.int32, (SUB, LANES), 0)


def roll_lanes(value, amount):
    amount %= LANES
    return value if amount == 0 else pltpu.roll(value, amount, 1)


def roll_rows(value, amount):
    amount %= SUB
    return value if amount == 0 else pltpu.roll(value, amount, 0)


def at(value, shift):
    return roll_lanes(value, -shift)


def row_of(tile, row):
    return jnp.broadcast_to(tile[row : row + 1, :], (SUB, LANES))


def group_count(levels):
    return -(-levels // SUB)


def load_group(ref, row, q, levels):
    first = min(q * SUB, levels - SUB)
    value = ref[pl.ds(first * SUB + row, SUB, stride=SUB), :]
    return roll_rows(value, first - q * SUB)


def store_group(ref, row, q, levels, value):
    count = min(SUB, levels - q * SUB)
    ref[pl.ds(q * SUB * SUB + row, count, stride=SUB), :] = value[:count]


def level_numbers(groups):
    rows = row_ids()
    numbers = [(rows + q * SUB).astype(jnp.float32) for q in range(groups)]
    return numbers + [(rows + (lane_ids() >> 5) * SUB).astype(jnp.float32)]


def edge_of_tile(west, centre, east):
    lanes = lane_ids()
    out = jnp.where(lanes < 8, roll_lanes(west, 8), roll_lanes(centre, 8))
    out = jnp.where(lanes >= 16, roll_lanes(centre, 24), out)
    out = jnp.where(lanes >= 24, roll_lanes(east, 24), out)
    out = jnp.where(lanes < SEG, out, roll_lanes(out, SEG))
    return jnp.where(lanes < 2 * SEG, out, roll_lanes(out, 2 * SEG))


def chunk_kernel(
    levels, peers, u_hbm, v_hbm, su_hbm, sv_hbm, count_hbm, elev_hbm, chunk_ref,
    u_ref, v_ref, su_ref, sv_ref, count_ref, elev_ref, sems,
):
    pairs = (
        (count_hbm, count_ref), (su_hbm, su_ref), (sv_hbm, sv_ref), (elev_hbm, elev_ref), (u_hbm, u_ref), (v_hbm, v_ref),
    )
    copies = [pltpu.make_async_copy(source, target, sems.at[n]) for n, (source, target) in enumerate(pairs)]
    for copy in copies:
        copy.start()
    groups = group_count(levels)
    lanes, rows = lane_ids(), row_ids()
    refs = {"u": u_ref, "v": v_ref, "su": su_ref, "sv": sv_ref}
    for copy in copies:
        copy.wait()
    count = count_ref[...].astype(jnp.float32)
    zero = jnp.zeros((SUB, LANES), jnp.float32)

    wet_u = jnp.where(lanes == 0, 0.0, jnp.minimum(count, roll_lanes(count, 1)))
    wet_v = jnp.where(rows == 0, 0.0, jnp.minimum(count, roll_rows(count, 1)))
    col_u, col_v = [zero] * 4, [zero] * 4
    west = [zero] * (levels // WEST_LEVELS + 1)
    for k in range(levels):
        su_level = su_ref[k * SUB : (k + 1) * SUB, :]
        col_u[k % 4] = col_u[k % 4] + jnp.where(wet_u > float(k), su_level, 0.0)
        col_v[k % 4] = col_v[k % 4] + jnp.where(wet_v > float(k), sv_ref[k * SUB : (k + 1) * SUB, :], 0.0)
        n = k // WEST_LEVELS
        there = lanes == rows + k % WEST_LEVELS * SUB
        west[n] = jnp.where(there, jnp.broadcast_to(su_level[:, 0:1], (SUB, LANES)), west[n])
    col_u, col_v = ((col[0] + col[1]) + (col[2] + col[3]) for col in (col_u, col_v))
    load = elev_ref[...] + GRAVITY_DT * (at(col_u, 1) - col_u + roll_rows(col_v, -1) - col_v)

    corners = [zero] * (len(CORNERS) // CORNERS_PER_ROW)
    for place, (name, row, column) in enumerate(CORNERS):
        n, base = place // CORNERS_PER_ROW, place % CORNERS_PER_ROW * SUB
        for q in range(groups):
            value = load_group(refs[name], row, q, levels)[:, column : column + 1]
            there = lanes == SEG * q + base + SUB - 1 - rows
            corners[n] = jnp.where(there, jnp.broadcast_to(value, (SUB, LANES)), corners[n])

    def in_a_row(tile):
        return jnp.broadcast_to(jnp.sum(tile, axis=0, keepdims=True), (SUB, LANES))

    tiles = [count, load] + [load_group(sv_ref, 0, q, levels) for q in range(groups)]
    for n, part in enumerate(west):
        tiles[-1] = jnp.where(rows == SUB - len(west) + n, in_a_row(part), tiles[-1])
    last = zero
    for n, part in enumerate(corners):
        last = jnp.where(rows == n, in_a_row(part), last)
    tiles = [tile.reshape(1, TILE) for tile in tiles + [last]]
    tiles[-1] = tiles[-1][:, : len(corners) * LANES]

    def put(peer, carry):
        first = 0
        for tile in tiles:
            chunk_ref[peer, :, first : first + tile.shape[1]] = tile
            first += tile.shape[1]
        return carry

    lax.fori_loop(0, peers, put, 0, unroll=4)


def packet_kernel(levels, u_ref, v_ref, t_ref, su_ref, sv_ref, st_ref, count_ref, y1_ref, y2_ref, x_ref):
    groups = group_count(levels)
    lanes = lane_ids()
    zero = jnp.zeros((SUB, LANES), jnp.float32)
    count = count_ref[...].astype(jnp.float32)
    even = lax.axis_index("ty") % 2 == 0
    refs = {"u": u_ref, "v": v_ref, "t": t_ref, "st": st_ref, "su": su_ref, "sv": sv_ref}
    loaded = {}
    for name in FIELDS:
        for row in range(SUB):
            for q in range(groups):
                loaded[name, row, q] = load_group(refs[name], row, q, levels)

    for slot in range(N_SLOTS):
        upper = [(name, row + SUB) for (name, row), place in SOUTH_SLOTS.items() if place == slot]
        lower = [(name, row - SUB) for (name, row), place in NORTH_SLOTS.items() if place == slot]
        for q in range(groups):
            to_north = loaded[(*upper[0], q)]
            to_south = loaded[(*lower[0], q)] if lower else zero
            place = pl.ds((slot * groups + q) * SUB, SUB)
            y1_ref[place, :] = jnp.where(even, to_north, to_south)
            y2_ref[place, :] = jnp.where(even, to_south, to_north)
    y1_ref[N_SLOTS * groups * SUB :, :] = count
    y2_ref[N_SLOTS * groups * SUB :, :] = count

    for row in range(SUB):
        packet = zero
        for field, name in enumerate(FIELDS):
            for q in range(groups):
                lane = SEG * q + 4 * field
                packet = jnp.where((lanes >= lane) & (lanes < lane + 4), roll_lanes(loaded[name, row, q], lane + 2), packet)
        x_ref[row * SUB : (row + 1) * SUB, :] = packet
    x_ref[SUB * SUB :, :] = count


def joined(parts):
    return Many([item for part in parts for item in part.items], len(parts))


class Many:
    def __init__(self, items, parts=1):
        self.items = list(items)
        self.parts = parts

    def __getitem__(self, where):
        if not isinstance(where, slice):
            return self.items[where]
        rows = len(self.items) // self.parts
        return Many([item for n in range(self.parts) for item in self.items[n * rows : (n + 1) * rows][where]], self.parts)

    def __len__(self):
        return len(self.items)

    def split(self):
        rows = len(self.items) // self.parts
        return [Many(self.items[n * rows : (n + 1) * rows]) for n in range(self.parts)]

    def apply(self, operation, *others):
        others = [other.items if isinstance(other, Many) else [other] * len(self) for other in others]
        assert all(len(other) == len(self) for other in others)
        return Many([operation(*parts) for parts in zip(self.items, *others)], self.parts)

    def __add__(self, other):
        return self.apply(lambda a, b: a + b, other)

    def __sub__(self, other):
        return self.apply(lambda a, b: a - b, other)

    def __mul__(self, other):
        return self.apply(lambda a, b: a * b, other)

    def __gt__(self, other):
        return self.apply(lambda a, b: a > b, other)

    def at(self, shift):
        return self.apply(lambda a: at(a, shift))

    def rolled(self, amount):
        return self.apply(lambda a: roll_lanes(a, amount))

    def minimum(self, other):
        return self.apply(jnp.minimum, other)

    def where(self, mask, other):
        return self.apply(lambda a, m, b: jnp.where(m, a, b), mask, other)


def edges_of_groups(parts):
    lanes = lane_ids()
    out = parts[0].rolled(8)
    for q in range(1, len(parts)):
        out = parts[q].rolled(SEG * q + 8).where(lanes >= SEG * q, out)
    return out.rolled(16).where((lanes & (SEG - 1)) >= 16, out)


def insert_sides(edge, west, east, field):
    place = lane_ids() & (SEG - 1)
    edge = west.rolled(6 - 4 * field).where((place == 6) | (place == 7), edge)
    return east.rolled(22 - 4 * field).where((place == 24) | (place == 25), edge)


def outer_columns(edge):
    return edge.rolled(-16).where((lane_ids() & (SEG - 1)) < 8, edge)


def merge_edges(values, outer, q):
    lanes = lane_ids()
    return outer.rolled(-(SEG * q + 8)).where((lanes < 2) | (lanes >= LANES - 2), values)


def load_rows(ref, q, levels):
    return Many(load_group(ref, row, q, levels) for row in range(SUB))


def store_rows(ref, q, levels, values):
    for row in range(SUB):
        store_group(ref, row, q, levels, values[row])


def rows_of(tiles, first, last):
    return Many(row_of(tiles[row // SUB + 1], row % SUB) for row in range(first, last + 1))


def slot_reader(y1_ref, y2_ref, groups):
    even = lax.axis_index("ty") % 2 == 0

    def read(name, row, q):
        slot = (SOUTH_SLOTS if row < 0 else NORTH_SLOTS)[name, row]
        place = pl.ds((slot * groups + q) * SUB, SUB)
        one, two = y1_ref[place, :], y2_ref[place, :]
        return jnp.where(even, two, one) if row < 0 else jnp.where(even, one, two)

    def counts():
        place = pl.ds(N_SLOTS * groups * SUB, SUB)
        one, two = y1_ref[place, :], y2_ref[place, :]
        return jnp.where(even, two, one), jnp.where(even, one, two)

    return read, counts


def side_reader(x1_ref, x2_ref):
    even = lax.axis_index("core") % 2 == 0

    def read(row):
        place = pl.ds(row * SUB, SUB)
        one, two = x1_ref[place, :], x2_ref[place, :]
        return jnp.where(even, two, one), jnp.where(even, one, two)

    return read


def face_values(t0, t_before, t_after, t_before2):
    return ((t0 + t_before) * 7.0 - (t_after + t_before2)) * (1.0 / 12.0)


def edge_rows(ref, west, east, levels, groups, name):
    own = edges_of_groups([load_rows(ref, q, levels) for q in range(groups)])
    return insert_sides(own, west, east, FIELDS.index(name))


def column_kernel(
    levels, u_ref, v_ref, t_ref, st_ref, su_ref, sv_ref, count_ref, x1_ref, x2_ref, dt_ref, du_ref, edge_ref
):
    groups = group_count(levels)
    read_sides = side_reader(x1_ref, x2_ref)
    numbers = level_numbers(groups)
    zero = jnp.zeros((SUB, LANES), jnp.float32)
    count = count_ref[...].astype(jnp.float32)
    count_west, count_east = read_sides(SUB)
    count_edge = edge_of_tile(count_west, count, count_east)

    def counts(tile):
        return tuple(rows_of((None, part, None), 0, 7) for part in (tile, jnp.minimum(tile, at(tile, -1))))

    def along(level, wet, wet_u, u, t, st):
        cell = (st * -ADVECT).where(wet > level, zero)
        flux = (cell.at(-1) - cell).where(wet_u > level, zero)
        back = u * flux
        face = face_values(t, t.at(-1), t.at(1), t.at(-2))
        return ((back + back.at(1)) * 7.0 - (back.at(-1) + back.at(2))) * (1.0 / 12.0), flux * face

    sides = [read_sides(row) for row in range(SUB)]
    west, east = Many(side[0] for side in sides), Many(side[1] for side in sides)
    u, t, st = (
        edge_rows(ref, west, east, levels, groups, name) for name, ref in (("u", u_ref), ("t", t_ref), ("st", st_ref))
    )
    edge_t, edge_u = (outer_columns(part) for part in along(numbers[groups], *counts(count_edge), u, t, st))
    own = counts(count)
    for q in range(groups):
        st = load_rows(st_ref, q, levels)
        from_x, to_u = along(numbers[q], *own, load_rows(u_ref, q, levels), load_rows(t_ref, q, levels), st)
        store_rows(dt_ref, q, levels, st + merge_edges(from_x, edge_t, q))
        store_rows(du_ref, q, levels, merge_edges(to_u, edge_u, q))
    flow = (u,) + tuple(
        edge_rows(ref, west, east, levels, groups, name) for name, ref in (("v", v_ref), ("su", su_ref), ("sv", sv_ref))
    )
    for n, rows in enumerate(flow):
        for row in range(SUB):
            edge_ref[(n * SUB + row) * SUB : (n * SUB + row + 1) * SUB, :] = rows[row]


def turns(ny):
    first_row = (lax.axis_index("ty") * SUB).astype(jnp.float32)
    scale = 0.5 / (ny * SUB)
    turn_u = Many(0.25 + (first_row + (row + 0.5)) * scale for row in range(-1, 8))
    return turn_u, Many(-0.25 - (first_row + row) * scale for row in range(0, 9))


def prepared(u, v, turn_u, turn_v):
    v_pair, u_pair = v[:-1] + v[1:], u[2:10] + u[1:9]
    return (
        (v_pair + v_pair.at(-1)) * 0.25,
        (u_pair + u_pair.at(1)) * 0.25,
        (u[:-2] - u[2:]) * 0.25 + turn_u,
        (v[1:10].at(-1) - v[1:10].at(1)) * 0.25 + turn_v,
        u[2:10].at(1) - u[2:10].at(-1),
        v[2:10] - v[0:8],
    )


def row_kernel(
    levels, ny, u_ref, v_ref, t_ref, st_ref, count_ref, y1_ref, y2_ref, dtx_ref, dt_hbm, dv_ref, made_ref, edge_ref, dt_ref, sems
):
    groups = group_count(levels)
    read_row, read_counts = slot_reader(y1_ref, y2_ref, groups)
    numbers = level_numbers(groups)
    zero = jnp.zeros((SUB, LANES), jnp.float32)
    count = count_ref[...].astype(jnp.float32)
    count_south, count_north = read_counts()
    counts = rows_of((count_south, count, count_north), -2, 9)
    counts_v = counts[1:].minimum(counts[:-1])
    out = []
    for n, (name, row) in enumerate(OUTER_ROWS):
        (edge,) = edges_of_groups([Many([read_row(name, row, q)]) for q in range(groups)]).items
        edge_ref[n * SUB : (n + 1) * SUB, :] = edge
    for q in range(groups):
        level = numbers[q]

        def rows(name, ref, first, last):
            south = [read_row(name, row, q) for row in range(first, 0)]
            north = [read_row(name, row, q) for row in range(SUB, last + 1)]
            return Many(south + load_rows(ref, q, levels).items + north)

        t, st, v = rows("t", t_ref, -2, 8), rows("st", st_ref, -2, 9), rows("v", v_ref, -1, 9)
        made = prepared(rows("u", u_ref, -2, 8), v, *turns(ny))
        for n, value in enumerate(value for values in made for value in values.items):
            place = pl.ds((q * MADE_ROWS + n) * SUB, SUB)
            made_ref[place, :] = value
        cell = (st * -ADVECT).where(counts > level, zero)
        flux = (cell[:-1] - cell[1:]).where(counts_v > level, zero)
        back = v * flux
        from_y = ((back[1:9] + back[2:10]) * 7.0 - (back[0:8] + back[3:11])) * (1.0 / 12.0)
        to_v = flux[1:9] * face_values(t[2:10], t[1:9], t[3:11], t[0:8])
        store_rows(dt_ref, q, levels, load_rows(dtx_ref, q, levels) + from_y)
        store_rows(dv_ref, q, levels, to_v)
        part = pl.ds(q * SUB * SUB, min(SUB, levels - q * SUB) * SUB)
        out.append(pltpu.make_async_copy(dt_ref.at[part, :], dt_hbm.at[part, :], sems.at[q]))
        out[-1].start()
    for copy in out:
        copy.wait()


def total(value):
    return jnp.sum(value, axis=(0, 1), keepdims=True)


def surface_solve(levels, ny, nx, read, count_ref, face_ref, r_refs, beside_setup, beside_sum):
    groups = group_count(levels)
    lanes, rows = lane_ids(), row_ids()
    numbers = level_numbers(groups)
    zero = jnp.zeros((SUB, LANES), jnp.float32)
    band = max(1, min(ny, BAND_BLOCKS // nx))
    while ny % band:
        band -= 1
    cells = [(dj, i) for dj in range(band) for i in range(nx)]

    def loop(body, init=0):
        if ny * nx <= 32:
            for j in range(0, ny, band):
                init = body(j, init)
            return init
        return lax.fori_loop(0, ny // band, lambda step, carry: body(step * band, carry), init)

    def get(ref, j):
        return Many(ref[j + dj, i] for dj, i in cells)

    def put(ref, j, values):
        for (dj, i), value in zip(cells, values.items):
            ref[j + dj, i] = value

    def beside(values, step):
        return Many(values[dj * nx + min(max(i + step, 0), nx - 1)] for dj, i in cells)

    def below(ref, j, values):
        outside = [ref[max(j - 1, 0) if isinstance(j, int) else jnp.maximum(j - 1, 0), i] for i in range(nx)]
        return Many(outside + values.items[:-nx])

    def above(ref, j, values):
        top = min(j + band, ny - 1) if isinstance(j, int) else jnp.minimum(j + band, ny - 1)
        outside = [ref[top, i] for i in range(nx)]
        return Many(values.items[nx:] + outside)

    def west_of(values):
        return beside(values, -1).where(lanes == LANES - 1, values).rolled(1)

    def east_of(values):
        return beside(values, 1).where(lanes == 0, values).rolled(-1)

    def south_of(ref, j, values):
        return below(ref, j, values).where(rows == SUB - 1, values).apply(lambda a: roll_rows(a, 1))

    def north_of(ref, j, values):
        return above(ref, j, values).where(rows == 0, values).apply(lambda a: roll_rows(a, -1))

    def depth(wet):
        return wet.apply(lambda m: m * (m * (GRAVITY_DT * 0.5 / levels) + GRAVITY_DT * (1.0 - 0.5 / levels)))

    def gather(j, carry):
        put(count_ref, j, Many(read(j + dj, i, 0) for dj, i in cells))
        return carry

    loop(gather)

    def faces(j, carry):
        count = get(count_ref, j)
        wet_u, wet_v = count.minimum(west_of(count)), count.minimum(south_of(count_ref, j, count))
        first_column = [(lanes == 0) if i == 0 else (lanes < 0) for dj, i in cells]
        first_row = [(rows == 0) & (j + dj == 0) for dj, i in cells]
        wet_u = Many([zero] * len(cells)).where(Many(first_column), wet_u)
        wet_v = Many([zero] * len(cells)).where(Many(first_row), wet_v)
        put(face_ref.at[0], j, depth(wet_u))
        put(face_ref.at[1], j, depth(wet_v))
        wet_west = wet_u.apply(lambda a: jnp.broadcast_to(a[:, 0:1], (SUB, LANES)))
        souths = [Many(read(j + dj, i, CHUNK_ROW + q * TILE) for dj, i in cells) for q in range(groups)]
        inside = Many([zero] * len(cells))
        for n in range(levels // WEST_LEVELS + 1):
            reach = jnp.where((lanes & (SUB - 1)) == rows, (lanes >> 3) + n * WEST_LEVELS, levels).astype(jnp.float32)
            west = souths[-1].apply(lambda a: row_of(a, SUB - 1 - levels // WEST_LEVELS + n))
            inside = inside + west.where(wet_west > reach, zero)
        col_u = inside.apply(lambda a: jnp.broadcast_to(jnp.sum(a, axis=1, keepdims=True), (SUB, LANES)))
        put(face_ref.at[4], j, col_u * GRAVITY_DT)
        wet_south = wet_v.apply(lambda a: row_of(a, 0))
        col_v = Many([zero] * len(cells))
        for q in range(groups):
            col_v = col_v + souths[q].where(wet_south > numbers[q], zero)
        col_v = col_v.apply(lambda a: jnp.broadcast_to(jnp.sum(a, axis=0, keepdims=True), (SUB, LANES)))
        put(face_ref.at[5], j, col_v * GRAVITY_DT)
        return carry

    loop(faces)
    beside_setup()

    def start(j, carry):
        load = Many(read(j + dj, i, CHUNK_LOAD) for dj, i in cells)
        col_u, col_v = get(face_ref.at[4], j), get(face_ref.at[5], j)
        depth_u, depth_v = get(face_ref.at[0], j), get(face_ref.at[1], j)
        last_column = Many((lanes == LANES - 1) if i + 1 < nx else (lanes < 0) for dj, i in cells)
        at_end = Many((lanes == LANES - 1) if i + 1 == nx else (lanes < 0) for dj, i in cells)
        last_row = Many((rows == SUB - 1) & (j + dj + 1 < ny) for dj, i in cells)
        at_top = Many((rows == SUB - 1) & (j + dj + 1 == ny) for dj, i in cells)
        none = Many([zero] * len(cells))
        load = load - col_u.where(lanes == 0, zero) - col_v.where(rows == 0, zero)
        load = load + beside(col_u, 1).where(last_column, none) + above(face_ref.at[5], j, col_v).where(last_row, none)
        depth_east = none.where(at_end, east_of(depth_u))
        depth_north = none.where(at_top, north_of(face_ref.at[1], j, depth_v))
        put(face_ref.at[2], j, depth_east)
        put(face_ref.at[3], j, depth_north)
        put(face_ref.at[6], j, (depth_u + depth_east) + (depth_v + depth_north) + 1.0)
        put(r_refs.at[0], j, load)
        return carry

    def gathered(partial, values):
        items = list(values.items)
        while len(items) > 1:
            items = [a + b for a, b in zip(items[::2], items[1::2])] + items[len(items) // 2 * 2 :]
        return partial + items[0]

    loop(start)

    def products(k):
        r_ref = r_refs.at[k]

        def body(j, carry):
            r = get(r_ref, j)
            image = r * get(face_ref.at[6], j) - get(face_ref.at[0], j) * west_of(r) - get(face_ref.at[2], j) * east_of(r)
            image = image - get(face_ref.at[1], j) * south_of(r_ref, j, r)
            image = image - get(face_ref.at[3], j) * north_of(r_ref, j, r)
            put(face_ref.at[4], j, image)
            return gathered(carry[0], r * r), gathered(carry[1], r * image)

        return [total(part) for part in loop(body, (zero, zero))]

    norm, product = products(0)
    beside_sum(0)
    step = norm / product
    steps, ratios = [step], []

    for k in range(ITERS - 1):

        def advance(j, carry):
            image = get(face_ref.at[4], j)
            if k > 0:
                image = image + get(face_ref.at[5], j) * ratio
            if k + 2 < ITERS:
                put(face_ref.at[5], j, image)
            put(r_refs.at[k + 1], j, get(r_refs.at[k], j) - image * step)
            return carry

        loop(advance)
        new, product = products(k + 1)
        beside_sum(k + 1)
        ratio = new / norm
        step = new / (product - ratio * new / step)
        norm = new
        steps.append(step)
        ratios.append(ratio)

    weights = [steps[-1]]
    for k in reversed(range(ITERS - 1)):
        weights.append(steps[k] + ratios[k] * weights[-1])
    weights.reverse()
    return weights


def flow_kernel(
    levels, ny, nx, u_ref, v_ref, su_ref, sv_ref, ga_ref, gb_ref, y1_ref, y2_ref, edge_ref, outer_ref, made_ref, dut_ref, dvt_ref,
    du_hbm, dv_hbm, eta_hbm, count_s, face_s, r_s, eta_ref, du_ref, dv_ref, sems,
):
    groups = group_count(levels)
    lanes, rows_id = lane_ids(), row_ids()
    core = lax.axis_index("core")
    my_j = lax.axis_index("ty")
    my_i = lax.axis_index("y") * 2 + core
    numbers = level_numbers(groups)
    thick = [1.0 + number * (1.0 / levels) for number in numbers]
    read_row, _ = slot_reader(y1_ref, y2_ref, groups)
    zero = jnp.zeros((SUB, LANES), jnp.float32)

    def read(j, i, first):
        where = (j * (nx // 2) + i // 2, slice(None), pl.ds(first, TILE))
        return jnp.where(core == i % 2, ga_ref[where].reshape(SUB, LANES), gb_ref[where].reshape(SUB, LANES))

    def read_corners(n, j, i):
        where = (j * (nx // 2) + i // 2, slice(None), pl.ds(CHUNK_ROW + groups * TILE + n * LANES, LANES))
        row = jnp.broadcast_to(jnp.where(core == i % 2, ga_ref[where], gb_ref[where]), (SUB, LANES))
        return pltpu.roll(row, LANES - SUB + 1, 1, stride=1, stride_axis=0)

    def block(dj, di, get):
        return get(jnp.clip(my_j + dj, 0, ny - 1), jnp.clip(my_i + di, 0, nx - 1))

    def near(dj, di, get):
        j, i = jnp.clip(my_j + dj, 0, ny - 1), jnp.clip(my_i + di, 0, nx - 1)
        inside = (my_j + dj >= 0) & (my_j + dj < ny) & (my_i + di >= 0) & (my_i + di < nx)
        return jnp.where(inside, get(j, i), 0.0)

    diagonal = {"se": (-1, 1), "sw": (-1, -1), "nw": (1, -1), "ne": (1, 1)}
    corner_tiles = {}
    for places in CORNER_PLACES.values():
        for which, value, _ in places:
            n = value // CORNERS_PER_ROW
            if (which, n) not in corner_tiles:
                corner_tiles[which, n] = near(*diagonal[which], functools.partial(read_corners, n))

    def insert_corners(edge, name, row):
        for which, value, target in CORNER_PLACES.get((name, row), ()):
            there = (lanes & (SEG - 1)) == target
            tile = corner_tiles[which, value // CORNERS_PER_ROW]
            edge = jnp.where(there, roll_lanes(tile, target - value % CORNERS_PER_ROW * SUB), edge)
        return edge

    def rows(name, ref, q, first, last):
        south = [read_row(name, row, q) for row in range(first, 0)]
        north = [read_row(name, row, q) for row in range(SUB, last + 1)]
        return Many(south + load_rows(ref, q, levels).items + north)

    def edges(name):
        first, last = FLOW_ROWS[name]
        n = FLOW_FIELDS.index(name)

        def register(row):
            if 0 <= row < SUB:
                return edge_ref[(n * SUB + row) * SUB : (n * SUB + row + 1) * SUB, :]
            place = OUTER_ROWS.index((name, row)) * SUB
            return insert_corners(outer_ref[place : place + SUB, :], name, row)

        return Many(register(row) for row in range(first, last + 1))

    refs = {"u": u_ref, "v": v_ref, "su": su_ref, "sv": sv_ref}
    data, made = {}, {}

    def prepare(part):
        if part == groups:
            data[part] = [edges(name) for name in FLOW_FIELDS]
            made[part] = prepared(*data[part][:2], *turns(ny))
            return
        data[part] = [rows(name, refs[name], part, *FLOW_ROWS[name]) for name in FLOW_FIELDS]
        made[part], n = [], part * MADE_ROWS
        for size in MADE_SIZES:
            made[part].append(Many(made_ref[k * SUB : (k + 1) * SUB, :] for k in range(n, n + size)))
            n += size

    def pairs(get, operation):
        tiles = [[get(dj, di) for di in (-1, 0, 1)] for dj in (-1, 0, 1)]
        out = []
        for south, own, north in ([row[1] for row in tiles], [edge_of_tile(*row) for row in tiles]):
            outer = jnp.where(rows_id == SUB - 1, south, north)
            below = roll_rows(jnp.where(rows_id == SUB - 1, south, own), 1)
            below_outer = roll_rows(jnp.where(rows_id == SUB - 2, south, own), 1)
            out.append(
                (operation(own, at(own, -1)), operation(outer, at(outer, -1)), operation(own, below), operation(outer, below_outer))
            )
        return out

    def outer_and_own(own, outer):
        return Many([row_of(outer, SUB - 1)] + [row_of(own, row) for row in range(SUB)] + [row_of(outer, 0)])

    wet_counts, differences = [], []

    def beside_setup():
        wet_counts.extend(pairs(lambda dj, di: near(dj, di, lambda j, i: count_s[j, i]), jnp.minimum))

    def beside_sum(k):
        if k == ITERS - 1:
            prepare(groups)
        differences.append(pairs(lambda dj, di: block(dj, di, lambda j, i: r_s[k, j, i]), lambda a, b: a - b))

    weights = surface_solve(levels, ny, nx, read, count_s, face_s, r_s, beside_setup, beside_sum)

    def weighted(parts):
        total_of = parts[0] * weights[0]
        for part, weight in zip(parts[1:], weights[1:]):
            total_of = total_of + part * weight
        return total_of

    slopes = [[weighted([d[kind][n] for d in differences]) for n in range(4)] for kind in range(2)]
    eta_ref[...] = weighted([r_s[k, my_j, my_i] for k in range(ITERS)])
    out = [pltpu.make_async_copy(eta_ref, eta_hbm, sems.at[0])]
    out[0].start()

    def adjoint(parts):
        u, v, su, sv = (joined([data[part][n] for part in parts]) for n in range(4))
        v_bar, u_bar, from_v_bar, from_u_bar, u_across, v_across = (
            joined([made[part][n] for part in parts]) for n in range(len(MADE_SIZES))
        )

        def each(values):
            return Many([values[part] for part in parts for _ in range(SUB + 2)], len(parts))

        def around(of, n):
            return joined([outer_and_own(*of[1 if part == groups else 0][n : n + 2]) for part in parts])

        wet_u, wet_v = around(wet_counts, 0) > each(numbers), around(wet_counts, 2) > each(numbers)
        u_cot = su + (around(slopes, 0) * each(thick)).where(wet_u, zero)
        v_cot = sv + (around(slopes, 2) * each(thick)).where(wet_v, zero)
        a, b = (u_cot * (0.5 * ADVECT)).where(wet_u, zero), (v_cot * (0.5 * ADVECT)).where(wet_v, zero)
        av, bu = a * v_bar, b[1:9] * u_bar
        au, bv = a[1:9] * u[2:10], b * v[:-1]
        to_v_bar, to_u_bar = a[:-1] * from_v_bar, b[1:] * from_u_bar
        near_u, near_v = to_u_bar[:-1] + to_u_bar[1:], to_v_bar[1:] + to_v_bar[:-1]
        du = u_cot[1:9] - a[1:9] * u_across + av[2:] - av[:-2] + near_u
        du = du + au.at(1) + (near_u - au).at(-1)
        dv = v_cot[1:9] - b[1:9] * v_across + bv[2:] - bv[:-2] + near_v
        dv = dv + (near_v + bu).at(1) - bu.at(-1)
        return list(zip(du.split(), dv.split()))

    for part in range(groups):
        prepare(part)
    flow = {}
    for parts in ADJOINT_PARTS:
        flow.update(zip(parts, adjoint(parts)))
    edge_u, edge_v = (outer_columns(part) for part in flow[groups])
    for q in range(groups):
        du, dv = flow[q]
        store_rows(du_ref, q, levels, merge_edges(du, edge_u, q) + load_rows(dut_ref, q, levels))
        store_rows(dv_ref, q, levels, merge_edges(dv, edge_v, q) + load_rows(dvt_ref, q, levels))
        part = pl.ds(q * SUB * SUB, min(SUB, levels - q * SUB) * SUB)
        for target, source in ((du_hbm, du_ref), (dv_hbm, dv_ref)):
            out.append(pltpu.make_async_copy(source.at[part, :], target.at[part, :], sems.at[len(out)]))
            out[-1].start()
    for copy in out:
        copy.wait()


def swaps(mesh_shape, along, parity):
    ny, nx = mesh_shape
    pairs = []
    for j in range(ny):
        for i in range(nx):
            k, size = (j, ny) if along == "y" else (i, nx)
            other = k + 1 if k % 2 == parity else k - 1
            if 0 <= other < size:
                pairs.append((j * nx + i, other * nx + i if along == "y" else j * nx + other))
    return pairs


def call(kernel, outs, args, scratch=(), flops=0, size=0, far_in=False, far_out=(), limit=48):
    near, far = pl.BlockSpec(memory_space=pltpu.VMEM), pl.BlockSpec(memory_space=pltpu.HBM)
    outs = [out if isinstance(out, jax.ShapeDtypeStruct) else jax.ShapeDtypeStruct(out, jnp.float32) for out in outs]
    return pl.pallas_call(
        kernel,
        out_shape=outs,
        in_specs=[far if far_in else near] * len(args),
        out_specs=[far if n in far_out else near for n in range(len(outs))],
        scratch_shapes=list(scratch),
        compiler_params=pltpu.CompilerParams(vmem_limit_bytes=limit * 1024 * 1024),
        cost_estimate=pl.CostEstimate(flops=flops, bytes_accessed=size, transcendentals=0),
    )(*args)


def on_device(shape, u, v, t, count, su, sv, st, elev):
    ny, nx = shape
    levels = u.shape[0]
    groups = group_count(levels)
    flat = (levels * SUB, LANES)
    room = (groups * SUB * SUB, LANES)
    u, v, t, su, sv, st = (field.reshape(flat) for field in (u, v, t, su, sv, st))
    peers = ny * nx // 2
    row_packet = ((N_SLOTS * groups + 1) * SUB, LANES)
    column_packet = ((SUB + 1) * SUB, LANES)
    chunk = (peers, 1, CHUNK_ROW + groups * TILE + len(CORNERS) // CORNERS_PER_ROW * LANES)
    tile = (SUB, LANES)
    (chunks,) = call(
        functools.partial(chunk_kernel, levels, peers),
        [chunk],
        (u, v, su, sv, count, elev),
        scratch=[pltpu.VMEM(flat, jnp.float32)] * 4
        + [pltpu.VMEM(tile, count.dtype), pltpu.VMEM(tile, jnp.float32), pltpu.SemaphoreType.DMA((6,))],
        flops=1 << 20,
        size=1 << 21,
        far_in=True,
        limit=60,
    )
    y1, y2, xp = call(
        functools.partial(packet_kernel, levels),
        [row_packet, row_packet, column_packet],
        (u, v, t, su, sv, st, count),
        flops=1 << 20,
        size=1 << 21,
    )
    axes = ("ty", "y", "core")
    ga = lax.all_to_all(chunks, ("ty", "y"), 0, 0)
    x1 = lax.ppermute(xp, axes, swaps(shape, "x", 0))
    x2 = lax.ppermute(xp, axes, swaps(shape, "x", 1))
    y1 = lax.ppermute(y1, axes, swaps(shape, "y", 0))
    y2 = lax.ppermute(y2, axes, swaps(shape, "y", 1))
    dtx, du_t, edge = call(
        functools.partial(column_kernel, levels),
        [room, room, (len(FLOW_FIELDS) * SUB * SUB, LANES)],
        (u, v, t, st, su, sv, count, x1, x2),
        flops=1 << 22,
        size=1 << 21,
    )
    ga, y1, y2, dtx = lax.optimization_barrier((ga, y1, y2, dtx))
    gb = lax.ppermute(ga, axes, swaps(shape, "x", 0))
    dt, dv_t, made, outer = call(
        functools.partial(row_kernel, levels, ny),
        [flat, room, (groups * MADE_ROWS * SUB, LANES), (len(OUTER_ROWS) * SUB, LANES)],
        (u, v, t, st, count, y1, y2, dtx),
        scratch=(pltpu.VMEM(room, jnp.float32), pltpu.SemaphoreType.DMA((groups,))),
        flops=1 << 22,
        size=1 << 21,
        far_out=(0,),
    )
    grid = pltpu.VMEM((ny, nx, SUB, LANES), jnp.float32)
    faces, residuals = (pltpu.VMEM((n, ny, nx, SUB, LANES), jnp.float32) for n in (7, ITERS))
    du, dv, eta = call(
        functools.partial(flow_kernel, levels, ny, nx),
        [flat, flat, (SUB, LANES)],
        (u, v, su, sv, ga, gb, y1, y2, edge, outer, made, du_t, dv_t),
        far_out=(0, 1, 2),
        scratch=(grid, faces, residuals)
        + tuple(pltpu.VMEM(shape, jnp.float32) for shape in (tile, room, room))
        + (pltpu.SemaphoreType.DMA((2 * groups + 1,)),),
        flops=1 << 23,
        size=1 << 22,
    )
    whole = (levels, SUB, LANES)
    return du.reshape(whole), dv.reshape(whole), dt.reshape(whole), eta


def solution(mesh):
    ny, nx = mesh.shape["ty"], mesh.shape["tx"]
    split = Mesh(mesh.devices.reshape(ny, nx // 2, 2), ("ty", "y", "core"))
    deep, flat = P(None, "ty", ("y", "core")), P("ty", ("y", "core"))
    return jax.shard_map(
        functools.partial(on_device, (ny, nx)),
        mesh=split,
        in_specs=(deep, deep, deep, flat, deep, deep, deep, flat),
        out_specs=(deep, deep, deep, flat),
        check_vma=False,
    )
```
